128 devices in a mesh: row: 16 (over x, z), col: 8 (over y, core).
Axes of the slice: x: 4, y: 4, z: 4, core: 2. Of those that a mesh axis runs over, the one named last changes fastest.
Arguments:
- kernel_tiles: float32 [1, 16, 2, 8, 1024, 1024], P(None, 'row', None, 'col'), may hold values from 0 to 2.5, as said below
- profile: int32 [2, 16], replicated, may hold values from 0 to 15, as said below
Outputs:
- factored: float32 [1, 16, 2, 8, 1024, 1024], P(None, 'row', None, 'col')
The draws below stay inside these ranges and needn't reach their ends.
Inputs may be any that keep to these rules, and one draw needn't show every extreme that they name: profile[0] never falls along the tile rows; profile[0, i] >= i - 9, and profile[0, i] = 0 for i <= 9; profile[1, i] is the last j with profile[0, j] <= i. `kernel_tiles`: symmetric; every tile outside the pattern is zero; the matrix restricted to the pattern is positive definite.
All inputs are finite; a program needn't handle non-finite values.
Results may differ from the reference program's by a relative error of at most 0.0001.
Values sent between devices are 32-bit elements; how exact they have to be, the bound alone decides.
A program may use at most 256 MiB of HBM per device.

```python
import jax
import jax.numpy as jnp
from jax import lax

TILE = 1024
TR_DEV = 1
STEPS = 2
NT = 16
BAND = 9
TC_DEV = 2
N_ROW = 16
N_COL = 8


def banded_profile(key):
    key = jax.random.fold_in(key, 11)
    widths = jax.random.randint(key, (NT,), 1, BAND + 1)
    tile_ids = jnp.arange(NT, dtype=jnp.int32)
    widths = jnp.where(tile_ids <= BAND, BAND, widths)
    first_col = jnp.maximum(tile_ids - widths, 0)
    first_col = lax.cummax(first_col, axis=0)
    last_col = jnp.sum((first_col[None, :] <= tile_ids[:, None]).astype(jnp.int32), axis=1) - 1
    return jnp.stack([first_col, last_col]).astype(jnp.int32)


def draw_profile(key, part):
    return banded_profile(key)


def draw_kernel_tiles(key, part):
    profile = banded_profile(key)
    key = jax.random.fold_in(key, 5)
    key_points, key_noise = jax.random.split(key)
    points = jax.random.uniform(key_points, (3, NT, TILE), jnp.float32)
    noise = jax.random.uniform(key_noise, (NT, TILE), jnp.float32, 0.5, 1.5)
    last_col = profile[1]
    tile_ids = jnp.arange(NT, dtype=jnp.int32)
    lower_tile = jnp.minimum(tile_ids[:, None], tile_ids[None, :])
    upper_tile = jnp.maximum(tile_ids[:, None], tile_ids[None, :])
    taper = jnp.maximum(last_col[lower_tile] - upper_tile + 1, 0).astype(jnp.float32) / jnp.float32(BAND + 1)
    length_scale = jnp.float32(0.8 * float(TILE) ** (-1.0 / 3.0))
    inner = jnp.arange(TILE, dtype=jnp.int32)
    identity = (inner[:, None] == inner[None, :]).astype(jnp.float32)

    def tile_row(tile_index):
        own_points = points[:, tile_index]
        squared = jnp.zeros((NT, TILE, TILE), jnp.float32)
        for component in range(3):
            offset = own_points[component][None, :, None] - points[component][:, None, :]
            squared = squared + offset * offset
        values = jnp.exp(-jnp.sqrt(squared) / length_scale) * taper[tile_index][:, None, None]
        on_tile = (tile_ids == tile_index).astype(jnp.float32)[:, None, None]
        nugget = on_tile * identity[None] * noise[tile_index][None, :, None]
        return values + nugget
    all_rows = lax.map(tile_row, tile_ids)
    return all_rows.reshape(TR_DEV, N_ROW, TC_DEV, N_COL, TILE, TILE)


def setup_inputs(seed: int = 0) -> dict:
    arg_keys = jax.random.split(jax.random.key(seed), 3)
    return {
        "kernel_tiles": draw_kernel_tiles(jax.random.fold_in(arg_keys[2], 71), 0),
        "profile": draw_profile(jax.random.fold_in(arg_keys[2], 71), 0),
    }


def solve_right(block_tile, lower_factor):
    return lax.linalg.triangular_solve(lower_factor, block_tile, left_side=False, lower=True, transpose_a=True)

def reference(kernel_tiles, profile):
    count = TR_DEV * N_ROW
    matrix = kernel_tiles.reshape(count, count, TILE, TILE)
    indices = jnp.arange(count, dtype=jnp.int32)
    first_col = profile[0]
    last_col = profile[1]
    row_ids = indices[:, None]
    col_ids = indices[None, :]
    in_pattern = jnp.where(row_ids >= col_ids, first_col[:, None] <= col_ids, col_ids <= last_col[:, None])
    matrix = jnp.where(in_pattern[:, :, None, None], matrix, jnp.float32(0.0))
    for step in range(STEPS):
        diag_factor = jnp.linalg.cholesky(matrix[step, step])
        solved = jax.vmap(lambda block_tile: solve_right(block_tile, diag_factor))(matrix[:, step])
        below = indices > step
        panel = jnp.where(below[:, None, None], solved, jnp.float32(0.0))

        def row_update(pair):
            tile_row, left_tile = pair
            product = jnp.einsum('pq,jrq->jpr', left_tile, panel, precision=lax.Precision.HIGHEST)
            return tile_row - product
        matrix = lax.map(row_update, (matrix, panel))
        column = jnp.where(below[:, None, None], panel, matrix[:, step])
        column = column.at[step].set(diag_factor)
        matrix = matrix.at[:, step].set(column)
        upper = (indices > step)[:, None, None]
        matrix = matrix.at[step].set(jnp.where(upper, jnp.float32(0.0), matrix[step]))
    return matrix.reshape(kernel_tiles.shape)
```

```python
import jax
import jax.numpy as jnp
from jax import lax
from jax.experimental import pallas as pl
from jax.experimental.pallas import tpu as pltpu
from jax.sharding import PartitionSpec as P

F32 = jnp.float32
BF16 = jnp.bfloat16
TILE = 1024
HALF = 128
BLK = 256
NB = 8


def dot_nt(a, b):
    return lax.dot_general(
        a, b, (((1,), (1,)), ((), ())),
        precision=lax.Precision.HIGHEST, preferred_element_type=F32,
    )


def dot_nn(a, b):
    return lax.dot_general(
        a, b, (((1,), (0,)), ((), ())),
        precision=lax.Precision.HIGHEST, preferred_element_type=F32,
    )


def split3(x):
    high = x.astype(BF16).astype(F32)
    rest = x - high
    mid = rest.astype(BF16).astype(F32)
    return high, mid, rest - mid


def split2(x):
    high = x.astype(BF16)
    return high, (x - high.astype(F32)).astype(BF16)


def dot3(a, b, b_dim):
    dims = (((1,), (b_dim,)), ((), ()))

    def one(p, q):
        return lax.dot_general(p, q, dims, preferred_element_type=F32)

    return one(a[0], b[0]) + one(a[0], b[1]) + one(a[1], b[0])


def leaf(work):
    sub = lax.broadcasted_iota(jnp.int32, (8, 2 * HALF), 0)
    for o in range(0, HALF, 8):
        rows = [jnp.broadcast_to(work[o + p:o + p + 1, :], (8, 2 * HALF)) for p in range(8)]
        a = [
            [jnp.broadcast_to(rows[p][:, o + q:o + q + 1], (8, HALF)) for q in range(p + 1)]
            for p in range(8)
        ]
        low = [[None] * 8 for _ in range(8)]
        done = []
        for q in range(8):
            s = lax.rsqrt(a[q][q])
            for p in range(q + 1, 8):
                low[p][q] = a[p][q] * s
            for p in range(q + 1, 8):
                for t in range(q + 1, p + 1):
                    a[p][t] = a[p][t] - low[p][q] * low[t][q]
            acc = rows[q]
            for t in range(q):
                acc = acc - jnp.concatenate([low[q][t], low[q][t]], axis=1) * done[t]
            done.append(acc * jnp.concatenate([s, s], axis=1))
        u = done[0]
        for q in range(1, 8):
            u = jnp.where(sub == q, done[q], u)
        work[o:o + 8, :] = u
        if o + 8 < HALF:
            h, m, l = split3(u)
            left = jnp.concatenate([v[:, :HALF] for v in (h, h, m, h, l, m)], axis=0).astype(BF16)
            right = jnp.concatenate([h, m, h, l, h, m], axis=0).astype(BF16)
            update = lax.dot_general(
                left, right, (((0,), (0,)), ((), ())), preferred_element_type=F32
            )
            work[o + 8:, :] = work[o + 8:, :] - update[o + 8:, :]


def leaf_factor(work, block):
    ri = lax.broadcasted_iota(jnp.int32, (HALF, HALF), 0)
    ci = lax.broadcasted_iota(jnp.int32, (HALF, HALF), 1)
    work[:, :HALF] = block
    work[:, HALF:] = jnp.where(ri == ci, 1.0, 0.0).astype(F32)
    leaf(work)
    upper = jnp.where(ci >= ri, work[:, :HALF], 0.0)
    inverse = jnp.where(ci <= ri, work[:, HALF:], 0.0)
    return upper, inverse


def block_factor(k, s, work, linv):
    here = pl.ds(pl.multiple_of(k * BLK, BLK), BLK)
    block = s[k, here, :]
    u1, inv1 = leaf_factor(work, block[:HALF, :HALF])
    l21 = dot_nt(block[HALF:, :HALF], inv1)
    u2, inv2 = leaf_factor(work, block[HALF:, HALF:] - dot_nt(l21, l21))
    inv21 = -dot_nn(inv2, dot_nn(l21, inv1))
    zero = jnp.zeros((HALF, HALF), F32)
    linv[k, :HALF, :HALF] = inv1
    linv[k, :HALF, HALF:] = zero
    linv[k, HALF:, :HALF] = inv21
    linv[k, HALF:, HALF:] = inv2
    s[k, here, :] = jnp.concatenate(
        [jnp.concatenate([u1.T, zero], axis=1), jnp.concatenate([l21, u2.T], axis=1)], axis=0
    )


def rows_of(i):
    return pl.ds(pl.multiple_of(i * BLK, BLK), BLK)


def panel_step(k, s, linv):
    @pl.loop(k + 1, NB)
    def _(i):
        s[k, rows_of(i), :] = dot_nt(s[k, rows_of(i), :], linv[k])


def trailing_step(k, s):
    @pl.loop(k + 1, NB)
    def _(j):
        @pl.loop(j, NB)
        def _(i):
            s[j, rows_of(i), :] = s[j, rows_of(i), :] - dot_nt(s[k, rows_of(i), :], s[k, rows_of(j), :])


def factor_kernel(a_ref, l_ref, linv_ref, s, work, sem):
    loads = []
    for j in range(NB):
        cols = pl.ds((j % 4) * BLK, BLK)
        if j < 4:
            loads.append(pltpu.make_async_copy(a_ref.at[0, :, cols], s.at[j, pl.ds(0, TILE)], sem.at[j, 0]))
        low = a_ref.at[1, :, cols] if j < 4 else a_ref.at[2, :, cols]
        loads.append(pltpu.make_async_copy(low, s.at[j, pl.ds(TILE, TILE)], sem.at[j, 1]))
    for c in loads:
        c.start()
    for c in loads:
        c.wait()

    @pl.loop(0, NB)
    def _(k):
        block_factor(k, s, work, linv_ref)
        panel_step(k, s, linv_ref)
        trailing_step(k, s)

    out = [pltpu.make_async_copy(s.at[j], l_ref.at[j], sem.at[j, 0]) for j in range(NB)]
    for c in out:
        c.start()
    for c in out:
        c.wait()


def factor(a):
    return pl.pallas_call(
        factor_kernel,
        out_shape=(
            jax.ShapeDtypeStruct((NB, 2 * TILE, BLK), F32),
            jax.ShapeDtypeStruct((NB, BLK, BLK), F32),
        ),
        in_specs=[pl.BlockSpec(memory_space=pl.ANY)],
        out_specs=(pl.BlockSpec(memory_space=pl.ANY), pl.BlockSpec(memory_space=pltpu.VMEM)),
        scratch_shapes=[
            pltpu.VMEM((NB, 2 * TILE, BLK), F32),
            pltpu.VMEM((HALF, 2 * HALF), F32),
            pltpu.SemaphoreType.DMA((NB, 2)),
        ],
        compiler_params=pltpu.CompilerParams(vmem_limit_bytes=50 * 2**20),
        name="factor",
    )(a)


def update_kernel(tiles, wi_ref, wj_ref, w10_ref, l_ref, linv_ref, out, w, v, v10, lbuf, t, sem, lsem, osem):
    r = lax.axis_index("row")
    c = lax.axis_index("col")
    live = r < 11
    full = (r >= 2) & live
    slot_a = jnp.where(c >= 2, 0, 1)
    slot_b = 1 - slot_a

    @pl.when(live)
    def _():
        loads = []
        for j in range(NB):
            cols = pl.ds((j % 4) * BLK, BLK)
            loads.append(pltpu.make_async_copy(wi_ref.at[j // 4, :, cols], w.at[j], sem.at[j]))
            loads.append(pltpu.make_async_copy(
                wj_ref.at[j // 4, pl.ds((j % 4) * BLK, BLK), :], v.at[j], sem.at[NB + j]))
        loads.append(pltpu.make_async_copy(w10_ref, v10, sem.at[2 * NB]))
        loads.append(pltpu.make_async_copy(tiles.at[slot_a], t.at[0], sem.at[2 * NB + 1]))
        loads.append(pltpu.make_async_copy(tiles.at[slot_b], t.at[1], sem.at[2 * NB + 2]))
        for x in loads:
            x.start()
        for x in loads:
            x.wait()

        @pl.loop(0, NB)
        def _(k):
            ld = pltpu.make_async_copy(l_ref.at[k], lbuf, lsem)
            ld.start()
            inv = split2(linv_ref[k])
            ld.wait()
            for rc in range(4):
                rows = pl.ds(rc * BLK, BLK)
                p = dot3(split2(w[k, rows, :]), inv, 1)
                w[k, rows, :] = p
                ps = split2(p)

                @pl.loop(k + 1, NB)
                def _(j):
                    w[j, rows, :] = w[j, rows, :] - dot3(ps, split2(lbuf[rows_of(j), :]), 1)

            @pl.when(full)
            def _():
                v[k] = dot3(inv, split2(v[k]), 0)
                vs = split2(v[k])

                @pl.loop(k + 1, NB)
                def _(j):
                    v[j] = v[j] - dot3(split2(lbuf[rows_of(j), :]), vs, 0)

                for rc in range(4):
                    rows = pl.ds(rc * BLK, BLK)
                    t[0, rows, :] = t[0, rows, :] - dot3(split2(w[k, rows, :]), vs, 0)

            @pl.when(full & (c == 2) & (k >= 4))
            def _():
                at = pl.ds(pl.multiple_of((k - 4) * BLK, BLK), BLK)
                v10[at, :] = dot3(inv, split2(v10[at, :]), 0)
                vs = split2(v10[at, :])

                @pl.loop(k + 1, NB)
                def _(j):
                    to = pl.ds(pl.multiple_of((j - 4) * BLK, BLK), BLK)
                    v10[to, :] = v10[to, :] - dot3(split2(lbuf[rows_of(j), :]), vs, 0)

                for rc in range(4):
                    rows = pl.ds(rc * BLK, BLK)
                    t[1, rows, :] = t[1, rows, :] - dot3(split2(w[k, rows, :]), vs, 0)

    @pl.when(r < 2)
    def _():
        t[0] = jnp.zeros((TILE, TILE), F32)
        t[1] = jnp.zeros((TILE, TILE), F32)

    @pl.when((r < 11) & (c < 2) & (r >= c))
    def _():
        for j in range(4):
            ri = lax.broadcasted_iota(jnp.int32, (TILE, BLK), 0)
            ci = lax.broadcasted_iota(jnp.int32, (TILE, BLK), 1) + j * BLK
            keep = (r > c) | (ri >= ci)
            t[1, :, j * BLK:(j + 1) * BLK] = jnp.where(keep, w[c * 4 + j], 0.0)

    @pl.when(live)
    def _():
        o = [pltpu.make_async_copy(t.at[0], out.at[slot_a], osem.at[0]),
             pltpu.make_async_copy(t.at[1], out.at[slot_b], osem.at[1])]
        for x in o:
            x.start()
        for x in o:
            x.wait()

    @pl.when(r >= 11)
    def _():
        o = [pltpu.make_async_copy(tiles.at[n], out.at[n], osem.at[n]) for n in range(2)]
        for x in o:
            x.start()
        for x in o:
            x.wait()


def update(tiles, wi, wj, w10, l, linv):
    anywhere = pl.BlockSpec(memory_space=pl.ANY)
    return pl.pallas_call(
        update_kernel,
        out_shape=jax.ShapeDtypeStruct((2, TILE, TILE), F32),
        in_specs=[anywhere] * 5 + [pl.BlockSpec(memory_space=pltpu.VMEM)],
        out_specs=anywhere,
        scratch_shapes=[
            pltpu.VMEM((NB, TILE, BLK), F32),
            pltpu.VMEM((NB, BLK, TILE), F32),
            pltpu.VMEM((TILE, TILE), F32),
            pltpu.VMEM((2 * TILE, BLK), F32),
            pltpu.VMEM((2, TILE, TILE), F32),
            pltpu.SemaphoreType.DMA((2 * NB + 3,)),
            pltpu.SemaphoreType.DMA,
            pltpu.SemaphoreType.DMA((2,)),
        ],
        compiler_params=pltpu.CompilerParams(vmem_limit_bytes=58 * 2**20),
        name="update",
    )(tiles, wi, wj, w10, l, linv)


def on_device(kernel_tiles, profile):
    tiles = kernel_tiles.reshape(2, TILE, TILE)
    r = lax.axis_index("row")
    c = lax.axis_index("col")
    zero = jnp.zeros((TILE, TILE), F32)
    a = lax.psum(
        jnp.stack([
            jnp.where((r == 0) & (c == 0), tiles[0], zero),
            jnp.where((r == 1) & (c == 0), tiles[0], zero),
            jnp.where((r == 1) & (c == 1), tiles[0], zero),
        ]), ("row", "col"))
    l, linv = factor(a)
    wi = lax.psum(jnp.stack([jnp.where(c == n, tiles[0], zero) for n in range(2)]), "col")
    mine = jnp.where(c >= 2, tiles[0], tiles[1])
    wj = lax.psum(jnp.stack([jnp.where(r == n, mine, zero) for n in range(2)]
                            + [jnp.where(r == 1, tiles[1], zero)]), "row")
    out = update(tiles, wi, wj[:2], wj[2], l, linv)
    return out.reshape(kernel_tiles.shape)


def solution(mesh):
    placed = (P(None, "row", None, "col", None, None), P())
    return jax.shard_map(
        on_device,
        mesh=mesh,
        in_specs=placed,
        out_specs=P(None, "row", None, "col", None, None),
        check_vma=False,
    )
```

```python
import jax
import jax.numpy as jnp
from jax import lax
from jax.experimental import pallas as pl
from jax.experimental.pallas import tpu as pltpu
from jax.sharding import PartitionSpec as P

F32 = jnp.float32
BF16 = jnp.bfloat16
TILE = 1024
HALF = 128
BLK = 256
NB = 8


def dot_nt(a, b):
    return lax.dot_general(
        a, b, (((1,), (1,)), ((), ())),
        precision=lax.Precision.HIGHEST, preferred_element_type=F32,
    )


def dot_nn(a, b):
    return lax.dot_general(
        a, b, (((1,), (0,)), ((), ())),
        precision=lax.Precision.HIGHEST, preferred_element_type=F32,
    )


def split3(x):
    high = x.astype(BF16).astype(F32)
    rest = x - high
    mid = rest.astype(BF16).astype(F32)
    return high, mid, rest - mid


def split2(x):
    high = x.astype(BF16)
    return high, (x - high.astype(F32)).astype(BF16)


def dot3(a, b, b_dim):
    dims = (((1,), (b_dim,)), ((), ()))

    def one(p, q):
        return lax.dot_general(p, q, dims, preferred_element_type=F32)

    return one(a[0], b[0]) + one(a[0], b[1]) + one(a[1], b[0])


def leaf(work):
    sub = lax.broadcasted_iota(jnp.int32, (8, 2 * HALF), 0)
    for o in range(0, HALF, 8):
        rows = [jnp.broadcast_to(work[o + p:o + p + 1, :], (8, 2 * HALF)) for p in range(8)]
        a = [
            [jnp.broadcast_to(rows[p][:, o + q:o + q + 1], (8, HALF)) for q in range(p + 1)]
            for p in range(8)
        ]
        low = [[None] * 8 for _ in range(8)]
        done = []
        for q in range(8):
            s = lax.rsqrt(a[q][q])
            for p in range(q + 1, 8):
                low[p][q] = a[p][q] * s
            for p in range(q + 1, 8):
                for t in range(q + 1, p + 1):
                    a[p][t] = a[p][t] - low[p][q] * low[t][q]
            acc = rows[q]
            for t in range(q):
                acc = acc - jnp.concatenate([low[q][t], low[q][t]], axis=1) * done[t]
            done.append(acc * jnp.concatenate([s, s], axis=1))
        u = done[0]
        for q in range(1, 8):
            u = jnp.where(sub == q, done[q], u)
        work[o:o + 8, :] = u
        if o + 8 < HALF:
            h, m, l = split3(u)
            left = jnp.concatenate([v[:, :HALF] for v in (h, h, m, h, l, m)], axis=0).astype(BF16)
            right = jnp.concatenate([h, m, h, l, h, m], axis=0).astype(BF16)
            update = lax.dot_general(
                left, right, (((0,), (0,)), ((), ())), preferred_element_type=F32
            )
            work[o + 8:, :] = work[o + 8:, :] - update[o + 8:, :]


def leaf_factor(work, block):
    ri = lax.broadcasted_iota(jnp.int32, (HALF, HALF), 0)
    ci = lax.broadcasted_iota(jnp.int32, (HALF, HALF), 1)
    work[:, :HALF] = block
    work[:, HALF:] = jnp.where(ri == ci, 1.0, 0.0).astype(F32)
    leaf(work)
    upper = jnp.where(ci >= ri, work[:, :HALF], 0.0)
    inverse = jnp.where(ci <= ri, work[:, HALF:], 0.0)
    return upper, inverse


def block_factor(k, s, work, linv, n):
    here = pl.ds(pl.multiple_of(k * BLK, BLK), BLK)
    block = s[k, here, :]
    u1, inv1 = leaf_factor(work, block[:HALF, :HALF])
    l21 = dot_nt(block[HALF:, :HALF], inv1)
    u2, inv2 = leaf_factor(work, block[HALF:, HALF:] - dot_nt(l21, l21))
    inv21 = -dot_nn(inv2, dot_nn(l21, inv1))
    zero = jnp.zeros((HALF, HALF), F32)
    linv[n, :HALF, :HALF] = inv1
    linv[n, :HALF, HALF:] = zero
    linv[n, HALF:, :HALF] = inv21
    linv[n, HALF:, HALF:] = inv2
    s[k, here, :] = jnp.concatenate(
        [jnp.concatenate([u1.T, zero], axis=1), jnp.concatenate([l21, u2.T], axis=1)], axis=0
    )


def rows_of(i):
    return pl.ds(pl.multiple_of(i * BLK, BLK), BLK)


FB = 4
MASKS = ((4017, 192, 560, 16), (8, 49160, 34944, 50377), (49152, 7937, 12544, 6400))


def first_id(k):
    return 4 * k - lax.div(k * (k - 1), jnp.int32(2))


def kernel(tiles, out, w, v, v10, t, lb, s, work, ph, pw, vh, vw,
           load, load_t, c_recv, d_recv, e_recv, r_own, r_sib, l_own, l_sib,
           c_send, d_send, e_send, r_send, a_send, b_send, s_send, root_send, osem):
    r = lax.axis_index("row")
    c = lax.axis_index("col")
    x = lax.div(r, 4)
    z = lax.rem(r, 4)
    y = lax.div(c, 2)
    core = lax.rem(c, 2)
    sibling = (r, c + 1 - 2 * core)
    dirs = (
        (lax.rem(x + 1, 4) * 4 + z, c),
        (lax.rem(x + 3, 4) * 4 + z, c),
        (x * 4 + lax.rem(z + 1, 4), c),
        (x * 4 + lax.rem(z + 3, 4), c),
    )
    is_f = (r == 0) & (c == 0)
    is_g = (r == 1) & (c == 1)
    plain = jnp.logical_not(is_f | is_g)
    full = (r >= 2) & (r <= 10)
    in_a = r != 1
    in_b = r != 0
    slot_a = jnp.where(c >= 2, 0, 1)
    mirror = x * 4 + lax.rem(5 - z, 4)

    def bit(mask, pos):
        return lax.rem(lax.shift_right_logical(jnp.int32(mask), pos), 2)

    flags_a = [[bit(m[d], r) for d in range(4)] for m in MASKS]
    flags_b = [[bit(m[d], mirror) for d in (0, 1, 3, 2)] for m in MASKS]

    def remote(src, dst, send, recv, device):
        return pltpu.make_async_remote_copy(
            src_ref=src, dst_ref=dst, send_sem=send, recv_sem=recv,
            device_id=device, device_id_type=pl.DeviceIdType.MESH,
        )

    def arrived(ref, sem):
        pltpu.make_async_copy(ref, ref, sem).wait()

    def drain(sem, rows):
        ref = t.at[0, pl.ds(0, rows)]
        pltpu.make_async_copy(ref, ref, sem).wait()

    def forward(flags, n, ref, sends, recv):
        tree = lax.rem(n, 3)
        for d in range(4):
            go = jnp.where(tree == 0, flags[0][d], jnp.where(tree == 1, flags[1][d], flags[2][d]))

            @pl.when(go == 1)
            def _():
                remote(ref, ref, sends.at[tree, d], recv, dirs[d]).start()

    def drain_tree(flags, sends, rows):
        for tree in range(3):
            for d in range(4):
                @pl.when(flags[tree][d] == 1)
                def _():
                    drain(sends.at[tree, d], rows[tree])

    barrier = pltpu.get_barrier_semaphore()
    for n in range(1, 8):
        pl.semaphore_signal(barrier, inc=1, device_id=(r, lax.rem(c + n, 8)),
                            device_id_type=pl.DeviceIdType.MESH)
    for d in range(4):
        pl.semaphore_signal(barrier, inc=1, device_id=dirs[d], device_id_type=pl.DeviceIdType.MESH)

    @pl.when(is_f | is_g)
    def _():
        pl.semaphore_signal(barrier, inc=1, device_id=(1 - r, 1 - c), device_id_type=pl.DeviceIdType.MESH)

    def block_cols(n):
        return pl.ds(pl.multiple_of(n * BLK, BLK), BLK)

    def local(src, dst, sem):
        return pltpu.make_async_copy(src, dst, sem)

    @pl.when(is_f | is_g)
    def _():
        for k in range(FB):
            local(tiles.at[0, pl.ds(k * BLK, TILE - k * BLK), pl.ds(k * BLK, BLK)],
                  s.at[k, pl.ds(k * BLK, TILE - k * BLK), :], load.at[4 + k]).start()
            if k:
                s[k, pl.ds(0, k * BLK), :] = jnp.zeros((k * BLK, BLK), F32)

    def tile_rows(base):
        return [local(tiles.at[slot_a, pl.ds(k * BLK, BLK), :], v.at[base + k], load.at[k]) for k in range(FB)]

    def extra_rows():
        return [local(tiles.at[1, pl.ds(k * BLK, BLK), :], v10.at[k], load.at[8 + k]) for k in range(FB)]

    def own_cols():
        return [local(tiles.at[0, :, pl.ds(k * BLK, BLK)], w.at[4 * core + k], load.at[k]) for k in range(FB)]

    def target(n):
        return local(tiles.at[slot_a if n == 0 else 1], t.at[n], load_t.at[n])

    def pass_on():
        return [local(tiles.at[n], out.at[n], osem.at[n]) for n in range(2)]

    @pl.when(r == 0)
    def _():
        for cp in tile_rows(0):
            cp.start()

    @pl.when(r == 1)
    def _():
        for cp in tile_rows(4):
            cp.start()

        @pl.when(c == 2)
        def _():
            for cp in extra_rows():
                cp.start()

    @pl.when(full & (y == 0))
    def _():
        for cp in own_cols():
            cp.start()

    @pl.when(r >= 11)
    def _():
        for cp in pass_on():
            cp.start()

    @pl.when(plain)
    def _():
        pl.semaphore_wait(barrier, 11)

    @pl.when(is_f | is_g)
    def _():
        pl.semaphore_wait(barrier, 12)

    @pl.when((full & (y == 0)) | ((r == 1) & (c == 0)))
    def _():
        for k in range(FB):
            remote(tiles.at[0, :, pl.ds(k * BLK, BLK)], w.at[4 * core + k],
                   r_send.at[2], r_sib.at[k], sibling).start()

    @pl.when(r == 0)
    def _():
        for cp in tile_rows(0):
            cp.wait()

    @pl.when(r == 1)
    def _():
        for cp in tile_rows(4):
            cp.wait()

        @pl.when(c == 2)
        def _():
            for cp in extra_rows():
                cp.wait()

    @pl.when(full)
    def _():
        target(0).start()

        @pl.when(c == 2)
        def _():
            target(1).start()

    def quarter(n):
        return pl.ds(pl.multiple_of(lax.rem(n, 4) * 64, 64), 64)

    def c_event(n):
        ref = v.at[lax.div(n, 4), quarter(n), :]

        @pl.when(in_a & (r != 0))
        def _():
            arrived(ref, c_recv.at[n])

        forward(flags_a, n, ref, c_send, c_recv.at[n])

    def d_event(n):
        ref = v.at[4 + lax.div(n, 4), quarter(n), :]

        @pl.when(in_b & (r != 1))
        def _():
            arrived(ref, d_recv.at[n])

        forward(flags_b, n, ref, d_send, d_recv.at[n])

    def e_event(n):
        ref = v10.at[lax.div(n, 4), quarter(n), :]

        @pl.when(c == 2)
        def _():
            @pl.when(in_b & (r != 1))
            def _():
                arrived(ref, e_recv.at[n])

            forward(flags_b, n, ref, e_send, e_recv.at[n])

    half_512 = pl.ds(pl.multiple_of(core * 512, 512), 512)
    other_512 = pl.ds(pl.multiple_of(512 - core * 512, 512), 512)

    def r_event(n):
        @pl.when(full)
        def _():
            ref = w.at[n, half_512, :]
            m = lax.rem(n, 4)

            @pl.when(y == 0)
            def _():
                @pl.when(lax.div(n, 4) == core)
                def _():
                    arrived(w.at[n], load.at[m])

                @pl.when(lax.div(n, 4) != core)
                def _():
                    arrived(w.at[n], r_sib.at[m])

                remote(ref, ref, r_send.at[0], r_own.at[n], (r, 2 + core)).start()
                remote(ref, ref, r_send.at[1], r_own.at[n], (r, 6 + core)).start()

            @pl.when(y != 0)
            def _():
                arrived(ref, r_own.at[n])
                remote(ref, ref, r_send.at[2], r_sib.at[n], sibling).start()

                @pl.when((y + 2 * lax.rem(n, 2) == 1) | ((y == 3) & (lax.rem(n, 2) == 1)))
                def _():
                    remote(ref, ref, r_send.at[0], r_own.at[n], (r, 4 + core)).start()

    half_128 = pl.ds(pl.multiple_of(core * HALF, HALF), HALF)
    other_128 = pl.ds(pl.multiple_of(HALF - core * HALF, HALF), HALF)

    def l_event(n, flags, member, sends):
        ref = lb.at[n, half_128, :]

        @pl.when(member)
        def _():
            arrived(ref, l_own.at[n])

            @pl.when(full)
            def _():
                remote(ref, ref, s_send, l_sib.at[n], sibling).start()

            forward(flags, n, ref, sends, l_own.at[n])

    def l_ready(n):
        arrived(lb.at[n, other_128, :], l_sib.at[n])

    def a_events(k):
        lo = first_id(k)

        @pl.loop(lo, lo + 4 - k)
        def _(n):
            l_event(n, flags_a, in_a, a_send)

        @pl.when(full)
        def _():
            @pl.loop(lo, lo + 4 - k)
            def _(n):
                l_ready(n)

    def b_events(lo, count):
        @pl.loop(lo, lo + count)
        def _(n):
            l_event(n, flags_b, in_b, b_send)

        @pl.when(full)
        def _():
            @pl.loop(lo, lo + count)
            def _(n):
                l_ready(n)

    def chain(base, send):
        @pl.loop(0, FB)
        def _(k):
            lo = base + first_id(k)
            block_factor(k, s, work, lb, lo)
            send(lo)

            @pl.loop(k + 1, FB)
            def _(i):
                p = dot_nt(s[k, rows_of(i), :], lb[lo])
                s[k, rows_of(i), :] = p
                lb[lo + i - k] = p
                send(lo + i - k)

            @pl.loop(k + 1, FB)
            def _(j):
                @pl.loop(j, FB)
                def _(i):
                    s[j, rows_of(i), :] = s[j, rows_of(i), :] - dot_nt(s[k, rows_of(i), :], s[k, rows_of(j), :])

    def half_of(core_no):
        return pl.ds(core_no * HALF, HALF)

    def send_f(n):
        for q, h in enumerate((0, 1)):
            remote(lb.at[n, half_of(h), :], lb.at[n, half_of(h), :], root_send.at[8 + q],
                   (l_own if h == 1 else l_sib).at[n], (1, 1)).start()
        for other in range(1, 8):
            ref = lb.at[n, half_of(other % 2), :]
            remote(ref, ref, root_send.at[other], l_own.at[n], (0, other)).start()
        forward(flags_a, n, lb.at[n, half_of(0), :], a_send, l_own.at[n])

    def send_g(n, both):
        for other in (0, 2, 3, 4, 5, 6, 7):
            ref = lb.at[n, half_of(other % 2), :]
            remote(ref, ref, root_send.at[other], l_own.at[n], (1, other)).start()
        if both:
            ref = lb.at[n, half_of(1), :]
            remote(ref, ref, root_send.at[8], l_sib.at[n], (1, 0)).start()
        forward(flags_b, n, lb.at[n, half_of(1), :], b_send, l_own.at[n])

    def factor_out():
        return [local(s.at[k], out.at[0, :, pl.ds(k * BLK, BLK)], osem.at[2 + k]) for k in range(FB)]

    @pl.when(is_f)
    def _():
        for k in range(FB):
            arrived(s.at[k, pl.ds(k * BLK, TILE - k * BLK), :], load.at[4 + k])

        @pl.loop(0, 16)
        def _(n):
            c_event(n)

        chain(0, send_f)
        for cp in factor_out():
            cp.start()
        for cp in factor_out():
            cp.wait()
        drain_tree(flags_a, c_send, (384, 320, 320))
        for other in range(1, 10):
            drain(root_send.at[other], 320)

    @pl.when(is_g)
    def _():
        for k in range(FB):
            arrived(s.at[k, pl.ds(k * BLK, TILE - k * BLK), :], load.at[4 + k])
            arrived(w.at[k], r_sib.at[k])

        @pl.loop(0, 16)
        def _(n):
            d_event(n)

        @pl.loop(0, FB)
        def _(k):
            lo = first_id(k)

            @pl.loop(lo, lo + 4 - k)
            def _(n):
                arrived(lb.at[n, half_of(1), :], l_own.at[n])
                arrived(lb.at[n, half_of(0), :], l_sib.at[n])

            @pl.loop(0, FB)
            def _(i):
                p = dot_nt(w[k, rows_of(i), :], lb[lo])
                w[k, rows_of(i), :] = p
                lb[10 + 4 * k + i] = p
                send_g(10 + 4 * k + i, True)

            @pl.loop(0, FB)
            def _(j):
                @pl.loop(j, FB)
                def _(i):
                    s[j, rows_of(i), :] = s[j, rows_of(i), :] - dot_nt(w[k, rows_of(i), :], w[k, rows_of(j), :])

            @pl.loop(k + 1, FB)
            def _(j):
                @pl.loop(0, FB)
                def _(i):
                    w[j, rows_of(i), :] = w[j, rows_of(i), :] - dot_nt(w[k, rows_of(i), :], lb[lo + j - k])

        chain(26, lambda n: send_g(n, False))
        for cp in factor_out():
            cp.start()
        for cp in factor_out():
            cp.wait()
        drain_tree(flags_b, d_send, (384, 320, 320))
        for other in (0, 2, 3, 4, 5, 6, 7):
            drain(root_send.at[other], 832)
        drain(root_send.at[8], 512)

    def v_split(buf, k):
        hi, lo = split2(buf[k])
        vh[...] = hi
        vw[...] = lo

    def v_solve(buf, k, n):
        buf[k] = dot3(split2(lb[n]), split2(buf[k]), 0)
        v_split(buf, k)

    def v_sub(buf, j, n):
        buf[j] = buf[j] - dot3(split2(lb[n]), (vh[...], vw[...]), 0)

    def w_solve(k, n):
        w[k] = dot3(split2(w[k]), split2(lb[n]), 1)
        hi, lo = split2(w[k])
        ph[...] = hi
        pw[...] = lo

    def w_sub(j, n):
        w[j] = w[j] - dot3((ph[...], pw[...]), split2(lb[n]), 1)

    def t_sub(slot):
        for n in range(4):
            cols = pl.ds(n * BLK, BLK)
            t[slot, :, cols] = t[slot, :, cols] - dot3((ph[...], pw[...]), (vh[:, cols], vw[:, cols]), 0)

    @pl.when(plain)
    def _():
        @pl.loop(0, FB)
        def _(g):
            @pl.loop(4 * g, 4 * g + 4)
            def _(n):
                c_event(n)

            r_event(g)

        drain_tree(flags_a, c_send, (384, 320, 320))

        @pl.loop(0, FB)
        def _(k):
            a_events(k)

            @pl.loop(4 * k, 4 * k + 4)
            def _(n):
                d_event(n)
                e_event(n)

            @pl.when(full)
            def _():
                lo = first_id(k)
                v_solve(v, k, lo)

                @pl.loop(k + 1, FB)
                def _(j):
                    v_sub(v, j, lo + j - k)

            b_events(10 + 4 * k, 4)
            r_event(4 + k)

        drain_tree(flags_b, d_send, (384, 320, 320))

        @pl.when(c == 2)
        def _():
            drain_tree(flags_b, e_send, (384, 320, 320))

    @pl.when(full)
    def _():
        @pl.when(y == 0)
        def _():
            drain(r_send.at[0], 1024)
            drain(r_send.at[1], 1024)

        @pl.when((y == 1) | (y == 3))
        def _():
            drain(r_send.at[0], 512)

        drain(r_send.at[2], 1024)

        @pl.when(y != 0)
        def _():
            @pl.loop(0, NB)
            def _(n):
                arrived(w.at[n, other_512, :], r_sib.at[n])

        target(0).wait()

        @pl.when(c == 2)
        def _():
            target(1).wait()

    @pl.when((r == 1) & (c == 0))
    def _():
        drain(r_send.at[2], 1024)

    @pl.when(plain)
    def _():
        @pl.loop(0, FB)
        def _(k):
            lo = first_id(k)

            @pl.when(full)
            def _():
                v_split(v, k)

                @pl.loop(0, FB)
                def _(j):
                    v_sub(v, 4 + j, 10 + 4 * k + j)

                w_solve(k, lo)

                @pl.loop(k + 1, FB)
                def _(j):
                    w_sub(j, lo + j - k)

                @pl.loop(0, FB)
                def _(j):
                    w_sub(4 + j, 10 + 4 * k + j)

                t_sub(0)

            @pl.when(lax.rem(k, 2) == 1)
            def _():
                q = lax.div(k, 2)
                b_events(26 + first_id(q), 4 - q)

        @pl.loop(0, FB)
        def _(k):
            lo = 26 + first_id(k)

            @pl.when(k >= 2)
            def _():
                b_events(lo, 4 - k)

            @pl.when(full)
            def _():
                w_solve(4 + k, lo)

                @pl.loop(k + 1, FB)
                def _(j):
                    w_sub(4 + j, lo + j - k)

                @pl.when(c == 2)
                def _():
                    v_solve(v10, k, lo)

                    @pl.loop(k + 1, FB)
                    def _(j):
                        v_sub(v10, j, lo + j - k)

                    t_sub(1)

                v_solve(v, 4 + k, lo)

                @pl.loop(k + 1, FB)
                def _(j):
                    v_sub(v, 4 + j, lo + j - k)

                t_sub(0)

    def run(copies):
        for cp in copies:
            cp.start()
        for cp in copies:
            cp.wait()

    @pl.when(full)
    def _():
        main = local(t.at[0], out.at[slot_a], osem.at[0])

        @pl.when(c < 2)
        def _():
            run([main] + [local(w.at[4 * c + k], out.at[0, :, pl.ds(k * BLK, BLK)], osem.at[2 + k])
                          for k in range(FB)])

        @pl.when(c == 2)
        def _():
            run([main, local(t.at[1], out.at[1], osem.at[1])])

        @pl.when(c > 2)
        def _():
            run([main, local(tiles.at[1], out.at[1], osem.at[1])])

        sent = t.at[:, pl.ds(0, 576)]
        arrived(sent, s_send)

    @pl.when(r >= 11)
    def _():
        for cp in pass_on():
            cp.wait()

    @pl.when(r < 2)
    def _():
        t[0] = jnp.zeros((TILE, TILE), F32)
        blank = [local(t.at[0], out.at[n], osem.at[n]) for n in range(2)]

        @pl.when(c <= r)
        def _():
            run(blank[1:])

        @pl.when(c > r)
        def _():
            run(blank)

    @pl.when((r == 1) & (c == 0))
    def _():
        @pl.loop(10, 26)
        def _(n):
            arrived(lb.at[n, half_of(1), :], l_sib.at[n])

        panel = [local(lb.at[10 + 4 * k + j], out.at[0, pl.ds(j * BLK, BLK), pl.ds(k * BLK, BLK)],
                       osem.at[6 + 4 * k + j]) for k in range(FB) for j in range(FB)]
        run(panel)

    drain_tree(flags_a, a_send, (128, 96, 96))
    drain_tree(flags_b, b_send, (256, 288, 288))


def on_device(kernel_tiles, profile):
    tiles = kernel_tiles.reshape(2, TILE, TILE)
    dma = pltpu.SemaphoreType.DMA
    out = pl.pallas_call(
        kernel,
        out_shape=jax.ShapeDtypeStruct((2, TILE, TILE), F32),
        in_specs=[pl.BlockSpec(memory_space=pl.ANY)],
        out_specs=pl.BlockSpec(memory_space=pl.ANY),
        scratch_shapes=[
            pltpu.VMEM((NB, TILE, BLK), F32),
            pltpu.VMEM((NB, BLK, TILE), F32),
            pltpu.VMEM((FB, BLK, TILE), F32),
            pltpu.VMEM((2, TILE, TILE), F32),
            pltpu.VMEM((36, BLK, BLK), F32),
            pltpu.VMEM((FB, TILE, BLK), F32),
            pltpu.VMEM((HALF, 2 * HALF), F32),
            pltpu.VMEM((TILE, BLK), BF16),
            pltpu.VMEM((TILE, BLK), BF16),
            pltpu.VMEM((BLK, TILE), BF16),
            pltpu.VMEM((BLK, TILE), BF16),
            dma((12,)), dma((2,)),
            dma((16,)), dma((16,)), dma((16,)),
            dma((8,)), dma((8,)), dma((36,)), dma((36,)),
            dma((3, 4)), dma((3, 4)), dma((3, 4)), dma((3,)),
            dma((3, 4)), dma((3, 4)), dma, dma((10,)), dma((22,)),
        ],
        compiler_params=pltpu.CompilerParams(
            vmem_limit_bytes=58 * 2**20, collective_id=0, has_side_effects=True
        ),
        name="panel_steps",
    )(tiles)
    return out.reshape(kernel_tiles.shape)


def solution(mesh):
    placed = (P(None, "row", None, "col", None, None), P())
    return jax.shard_map(
        on_device,
        mesh=mesh,
        in_specs=placed,
        out_specs=P(None, "row", None, "col", None, None),
        check_vma=False,
    )
```

```python
import jax
import jax.numpy as jnp
from jax import lax
from jax.experimental import pallas as pl
from jax.experimental.pallas import tpu as pltpu
from jax.sharding import PartitionSpec as P

F32 = jnp.float32
BF16 = jnp.bfloat16
TILE = 1024
HALF = 128
BLK = 256
NB = 8


def dot_nt(a, b):
    return lax.dot_general(
        a, b, (((1,), (1,)), ((), ())),
        precision=lax.Precision.HIGHEST, preferred_element_type=F32,
    )


def dot_nn(a, b):
    return lax.dot_general(
        a, b, (((1,), (0,)), ((), ())),
        precision=lax.Precision.HIGHEST, preferred_element_type=F32,
    )


def split3(x):
    high = x.astype(BF16).astype(F32)
    rest = x - high
    mid = rest.astype(BF16).astype(F32)
    return high, mid, rest - mid


def split2(x):
    high = x.astype(BF16)
    return high, (x - high.astype(F32)).astype(BF16)


def dot3(a, b, b_dim):
    dims = (((1,), (b_dim,)), ((), ()))

    def one(p, q):
        return lax.dot_general(p, q, dims, preferred_element_type=F32)

    return one(a[0], b[0]) + one(a[0], b[1]) + one(a[1], b[0])


def leaf(work):
    sub = lax.broadcasted_iota(jnp.int32, (8, 2 * HALF), 0)
    for o in range(0, HALF, 8):
        rows = [jnp.broadcast_to(work[o + p:o + p + 1, :], (8, 2 * HALF)) for p in range(8)]
        a = [
            [jnp.broadcast_to(rows[p][:, o + q:o + q + 1], (8, HALF)) for q in range(p + 1)]
            for p in range(8)
        ]
        low = [[None] * 8 for _ in range(8)]
        done = []
        for q in range(8):
            s = lax.rsqrt(a[q][q])
            for p in range(q + 1, 8):
                low[p][q] = a[p][q] * s
            for p in range(q + 1, 8):
                for t in range(q + 1, p + 1):
                    a[p][t] = a[p][t] - low[p][q] * low[t][q]
            acc = rows[q]
            for t in range(q):
                acc = acc - jnp.concatenate([low[q][t], low[q][t]], axis=1) * done[t]
            done.append(acc * jnp.concatenate([s, s], axis=1))
        u = done[0]
        for q in range(1, 8):
            u = jnp.where(sub == q, done[q], u)
        work[o:o + 8, :] = u
        if o + 8 < HALF:
            h, m, l = split3(u)
            left = jnp.concatenate([v[:, :HALF] for v in (h, h, m, h, l, m)], axis=0).astype(BF16)
            right = jnp.concatenate([h, m, h, l, h, m], axis=0).astype(BF16)
            update = lax.dot_general(
                left, right, (((0,), (0,)), ((), ())), preferred_element_type=F32
            )
            work[o + 8:, :] = work[o + 8:, :] - update[o + 8:, :]


def leaf_factor(work, block):
    ri = lax.broadcasted_iota(jnp.int32, (HALF, HALF), 0)
    ci = lax.broadcasted_iota(jnp.int32, (HALF, HALF), 1)
    work[:, :HALF] = block
    work[:, HALF:] = jnp.where(ri == ci, 1.0, 0.0).astype(F32)
    leaf(work)
    upper = jnp.where(ci >= ri, work[:, :HALF], 0.0)
    inverse = jnp.where(ci <= ri, work[:, HALF:], 0.0)
    return upper, inverse


def block_factor(k, s, work, linv, n):
    here = pl.ds(pl.multiple_of(k * BLK, BLK), BLK)
    block = s[k, here, :]
    u1, inv1 = leaf_factor(work, block[:HALF, :HALF])
    l21 = dot_nt(block[HALF:, :HALF], inv1)
    u2, inv2 = leaf_factor(work, block[HALF:, HALF:] - dot_nt(l21, l21))
    inv21 = -dot_nn(inv2, dot_nn(l21, inv1))
    zero = jnp.zeros((HALF, HALF), F32)
    linv[n, :HALF, :HALF] = inv1
    linv[n, :HALF, HALF:] = zero
    linv[n, HALF:, :HALF] = inv21
    linv[n, HALF:, HALF:] = inv2
    s[k, here, :] = jnp.concatenate(
        [jnp.concatenate([u1.T, zero], axis=1), jnp.concatenate([l21, u2.T], axis=1)], axis=0
    )


def rows_of(i):
    return pl.ds(pl.multiple_of(i * BLK, BLK), BLK)


FB = 4
SLOTS = 38
EXTRA_SLOTS = 46


def first_id(k):
    return 4 * k - lax.div(k * (k - 1), jnp.int32(2))


def kernel(tiles, out, w, v, v10, t, lb, s, work, ph, pw, vh, vw,
           load, load_t, c_recv, d_recv, e_recv, r_own, r_sib, l_own, l_sib,
           c_send, d_send, e_send, r_send, a_send, b_send, y_send, s_send, root_send, osem):
    r = lax.axis_index("row")
    c = lax.axis_index("col")
    x = lax.div(r, 4)
    z = lax.rem(r, 4)
    y = lax.div(c, 2)
    core = lax.rem(c, 2)
    sibling = (r, c + 1 - 2 * core)
    dirs = (
        (lax.rem(x + 1, 4) * 4 + z, c),
        (lax.rem(x + 3, 4) * 4 + z, c),
        (x * 4 + lax.rem(z + 1, 4), c),
        (x * 4 + lax.rem(z + 3, 4), c),
    )
    is_f = (r == 0) & (c == 0)
    is_g = (r == 1) & (c == 1)
    plain = jnp.logical_not(is_f | is_g)
    full = (r >= 2) & (r <= 10)
    slot_a = jnp.where(c >= 2, 0, 1)
    never = r < 0

    c_out = (((x <= 1) & (z == 0)), never, ((x == 1) | (x == 2)) & (z <= 1),
             ((x == 0) & ((z == 0) | (z == 3))) | ((x == 1) & (z == 0)))
    c_in = jnp.logical_not((x == 3) | ((x == 0) & (z == 1)) | ((x == 2) & (z == 3)))
    c_depth = jnp.where(x == 0, lax.rem(4 - z, 4), jnp.where(x == 1, 1 + jnp.minimum(z, 4 - z), 2 + z))
    d_out = (((x == 0) & (z >= 1)) | ((x == 1) & ((z == 1) | (z == 2))), never,
             (x == 0) & ((z == 1) | (z == 2)), ((x == 1) | (x == 2)) & (z == 1))
    d_in = jnp.logical_not((x == 3) | ((x == 0) & (z == 0)) | ((x == 2) & (z == 3)))
    d_depth = jnp.where(x == 0, z - 1, jnp.where(x == 1, jnp.where(z == 0, 2, z), jnp.where(z == 1, 2, 3)))

    def stream_tree(z0):
        dz = lax.rem(z + 4 - z0, 4)
        root = (x == 0) & (z == z0)
        turn = jnp.minimum(dz, 4 - dz)
        outs = (root | (x == 2) | (x == 3), (x == 3) & (z >= 2), (x == 3) & (dz <= 1), (x == 3) & (dz == 0))
        outs = (outs[1], outs[0], outs[2], outs[3])
        depth = jnp.where(root, 0, jnp.where(x == 0, 2, 4 - x) + turn)
        return outs, (x >= 1) | (z >= 2) | root, depth

    y_depth = jnp.where(y == 0, 0, jnp.where(y == 2, 2, 1))
    a_out, a_in, a_depth = stream_tree(0)
    b_out, b_in, b_depth = stream_tree(1)

    def remote(src, dst, send, recv, device):
        return pltpu.make_async_remote_copy(
            src_ref=src, dst_ref=dst, send_sem=send, recv_sem=recv,
            device_id=device, device_id_type=pl.DeviceIdType.MESH,
        )

    def arrived(ref, sem):
        pltpu.make_async_copy(ref, ref, sem).wait()

    def drain(sem, rows):
        ref = t.at[0, pl.ds(0, rows)]
        pltpu.make_async_copy(ref, ref, sem).wait()

    def forward(outs, ref, sends, recv):
        for d in range(4):
            @pl.when(outs[d])
            def _():
                remote(ref, ref, sends(d), recv, dirs[d]).start()

    def drain_outs(outs, sends, rows):
        for d in range(4):
            @pl.when(outs[d])
            def _():
                drain(sends(d), rows)

    barrier = pltpu.get_barrier_semaphore()
    for n in range(1, 8):
        pl.semaphore_signal(barrier, inc=1, device_id=(r, lax.rem(c + n, 8)),
                            device_id_type=pl.DeviceIdType.MESH)
    for d in range(4):
        pl.semaphore_signal(barrier, inc=1, device_id=dirs[d], device_id_type=pl.DeviceIdType.MESH)

    @pl.when(is_f | is_g)
    def _():
        pl.semaphore_signal(barrier, inc=1, device_id=(1 - r, 1 - c), device_id_type=pl.DeviceIdType.MESH)

    def block_cols(n):
        return pl.ds(pl.multiple_of(n * BLK, BLK), BLK)

    def local(src, dst, sem):
        return pltpu.make_async_copy(src, dst, sem)

    @pl.when(is_f | is_g)
    def _():
        for k in range(FB):
            local(tiles.at[0, pl.ds(k * BLK, TILE - k * BLK), pl.ds(k * BLK, BLK)],
                  s.at[k, pl.ds(k * BLK, TILE - k * BLK), :], load.at[4 + k]).start()
            if k:
                s[k, pl.ds(0, k * BLK), :] = jnp.zeros((k * BLK, BLK), F32)

    def tile_rows(base):
        return [local(tiles.at[slot_a, pl.ds(k * BLK, BLK), :], v.at[base + k], load.at[k]) for k in range(FB)]

    def extra_rows():
        return [local(tiles.at[1, pl.ds(k * BLK, BLK), :], v10.at[k], load.at[8 + k]) for k in range(FB)]

    def own_cols():
        return [local(tiles.at[0, :, pl.ds(k * BLK, BLK)], w.at[4 * core + k], load.at[k]) for k in range(FB)]

    def target(n):
        return local(tiles.at[slot_a if n == 0 else 1], t.at[n], load_t.at[n])

    def pass_in(n):
        return local(tiles.at[n], t.at[n], load_t.at[n])

    def pass_out(n):
        return local(t.at[n], out.at[n], osem.at[n])

    @pl.when(r == 0)
    def _():
        for cp in tile_rows(0):
            cp.start()

    @pl.when(r == 1)
    def _():
        for cp in tile_rows(4):
            cp.start()

        @pl.when(c == 2)
        def _():
            for cp in extra_rows():
                cp.start()

    @pl.when(full & (y == 0))
    def _():
        for cp in own_cols():
            cp.start()

    @pl.when(r >= 11)
    def _():
        pass_in(0).start()
        pass_in(1).start()

    @pl.when(full & (c > 2))
    def _():
        pass_in(1).start()

    @pl.when(plain)
    def _():
        pl.semaphore_wait(barrier, 11)

    @pl.when(is_f | is_g)
    def _():
        pl.semaphore_wait(barrier, 12)

    @pl.when((full & (y == 0)) | ((r == 1) & (c == 0)))
    def _():
        for k in range(FB):
            remote(tiles.at[0, :, pl.ds(k * BLK, BLK)], w.at[4 * core + k],
                   r_send.at[2, 4 * core + k], r_sib.at[k], sibling).start()

    @pl.when(r == 0)
    def _():
        for cp in tile_rows(0):
            cp.wait()

    @pl.when(r == 1)
    def _():
        for cp in tile_rows(4):
            cp.wait()

        @pl.when(c == 2)
        def _():
            for cp in extra_rows():
                cp.wait()

    @pl.when(r >= 11)
    def _():
        for n in range(2):
            pass_in(n).wait()
            pass_out(n).start()

    @pl.when(full & (c > 2))
    def _():
        pass_in(1).wait()
        pass_out(1).start()

    @pl.when(full)
    def _():
        target(0).start()

        @pl.when(c == 2)
        def _():
            target(1).start()

    def within(n, count):
        return (n >= 0) & (n < count)

    def c_event(n):
        k = lax.div(n, 8)
        ref = v.at[k, pl.ds(pl.multiple_of(lax.rem(n, 8) * 32, 32), 32), :]

        @pl.when(r != 0)
        def _():
            arrived(ref, c_recv.at[n])

        forward(c_out, ref, lambda d: c_send.at[d, k], c_recv.at[n])

    def d_event(n):
        k = lax.div(n, 8)
        ref = v.at[4 + k, pl.ds(pl.multiple_of(lax.rem(n, 8) * 32, 32), 32), :]

        @pl.when(r != 1)
        def _():
            arrived(ref, d_recv.at[n])

        forward(d_out, ref, lambda d: d_send.at[d], d_recv.at[n])

    def e_ref(n):
        return v10.at[lax.div(n, 4), pl.ds(pl.multiple_of(lax.rem(n, 4) * 64, 64), 64), :]

    def e_even(m):
        n = 2 * m

        @pl.when(r != 1)
        def _():
            arrived(e_ref(n), e_recv.at[n])

        forward(d_out, e_ref(n), lambda d: e_send.at[0, d], e_recv.at[n])

    def e_odd(m):
        n = 2 * m + 1

        @pl.when(r != 1)
        def _():
            arrived(e_ref(n), e_recv.at[n])

        forward(c_out[:3] + (c_out[3] | (r == 1),), e_ref(n), lambda d: e_send.at[1, d], e_recv.at[n])

    def r_rows(n, half):
        return pl.ds(pl.multiple_of(half * 512 + lax.rem(n, 4) * 128, 128), 128)

    def r_event(n):
        b = lax.div(n, 4)
        ref = w.at[b, r_rows(n, core), :]

        @pl.when(y == 0)
        def _():
            m = lax.rem(b, 4)

            @pl.when(lax.rem(n, 4) == 0)
            def _():
                @pl.when(lax.div(b, 4) == core)
                def _():
                    arrived(w.at[b], load.at[m])

                @pl.when(lax.div(b, 4) != core)
                def _():
                    arrived(w.at[b], r_sib.at[m])

            remote(ref, ref, r_send.at[0, b], r_own.at[n], (r, 2 + core)).start()
            remote(ref, ref, r_send.at[1, b], r_own.at[n], (r, 6 + core)).start()

        @pl.when(y != 0)
        def _():
            arrived(ref, r_own.at[n])
            remote(ref, ref, r_send.at[2, b], r_sib.at[n], sibling).start()
            odd = lax.rem(n, 2)

            @pl.when(((y == 1) & (odd == 0)) | ((y == 3) & (odd == 1)))
            def _():
                remote(ref, ref, r_send.at[0, b], r_own.at[n], (r, 4 + core)).start()

    def w_ready(b):
        @pl.when(y == 0)
        def _():
            drain(r_send.at[0, b], 128)
            drain(r_send.at[1, b], 128)

            @pl.when(lax.div(b, 4) == core)
            def _():
                drain(r_send.at[2, b], 256)

        @pl.when(y != 0)
        def _():
            drain(r_send.at[2, b], 128)

            @pl.when(y != 2)
            def _():
                drain(r_send.at[0, b], 64)

            @pl.loop(4 * b, 4 * b + 4)
            def _(n):
                arrived(w.at[b, r_rows(n, 1 - core), :], r_sib.at[n])

    half_128 = pl.ds(pl.multiple_of(core * HALF, HALF), HALF)
    other_128 = pl.ds(pl.multiple_of(HALF - core * HALF, HALF), HALF)

    def l_event(n, outs, sends, root_row):
        ref = lb.at[n, half_128, :]
        arrived(ref, l_own.at[n])

        @pl.when(full)
        def _():
            remote(ref, ref, s_send, l_sib.at[n], sibling).start()

        forward(outs, ref, lambda d: sends.at[d], l_own.at[n])
        odd = lax.rem(n, 2)

        @pl.when((r == root_row) & (((y == 1) & (odd == 0)) | ((y == 3) & (odd == 1))))
        def _():
            remote(ref, ref, y_send.at[root_row], l_own.at[n], (r, 4 + core)).start()

    def l_ready(lo, count):
        @pl.loop(lo, lo + count)
        def _(n):
            arrived(lb.at[n, other_128, :], l_sib.at[n])

    def a_event(n):
        l_event(n, a_out, a_send, 0)

    def b_event(n):
        l_event(n, b_out, b_send, 1)

    def last_events(k):
        lo = 26 + first_id(k)

        @pl.when(b_in)
        def _():
            @pl.loop(lo, lo + 4 - k)
            def _(n):
                b_event(n)

        @pl.when(full)
        def _():
            l_ready(lo, 4 - k)

    def chain(base, send):
        @pl.loop(0, FB)
        def _(k):
            lo = base + first_id(k)
            block_factor(k, s, work, lb, lo)
            send(lo)

            @pl.loop(k + 1, FB)
            def _(i):
                p = dot_nt(s[k, rows_of(i), :], lb[lo])
                s[k, rows_of(i), :] = p
                lb[lo + i - k] = p
                send(lo + i - k)

            @pl.loop(k + 1, FB)
            def _(j):
                @pl.loop(j, FB)
                def _(i):
                    s[j, rows_of(i), :] = s[j, rows_of(i), :] - dot_nt(s[k, rows_of(i), :], s[k, rows_of(j), :])

    def half_of(core_no):
        return pl.ds(core_no * HALF, HALF)

    def send_f(n):
        for q, h in enumerate((0, 1)):
            remote(lb.at[n, half_of(h), :], lb.at[n, half_of(h), :], root_send.at[8 + q],
                   (l_own if h == 1 else l_sib).at[n], (1, 1)).start()
        for other in (1, 2, 3, 6, 7):
            ref = lb.at[n, half_of(other % 2), :]
            remote(ref, ref, root_send.at[other], l_own.at[n], (0, other)).start()
        forward(a_out, lb.at[n, half_of(0), :], lambda d: a_send.at[d], l_own.at[n])

    def send_g(n, both):
        for other in (0, 2, 3, 6, 7):
            ref = lb.at[n, half_of(other % 2), :]
            remote(ref, ref, root_send.at[other], l_own.at[n], (1, other)).start()
        if both:
            ref = lb.at[n, half_of(1), :]
            remote(ref, ref, root_send.at[8], l_sib.at[n], (1, 0)).start()
        forward(b_out, lb.at[n, half_of(1), :], lambda d: b_send.at[d], l_own.at[n])

    def factor_out():
        return [local(s.at[k], out.at[0, :, pl.ds(k * BLK, BLK)], osem.at[2 + k]) for k in range(FB)]

    @pl.when(is_f)
    def _():
        for k in range(FB):
            arrived(s.at[k, pl.ds(k * BLK, TILE - k * BLK), :], load.at[4 + k])

        @pl.loop(0, 32)
        def _(n):
            c_event(n)

        chain(0, send_f)
        for cp in factor_out():
            cp.start()
        for cp in factor_out():
            cp.wait()
        for k in range(FB):
            drain_outs(c_out, lambda d: c_send.at[d, k], 256)
        drain_outs(a_out, lambda d: a_send.at[d], 320)
        for other in (1, 2, 3, 6, 7, 8, 9):
            drain(root_send.at[other], 320)

    @pl.when(is_g)
    def _():
        for k in range(FB):
            arrived(s.at[k, pl.ds(k * BLK, TILE - k * BLK), :], load.at[4 + k])
            arrived(w.at[k], r_sib.at[k])

        @pl.loop(0, 32)
        def _(n):
            d_event(n)

        @pl.loop(0, FB)
        def _(k):
            lo = first_id(k)

            @pl.loop(lo, lo + 4 - k)
            def _(n):
                arrived(lb.at[n, half_of(1), :], l_own.at[n])
                arrived(lb.at[n, half_of(0), :], l_sib.at[n])

            @pl.loop(0, FB)
            def _(i):
                p = dot_nt(w[k, rows_of(i), :], lb[lo])
                w[k, rows_of(i), :] = p
                lb[10 + 4 * k + i] = p
                send_g(10 + 4 * k + i, True)

            @pl.loop(0, FB)
            def _(j):
                @pl.loop(j, FB)
                def _(i):
                    s[j, rows_of(i), :] = s[j, rows_of(i), :] - dot_nt(w[k, rows_of(i), :], w[k, rows_of(j), :])

            @pl.loop(k + 1, FB)
            def _(j):
                @pl.loop(0, FB)
                def _(i):
                    w[j, rows_of(i), :] = w[j, rows_of(i), :] - dot_nt(w[k, rows_of(i), :], lb[lo + j - k])

        chain(26, lambda n: send_g(n, False))
        for cp in factor_out():
            cp.start()
        for cp in factor_out():
            cp.wait()
        drain_outs(d_out, lambda d: d_send.at[d], 1024)
        drain_outs(b_out, lambda d: b_send.at[d], 832)
        for other in (0, 2, 3, 6, 7):
            drain(root_send.at[other], 832)
        drain(root_send.at[8], 512)

    def low_id(k, m):
        return jnp.where(
            k < 4, first_id(m) + k - m,
            jnp.where(m < 4, 10 + 4 * m + k - 4, 26 + first_id(m - 4) + k - m),
        )

    def v_sub(buf, at, k, m):
        buf[k - at] = buf[k - at] - dot3(split2(lb[low_id(k, m)]), split2(buf[m - at]), 0)

    def v_solve(buf, at, k):
        buf[k - at] = dot3(split2(lb[low_id(k, k)]), split2(buf[k - at]), 0)
        hi, lo = split2(buf[k - at])
        vh[...] = hi
        vw[...] = lo

    def w_sub(k, m):
        w[k] = w[k] - dot3(split2(w[m]), split2(lb[low_id(k, m)]), 1)

    def w_solve(k):
        w[k] = dot3(split2(w[k]), split2(lb[low_id(k, k)]), 1)
        hi, lo = split2(w[k])
        ph[...] = hi
        pw[...] = lo

    def t_sub(slot):
        for n in range(4):
            cols = pl.ds(n * BLK, BLK)
            t[slot, :, cols] = t[slot, :, cols] - dot3((ph[...], pw[...]), (vh[:, cols], vw[:, cols]), 0)

    def one_row(k, start):
        @pl.loop(start, k)
        def _(m):
            v_sub(v, 0, k, m)
            w_sub(k, m)

        v_solve(v, 0, k)
        w_solve(k)
        t_sub(0)

    def row_of_first(k):
        w_ready(k)
        drain_outs(c_out, lambda d: c_send.at[d, k], 256)

        @pl.loop(0, k + 1)
        def _(m):
            l_ready(low_id(k, m), 1)

        @pl.when(k == 0)
        def _():
            target(0).wait()

        one_row(k, 0)

    @pl.when(plain)
    def _():
        @pl.loop(0, jnp.where(c == 2, EXTRA_SLOTS, SLOTS))
        def _(slot):
            n_c = slot - c_depth

            @pl.when(c_in & within(n_c, 32))
            def _():
                c_event(n_c)

            n_d = slot - d_depth

            @pl.when(d_in & within(n_d, 32))
            def _():
                d_event(n_d)

            n_r = slot - y_depth

            @pl.when(full & within(n_r, 32))
            def _():
                r_event(n_r)

            n_a = slot - 7 - a_depth - y_depth

            @pl.when(a_in & within(n_a, 20) & (lax.rem(n_a + 16, 2) == 0))
            def _():
                a_event(lax.div(n_a, 2))

            n_b = slot - 13 - b_depth - y_depth

            @pl.when(b_in & within(n_b, 16))
            def _():
                b_event(10 + n_b)

            @pl.when(c == 2)
            def _():
                n_e = slot - 32 - d_depth

                @pl.when(d_in & within(n_e, 8))
                def _():
                    e_even(n_e)

                n_f = slot - 32 - jnp.where(r == 1, 0, 1 + c_depth)

                @pl.when((c_in | (r == 1)) & within(n_f, 8))
                def _():
                    e_odd(n_f)

            k = jnp.where(slot == 15, 0, jnp.where(slot == 23, 1, jnp.where(slot == 29, 2, jnp.where(slot == 36, 3, -1))))

            @pl.when(full & (k >= 0))
            def _():
                row_of_first(k)

    @pl.when(plain & (r < 2))
    def _():
        @pl.when(r == 0)
        def _():
            for k in range(FB):
                drain_outs(c_out, lambda d: c_send.at[d, k], 256)

        @pl.when(r == 1)
        def _():
            drain_outs(d_out, lambda d: d_send.at[d], 1024)

    @pl.when(r >= 11)
    def _():
        for k in range(FB):
            drain_outs(c_out, lambda d: c_send.at[d, k], 256)
        drain_outs(d_out, lambda d: d_send.at[d], 1024)

    @pl.when(c == 2)
    def _():
        drain_outs(d_out, lambda d: e_send.at[0, d], 512)
        drain_outs(c_out[:3] + (c_out[3] | (r == 1),), lambda d: e_send.at[1, d], 512)

    @pl.when(full)
    def _():
        drain_outs(d_out, lambda d: d_send.at[d], 1024)
        l_ready(10, 16)

        @pl.loop(FB, NB)
        def _(b):
            w_ready(b)

        @pl.when(c == 2)
        def _():
            target(1).wait()

    @pl.when((r == 1) & (c == 0))
    def _():
        for k in range(FB):
            drain(r_send.at[2, k], 256)

    @pl.when(plain)
    def _():
        last_events(0)

        @pl.when(full)
        def _():
            @pl.loop(FB, NB)
            def _(k):
                @pl.loop(0, FB)
                def _(m):
                    v_sub(v, 0, k, m)
                    w_sub(k, m)

        @pl.loop(0, FB)
        def _(k):
            @pl.when(k > 0)
            def _():
                last_events(k)

            @pl.when(full)
            def _():
                one_row(4 + k, 4)

                @pl.when(c == 2)
                def _():
                    @pl.loop(4, 4 + k)
                    def _(m):
                        v_sub(v10, 4, 4 + k, m)

                    v_solve(v10, 4, 4 + k)
                    t_sub(1)

    def run(copies):
        for cp in copies:
            cp.start()
        for cp in copies:
            cp.wait()

    @pl.when(full)
    def _():
        main = local(t.at[0], out.at[slot_a], osem.at[0])

        @pl.when(c < 2)
        def _():
            run([main] + [local(w.at[4 * c + k], out.at[0, :, pl.ds(k * BLK, BLK)], osem.at[2 + k])
                          for k in range(FB)])

        @pl.when(c == 2)
        def _():
            run([main, local(t.at[1], out.at[1], osem.at[1])])

        @pl.when(c > 2)
        def _():
            run([main])
            pass_out(1).wait()

        sent = t.at[:, pl.ds(0, 576)]
        arrived(sent, s_send)

    @pl.when(r >= 11)
    def _():
        for n in range(2):
            pass_out(n).wait()

    @pl.when(r < 2)
    def _():
        t[0] = jnp.zeros((TILE, TILE), F32)
        blank = [local(t.at[0], out.at[n], osem.at[n]) for n in range(2)]

        @pl.when(c <= r)
        def _():
            run(blank[1:])

        @pl.when(c > r)
        def _():
            run(blank)

    @pl.when((r == 1) & (c == 0))
    def _():
        @pl.loop(10, 26)
        def _(n):
            arrived(lb.at[n, half_of(1), :], l_sib.at[n])

        panel = [local(lb.at[10 + 4 * k + j], out.at[0, pl.ds(j * BLK, BLK), pl.ds(k * BLK, BLK)],
                       osem.at[6 + 4 * k + j]) for k in range(FB) for j in range(FB)]
        run(panel)

    @pl.when(plain)
    def _():
        drain_outs(a_out, lambda d: a_send.at[d], 320)
        drain_outs(b_out, lambda d: b_send.at[d], 832)

        @pl.when((r < 2) & ((y == 1) | (y == 3)))
        def _():
            @pl.when(r == 0)
            def _():
                drain(y_send.at[0], 160)

            @pl.when(r == 1)
            def _():
                drain(y_send.at[1], 416)


def on_device(kernel_tiles, profile):
    tiles = kernel_tiles.reshape(2, TILE, TILE)
    dma = pltpu.SemaphoreType.DMA
    out = pl.pallas_call(
        kernel,
        out_shape=jax.ShapeDtypeStruct((2, TILE, TILE), F32),
        in_specs=[pl.BlockSpec(memory_space=pl.ANY)],
        out_specs=pl.BlockSpec(memory_space=pl.ANY),
        scratch_shapes=[
            pltpu.VMEM((NB, TILE, BLK), F32),
            pltpu.VMEM((NB, BLK, TILE), F32),
            pltpu.VMEM((FB, BLK, TILE), F32),
            pltpu.VMEM((2, TILE, TILE), F32),
            pltpu.VMEM((36, BLK, BLK), F32),
            pltpu.VMEM((FB, TILE, BLK), F32),
            pltpu.VMEM((HALF, 2 * HALF), F32),
            pltpu.VMEM((TILE, BLK), BF16),
            pltpu.VMEM((TILE, BLK), BF16),
            pltpu.VMEM((BLK, TILE), BF16),
            pltpu.VMEM((BLK, TILE), BF16),
            dma((12,)), dma((2,)),
            dma((32,)), dma((32,)), dma((16,)),
            dma((32,)), dma((32,)), dma((36,)), dma((36,)),
            dma((4, 4)), dma((4,)), dma((2, 4)), dma((3, 8)),
            dma((4,)), dma((4,)), dma((2,)), dma, dma((10,)), dma((22,)),
        ],
        compiler_params=pltpu.CompilerParams(
            vmem_limit_bytes=58 * 2**20, collective_id=0, has_side_effects=True
        ),
        name="panel_steps",
    )(tiles)
    return out.reshape(kernel_tiles.shape)


def solution(mesh):
    placed = (P(None, "row", None, "col", None, None), P())
    return jax.shard_map(
        on_device,
        mesh=mesh,
        in_specs=placed,
        out_specs=P(None, "row", None, "col", None, None),
        check_vma=False,
    )
```

```python
import jax
import jax.numpy as jnp
from jax import lax
from jax.experimental import pallas as pl
from jax.experimental.pallas import tpu as pltpu
from jax.sharding import PartitionSpec as P

F32 = jnp.float32
BF16 = jnp.bfloat16
TILE = 1024
HALF = 128
BLK = 256
NB = 8


def dot_nt(a, b):
    return lax.dot_general(
        a, b, (((1,), (1,)), ((), ())),
        precision=lax.Precision.HIGHEST, preferred_element_type=F32,
    )


def dot_nn(a, b):
    return lax.dot_general(
        a, b, (((1,), (0,)), ((), ())),
        precision=lax.Precision.HIGHEST, preferred_element_type=F32,
    )


def split3(x):
    high = x.astype(BF16).astype(F32)
    rest = x - high
    mid = rest.astype(BF16).astype(F32)
    return high, mid, rest - mid


def split2(x):
    high = x.astype(BF16)
    return high, (x - high.astype(F32)).astype(BF16)


def dot3(a, b, b_dim):
    dims = (((1,), (b_dim,)), ((), ()))

    def one(p, q):
        return lax.dot_general(p, q, dims, preferred_element_type=F32)

    return one(a[0], b[0]) + one(a[0], b[1]) + one(a[1], b[0])


def leaf(work):
    sub = lax.broadcasted_iota(jnp.int32, (8, 2 * HALF), 0)
    for o in range(0, HALF, 8):
        rows = [jnp.broadcast_to(work[o + p:o + p + 1, :], (8, 2 * HALF)) for p in range(8)]
        a = [
            [jnp.broadcast_to(rows[p][:, o + q:o + q + 1], (8, HALF)) for q in range(p + 1)]
            for p in range(8)
        ]
        low = [[None] * 8 for _ in range(8)]
        done = []
        for q in range(8):
            s = lax.rsqrt(a[q][q])
            for p in range(q + 1, 8):
                low[p][q] = a[p][q] * s
            for p in range(q + 1, 8):
                for t in range(q + 1, p + 1):
                    a[p][t] = a[p][t] - low[p][q] * low[t][q]
            acc = rows[q]
            for t in range(q):
                acc = acc - jnp.concatenate([low[q][t], low[q][t]], axis=1) * done[t]
            done.append(acc * jnp.concatenate([s, s], axis=1))
        u = done[0]
        for q in range(1, 8):
            u = jnp.where(sub == q, done[q], u)
        work[o:o + 8, :] = u
        if o + 8 < HALF:
            h, m, l = split3(u)
            left = jnp.concatenate([v[:, :HALF] for v in (h, h, m, h, l, m)], axis=0).astype(BF16)
            right = jnp.concatenate([h, m, h, l, h, m], axis=0).astype(BF16)
            update = lax.dot_general(
                left, right, (((0,), (0,)), ((), ())), preferred_element_type=F32
            )
            work[o + 8:, :] = work[o + 8:, :] - update[o + 8:, :]


def leaf_factor(work, block):
    ri = lax.broadcasted_iota(jnp.int32, (HALF, HALF), 0)
    ci = lax.broadcasted_iota(jnp.int32, (HALF, HALF), 1)
    work[:, :HALF] = block
    work[:, HALF:] = jnp.where(ri == ci, 1.0, 0.0).astype(F32)
    leaf(work)
    upper = jnp.where(ci >= ri, work[:, :HALF], 0.0)
    inverse = jnp.where(ci <= ri, work[:, HALF:], 0.0)
    return upper, inverse


def block_factor(k, s, work, linv, n):
    here = pl.ds(pl.multiple_of(k * BLK, BLK), BLK)
    block = s[k, here, :]
    u1, inv1 = leaf_factor(work, block[:HALF, :HALF])
    l21 = dot_nt(block[HALF:, :HALF], inv1)
    u2, inv2 = leaf_factor(work, block[HALF:, HALF:] - dot_nt(l21, l21))
    inv21 = -dot_nn(inv2, dot_nn(l21, inv1))
    zero = jnp.zeros((HALF, HALF), F32)
    linv[n, :HALF, :HALF] = inv1
    linv[n, :HALF, HALF:] = zero
    linv[n, HALF:, :HALF] = inv21
    linv[n, HALF:, HALF:] = inv2
    s[k, here, :] = jnp.concatenate(
        [jnp.concatenate([u1.T, zero], axis=1), jnp.concatenate([l21, u2.T], axis=1)], axis=0
    )


def rows_of(i):
    return pl.ds(pl.multiple_of(i * BLK, BLK), BLK)


FB = 4
STREAM_SLOTS = (6, 7, 8, 9, 11, 12, 13, 16, 17, 21)
SLOT_TIME = 1.5
PREP, VSUB, VSOLVE, WSUB, WSOLVE, HSUB, HSOLVE, TSUB = range(8)


def plan():
    stream = [STREAM_SLOTS[4 * k - k * (k - 1) // 2] + 8 for k in range(FB)]
    ops = []

    def add(kind, k, m, ready, after):
        ops.append(((kind, k, m), ready, after))

    for k in range(FB):
        add(PREP, k, 0, max(4 * k + 11, stream[k]), [])
        add(PREP, k, 3, 0, [(HSOLVE, k, 0)])
        add(PREP, k, 1, 8 * k + 15, [])
        add(PREP, k, 2, 8 * k + 13, [])
        add(PREP, FB + k, 0, 2 * k + 15, [])
    for k in range(FB):
        for m in range(k):
            add(WSUB, k, m, 0, [(PREP, k, 0), (WSOLVE, m, 0)])
            add(HSUB, k, m, 0, [(PREP, k, 0), (HSOLVE, m, 0)])
            add(VSUB, k, m, 0, [(PREP, k, 0), (PREP, k, 1), (VSOLVE, m, 0)])
        add(WSOLVE, k, 0, 0, [(PREP, k, 0)] + [(WSUB, k, m) for m in range(k)])
        add(HSOLVE, k, 0, 0, [(PREP, k, 0)] + [(HSUB, k, m) for m in range(k)])
        add(VSOLVE, k, 0, 0, [(PREP, k, 0), (PREP, k, 1)] + [(VSUB, k, m) for m in range(k)])
        add(TSUB, k, 0, 0, [(VSOLVE, k, 0), (WSOLVE, k, 0)])
    for k in range(FB, NB):
        for m in range(FB):
            add(WSUB, k, m, 0, [(PREP, k, 0), (WSOLVE, m, 0), (PREP, m, 3)])
            add(VSUB, k, m, 0, [(PREP, k - FB, 2), (VSOLVE, m, 0), (PREP, m, 3)])
    slots, done, slot = [], set(), 0
    while len(done) < len(ops):
        here, used = [], 0.0
        moved = True
        while moved:
            moved = False
            for op, ready, after in ops:
                cost = {PREP: 0.1, TSUB: 1.8, VSUB: 0.6, VSOLVE: 0.6}.get(op[0], 0.35)
                fits = used == 0.0 or used + cost <= SLOT_TIME + 0.5
                if op not in done and ready <= slot and fits and used < SLOT_TIME and all(o in done for o in after):
                    here.append(op)
                    done.add(op)
                    used += cost
                    moved = True
                    break
        slots.append(here)
        slot += 1
    return slots


def lookup(i, values, other=-1):
    bits = max(1, (len(values) - 1).bit_length())
    at = jnp.clip(i, 0, 2 ** bits - 1)
    level = list(values) + [other] * (2 ** bits - len(values))
    for b in range(bits):
        odd = lax.rem(lax.shift_right_logical(at, b), 2) == 1
        level = [p if isinstance(p, int) and isinstance(q, int) and p == q
                 else jnp.where(odd, jnp.int32(q), jnp.int32(p)) for p, q in zip(level[::2], level[1::2])]
    return jnp.where(at == i, level[0], other)


def first_id(k):
    return 4 * k - lax.div(k * (k - 1), jnp.int32(2))


def kernel(tiles, out, w, v, v10, h, t, lb, s, work, ph, pw, vh, vw,
           load, load_t, c_recv, d_recv, e_recv, h_own, h_full, w_full, p_recv, r_own, r_sib, l_own, l_sib,
           c_send, d_send, e_send, h_send, w_send, r_send, a_send, b_send, y_send, s_send, root_send, osem):
    r = lax.axis_index("row")
    c = lax.axis_index("col")
    x = lax.div(r, 4)
    z = lax.rem(r, 4)
    y = lax.div(c, 2)
    core = lax.rem(c, 2)
    sibling = (r, c + 1 - 2 * core)
    dirs = (
        (lax.rem(x + 1, 4) * 4 + z, c),
        (lax.rem(x + 3, 4) * 4 + z, c),
        (x * 4 + lax.rem(z + 1, 4), c),
        (x * 4 + lax.rem(z + 3, 4), c),
    )
    is_f = (r == 0) & (c == 0)
    is_g = (r == 1) & (c == 1)
    plain = jnp.logical_not(is_f | is_g)
    full = (r >= 2) & (r <= 10)
    slot_a = jnp.where(c >= 2, 0, 1)
    never = r < 0

    c_out = (((x <= 1) & (z == 0)), never, ((x == 1) | (x == 2)) & (z <= 1),
             ((x == 0) & ((z == 0) | (z == 3))) | ((x == 1) & (z == 0)))
    c_in = jnp.logical_not((x == 3) | ((x == 0) & (z == 1)) | ((x == 2) & (z == 3)))
    c_depth = jnp.where(x == 0, lax.rem(4 - z, 4), jnp.where(x == 1, 1 + jnp.minimum(z, 4 - z), 2 + z))
    d_out = (((x == 0) & (z >= 1)) | ((x == 1) & ((z == 1) | (z == 2))), never,
             (x == 0) & ((z == 1) | (z == 2)), ((x == 1) | (x == 2)) & (z == 1))
    d_in = jnp.logical_not((x == 3) | ((x == 0) & (z == 0)) | ((x == 2) & (z == 3)))
    d_depth = jnp.where(x == 0, z - 1, jnp.where(x == 1, jnp.where(z == 0, 2, z), jnp.where(z == 1, 2, 3)))

    def stream_tree(z0):
        dz = lax.rem(z + 4 - z0, 4)
        root = (x == 0) & (z == z0)
        turn = jnp.minimum(dz, 4 - dz)
        outs = (root | (x == 2) | (x == 3), (x == 3) & (z >= 2), (x == 3) & (dz <= 1), (x == 3) & (dz == 0))
        outs = (outs[1], outs[0], outs[2], outs[3])
        depth = jnp.where(root, 0, jnp.where(x == 0, 2, 4 - x) + turn)
        return outs, (x >= 1) | (z >= 2) | root, depth

    y_depth = jnp.where(y == 0, 0, jnp.where(y == 2, 2, 1))
    a_out, a_in, a_depth = stream_tree(0)
    h_out, b_in, b_depth = stream_tree(1)
    b_out = (h_out[0], h_out[1] & (x != 2), h_out[2], h_out[3])
    across = (lax.rem(r + 8, 16), c)
    odd_x = lax.rem(x, 2) == 1

    def remote(src, dst, send, recv, device):
        return pltpu.make_async_remote_copy(
            src_ref=src, dst_ref=dst, send_sem=send, recv_sem=recv,
            device_id=device, device_id_type=pl.DeviceIdType.MESH,
        )

    def arrived(ref, sem):
        pltpu.make_async_copy(ref, ref, sem).wait()

    def drain(sem, rows):
        ref = t.at[0, pl.ds(0, rows)]
        pltpu.make_async_copy(ref, ref, sem).wait()

    def forward(outs, ref, sends, recv):
        for d in range(4):
            @pl.when(outs[d])
            def _():
                remote(ref, ref, sends(d), recv, dirs[d]).start()

    def drain_outs(outs, sends, rows):
        for d in range(4):
            @pl.when(outs[d])
            def _():
                drain(sends(d), rows)

    barrier = pltpu.get_barrier_semaphore()
    for n in range(1, 8):
        pl.semaphore_signal(barrier, inc=1, device_id=(r, lax.rem(c + n, 8)),
                            device_id_type=pl.DeviceIdType.MESH)
    for d in range(4):
        pl.semaphore_signal(barrier, inc=1, device_id=dirs[d], device_id_type=pl.DeviceIdType.MESH)

    @pl.when(is_f | is_g)
    def _():
        pl.semaphore_signal(barrier, inc=1, device_id=(1 - r, 1 - c), device_id_type=pl.DeviceIdType.MESH)

    @pl.when(odd_x)
    def _():
        pl.semaphore_signal(barrier, inc=1, device_id=across, device_id_type=pl.DeviceIdType.MESH)

    def block_cols(n):
        return pl.ds(pl.multiple_of(n * BLK, BLK), BLK)

    half_512 = pl.ds(pl.multiple_of(core * 512, 512), 512)
    other_512 = pl.ds(pl.multiple_of(512 - core * 512, 512), 512)

    def local(src, dst, sem):
        return pltpu.make_async_copy(src, dst, sem)

    @pl.when(is_f | is_g)
    def _():
        for k in range(FB):
            local(tiles.at[0, pl.ds(k * BLK, TILE - k * BLK), pl.ds(k * BLK, BLK)],
                  s.at[k, pl.ds(k * BLK, TILE - k * BLK), :], load.at[4 + k]).start()
            if k:
                s[k, pl.ds(0, k * BLK), :] = jnp.zeros((k * BLK, BLK), F32)

    def tile_rows(base):
        return [local(tiles.at[slot_a, pl.ds(k * BLK, BLK), :], v.at[base + k], load.at[k]) for k in range(FB)]

    def extra_rows():
        return [local(tiles.at[1, pl.ds(k * BLK, BLK), :], v10.at[k], load.at[8 + k]) for k in range(FB)]

    def own_cols():
        return [local(tiles.at[0, half_512, pl.ds(k * BLK, BLK)], w.at[4 * core + k, half_512, :], load.at[k])
                for k in range(FB)]

    def target(n):
        return local(tiles.at[slot_a if n == 0 else 1], t.at[n], load_t.at[n])

    def pass_in(n):
        return local(tiles.at[n], t.at[n], load_t.at[n])

    def pass_out(n):
        return local(t.at[n], out.at[n], osem.at[n])

    @pl.when(r == 0)
    def _():
        for cp in tile_rows(0):
            cp.start()

    @pl.when(r == 1)
    def _():
        for cp in tile_rows(4):
            cp.start()

        @pl.when(c == 2)
        def _():
            for cp in extra_rows():
                cp.start()

    @pl.when(full & (y == 0))
    def _():
        for cp in own_cols():
            cp.start()

    def panel_in():
        return [local(tiles.at[0, :, pl.ds(k * BLK, BLK)], h.at[k], osem.at[2 + k]) for k in range(FB)]

    @pl.when((r == 1) & (c == 0))
    def _():
        for cp in panel_in():
            cp.start()

    @pl.when(r >= 11)
    def _():
        pass_in(0).start()
        pass_in(1).start()

    @pl.when(full & (c > 2))
    def _():
        pass_in(1).start()

    @pl.when(jnp.logical_not(is_f | is_g | odd_x))
    def _():
        pl.semaphore_wait(barrier, 11)

    @pl.when(is_f | is_g | odd_x)
    def _():
        pl.semaphore_wait(barrier, 12)

    @pl.when(full & (y == 0))
    def _():
        for k in range(FB):
            remote(tiles.at[0, other_512, pl.ds(k * BLK, BLK)], w.at[4 * core + k, other_512, :],
                   r_send.at[2, 4 * core + k], r_sib.at[k], sibling).start()

    @pl.when((r == 1) & (c == 0))
    def _():
        for k in range(FB):
            remote(tiles.at[0, :, pl.ds(k * BLK, BLK)], w.at[k],
                   r_send.at[2, k], r_sib.at[k], sibling).start()

    @pl.when(r == 0)
    def _():
        for cp in tile_rows(0):
            cp.wait()

    @pl.when(r == 1)
    def _():
        for cp in tile_rows(4):
            cp.wait()

        @pl.when(c == 2)
        def _():
            for cp in extra_rows():
                cp.wait()

    @pl.when(r >= 11)
    def _():
        for n in range(2):
            pass_in(n).wait()
            pass_out(n).start()

    @pl.when(full & (c > 2))
    def _():
        pass_in(1).wait()
        pass_out(1).start()

    @pl.when(full)
    def _():
        target(0).start()

        @pl.when(c == 2)
        def _():
            target(1).start()

    def within(n, count):
        return (n >= 0) & (n < count)

    def c_event(n):
        k = lax.div(n, 8)
        ref = v.at[k, pl.ds(pl.multiple_of(lax.rem(n, 8) * 32, 32), 32), :]

        @pl.when(r != 0)
        def _():
            arrived(ref, c_recv.at[n])

        forward(c_out, ref, lambda d: c_send.at[d, k], c_recv.at[n])

    def d_event(n):
        k = lax.div(n, 8)
        ref = v.at[4 + k, pl.ds(pl.multiple_of(lax.rem(n, 8) * 32, 32), 32), :]

        @pl.when(r != 1)
        def _():
            arrived(ref, d_recv.at[n])

        forward(d_out, ref, lambda d: d_send.at[d, k], d_recv.at[n])

    def e_ref(n):
        return v10.at[lax.div(n, 4), pl.ds(pl.multiple_of(lax.rem(n, 4) * 64, 64), 64), :]

    def e_even(m):
        n = 2 * m

        @pl.when(r != 1)
        def _():
            arrived(e_ref(n), e_recv.at[n])

        forward(d_out, e_ref(n), lambda d: e_send.at[0, d], e_recv.at[n])

    def e_odd(m):
        n = 2 * m + 1

        @pl.when(r != 1)
        def _():
            arrived(e_ref(n), e_recv.at[n])

        forward(c_out[:3] + (c_out[3] | (r == 1),), e_ref(n), lambda d: e_send.at[1, d], e_recv.at[n])

    def r_ref(n):
        rows = pl.ds(pl.multiple_of(core * 512 + lax.rem(n, 4) * 128, 128), 128)
        return w.at[lax.div(n, 4), rows, :]

    def r_event(n, way, target, first, last):
        @pl.when(y == 0)
        def _():
            if first:
                b = lax.div(n, 4)
                m = lax.rem(b, 4)

                @pl.when((lax.rem(n, 4) == 0) & (lax.div(b, 4) == core))
                def _():
                    arrived(w.at[b, half_512, :], load.at[m])

                @pl.when((lax.rem(n, 4) == 0) & (lax.div(b, 4) != core))
                def _():
                    arrived(w.at[b, half_512, :], r_sib.at[m])

        @pl.when(y != 0)
        def _():
            arrived(r_ref(n), r_own.at[n])

        @pl.when(y != last)
        def _():
            remote(r_ref(n), r_ref(n), r_send.at[way, lax.div(n, 4)], r_own.at[n], (r, target)).start()

    def w_ready(b):
        @pl.when(y != 3)
        def _():
            drain(r_send.at[0, b], 64)

        @pl.when(y != 1)
        def _():
            drain(r_send.at[1, b], 64)

        @pl.when((y == 0) & (lax.div(b, 4) == core))
        def _():
            drain(r_send.at[2, b], 128)

    half_128 = pl.ds(pl.multiple_of(core * HALF, HALF), HALF)
    other_128 = pl.ds(pl.multiple_of(HALF - core * HALF, HALF), HALF)

    def l_event(n, outs, sends, root_row):
        ref = lb.at[n, half_128, :]
        arrived(ref, l_own.at[n])

        @pl.when(full)
        def _():
            remote(ref, ref, s_send, l_sib.at[n], sibling).start()

        forward(outs, ref, lambda d: sends.at[d], l_own.at[n])
        odd = lax.rem(n, 2)

        @pl.when((r == root_row) & (((y == 1) & (odd == 0)) | ((y == 3) & (odd == 1))))
        def _():
            remote(ref, ref, y_send.at[root_row], l_own.at[n], (r, 4 + core)).start()

    def l_ready(lo, count):
        @pl.loop(lo, lo + count)
        def _(n):
            arrived(lb.at[n, other_128, :], l_sib.at[n])

    def a_event(n):
        l_event(n, a_out, a_send, 0)

    def b_event(n):
        l_event(n, b_out, b_send, 1)

        @pl.when(x == 3)
        def _():
            ref = lb.at[n, half_128, :]
            remote(ref, ref, y_send.at[3], l_own.at[n], across).start()

    def h_rows(n, half):
        return pl.ds(pl.multiple_of(half * 512 + lax.rem(n, 4) * 128, 128), 128)

    def h_event(n):
        k = lax.div(n, 4)
        ref = h.at[k, h_rows(n, core), :]
        origin = (r == 1) & (c == 0)

        @pl.when(origin)
        def _():
            @pl.when(lax.rem(n, 4) == 0)
            def _():
                arrived(h.at[k], osem.at[2 + k])

            for other in (1, 2, 3, 6, 7):
                part = h.at[k, h_rows(n, other % 2), :]
                remote(part, part, root_send.at[other], h_own.at[n], (1, other)).start()

        @pl.when(jnp.logical_not(origin))
        def _():
            arrived(ref, h_own.at[n])

        forward(h_out, ref, lambda d: h_send.at[d, k], h_own.at[n])
        odd = lax.rem(n, 2)

        @pl.when((r == 1) & (((y == 1) & (odd == 0)) | ((y == 3) & (odd == 1))))
        def _():
            remote(ref, ref, y_send.at[2], h_own.at[n], (r, 4 + core)).start()

    def h_drain(k):
        drain_outs(h_out, lambda d: h_send.at[d, k], 128)

    def swap(buf, k, send, recv):
        ref = buf.at[k, half_512, :]
        remote(ref, ref, send, recv, sibling).start()

    def swapped(buf, k, recv):
        arrived(buf.at[k, other_512, :], recv)

    def last_events(k):
        lo = 10 + first_id(k)

        @pl.when(b_in)
        def _():
            @pl.loop(lo, lo + 4 - k)
            def _(n):
                b_event(n)

        @pl.when(full)
        def _():
            l_ready(lo, 4 - k)

    def chain(base, send):
        @pl.loop(0, FB)
        def _(k):
            lo = base + first_id(k)
            block_factor(k, s, work, lb, lo)
            send(lo)

            @pl.loop(k + 1, FB)
            def _(i):
                p = dot_nt(s[k, rows_of(i), :], lb[lo])
                s[k, rows_of(i), :] = p
                lb[lo + i - k] = p
                send(lo + i - k)

            @pl.loop(k + 1, FB)
            def _(j):
                @pl.loop(j, FB)
                def _(i):
                    s[j, rows_of(i), :] = s[j, rows_of(i), :] - dot_nt(s[k, rows_of(i), :], s[k, rows_of(j), :])

    def half_of(core_no):
        return pl.ds(core_no * HALF, HALF)

    def send_f(n):
        for q, h in enumerate((0, 1)):
            remote(lb.at[n, half_of(h), :], lb.at[n, half_of(h), :], root_send.at[8 + q],
                   (l_own if h == 1 else l_sib).at[n], (1, 1)).start()
        for other in (1, 2, 3, 6, 7):
            ref = lb.at[n, half_of(other % 2), :]
            remote(ref, ref, root_send.at[other], l_own.at[n], (0, other)).start()
        forward(a_out, lb.at[n, half_of(0), :], lambda d: a_send.at[d], l_own.at[n])

    def send_g(n):
        for other in (0, 2, 3, 6, 7):
            ref = lb.at[n, half_of(other % 2), :]
            remote(ref, ref, root_send.at[other], l_own.at[n], (1, other)).start()
        forward(b_out, lb.at[n, half_of(1), :], lambda d: b_send.at[d], l_own.at[n])

    def factor_out():
        return [local(s.at[k], out.at[0, :, pl.ds(k * BLK, BLK)], osem.at[2 + k]) for k in range(FB)]

    @pl.when(is_f)
    def _():
        for k in range(FB):
            arrived(s.at[k, pl.ds(k * BLK, TILE - k * BLK), :], load.at[4 + k])

        @pl.loop(0, 32)
        def _(n):
            c_event(n)

        chain(0, send_f)
        for cp in factor_out():
            cp.start()
        for cp in factor_out():
            cp.wait()
        for k in range(FB):
            drain_outs(c_out, lambda d: c_send.at[d, k], 256)
        drain_outs(a_out, lambda d: a_send.at[d], 320)
        for other in (1, 2, 3, 6, 7, 8, 9):
            drain(root_send.at[other], 320)

    @pl.when(is_g)
    def _():
        @pl.loop(0, 32)
        def _(n):
            d_event(n)

        @pl.loop(0, 16)
        def _(n):
            h_event(n)

        for k in range(FB):
            arrived(s.at[k, pl.ds(k * BLK, TILE - k * BLK), :], load.at[4 + k])
            arrived(w.at[k], r_sib.at[k])

        @pl.loop(0, FB)
        def _(k):
            lo = first_id(k)

            @pl.loop(lo, lo + 4 - k)
            def _(n):
                arrived(lb.at[n, half_of(1), :], l_own.at[n])
                arrived(lb.at[n, half_of(0), :], l_sib.at[n])

            @pl.loop(0, FB)
            def _(i):
                p = dot_nt(w[k, rows_of(i), :], lb[lo])
                w[k, rows_of(i), :] = p
                ref = w.at[k, rows_of(i), :]
                remote(ref, ref, root_send.at[8], p_recv.at[4 * k + i], (1, 0)).start()

            @pl.loop(0, FB)
            def _(j):
                @pl.loop(j, FB)
                def _(i):
                    s[j, rows_of(i), :] = s[j, rows_of(i), :] - dot_nt(w[k, rows_of(i), :], w[k, rows_of(j), :])

            @pl.loop(k + 1, FB)
            def _(j):
                @pl.loop(0, FB)
                def _(i):
                    w[j, rows_of(i), :] = w[j, rows_of(i), :] - dot_nt(w[k, rows_of(i), :], lb[lo + j - k])

        chain(10, send_g)
        for cp in factor_out():
            cp.start()
        for cp in factor_out():
            cp.wait()
        for k in range(FB):
            drain_outs(d_out, lambda d: d_send.at[d, k], 256)
            h_drain(k)
        drain_outs(b_out, lambda d: b_send.at[d], 320)
        for other in (0, 2, 3, 6, 7):
            drain(root_send.at[other], 320)
        drain(root_send.at[8], 1024)

    def low_id(k, m):
        return jnp.where(k < FB, first_id(m), 10 + first_id(m - FB)) + k - m

    def v_sub(buf, at, k, low, m):
        buf[k - at] = buf[k - at] - dot3(split2(low), split2(buf[m - at]), 0)

    def v_solve(buf, at, k):
        buf[k - at] = dot3(split2(lb[low_id(k, k)]), split2(buf[k - at]), 0)

    def w_sub(buf, k, low, m):
        buf[k, half_512, :] = buf[k, half_512, :] - dot3(split2(buf[m, half_512, :]), split2(low), 1)

    def w_solve(buf, k, send, recv):
        buf[k, half_512, :] = dot3(split2(buf[k, half_512, :]), split2(lb[low_id(k, k)]), 1)
        swap(buf, k, send, recv)

    def t_sub(slot, k, right):
        hi, lo = split2(w[k])
        ph[...] = hi
        pw[...] = lo
        hi, lo = split2(right)
        vh[...] = hi
        vw[...] = lo
        for n in range(4):
            cols = pl.ds(n * BLK, BLK)
            t[slot, :, cols] = t[slot, :, cols] - dot3((ph[...], pw[...]), (vh[:, cols], vw[:, cols]), 0)

    def late_row(k):
        @pl.loop(FB, k)
        def _(m):
            w_sub(w, k, lb[low_id(k, m)], m)
            v_sub(v, 0, k, lb[low_id(k, m)], m)

        w_solve(w, k, w_send.at[k], w_full.at[k])
        v_solve(v, 0, k)
        swapped(w, k, w_full.at[k])
        t_sub(0, k, v[k])

    def run_op(kind, k, m):
        @pl.when(kind == PREP)
        def _():
            @pl.when(m == 0)
            def _():
                w_ready(k)

                @pl.when(k < FB)
                def _():
                    h_drain(k)

                    @pl.loop(0, k + 1)
                    def _(q):
                        l_ready(low_id(k, q), 1)

            @pl.when(m == 1)
            def _():
                drain_outs(c_out, lambda d: c_send.at[d, k], 256)

                @pl.when(k == 0)
                def _():
                    target(0).wait()

            @pl.when(m == 3)
            def _():
                swapped(h, k, h_full.at[k])

            @pl.when(m == 2)
            def _():
                drain_outs(d_out, lambda d: d_send.at[d, k], 256)

        @pl.when(kind == VSUB)
        def _():
            @pl.when(k < FB)
            def _():
                v_sub(v, 0, k, lb[low_id(k, m)], m)

            @pl.when(k >= FB)
            def _():
                v_sub(v, 0, k, h[m, rows_of(k - FB), :], m)

        @pl.when(kind == WSUB)
        def _():
            @pl.when(k < FB)
            def _():
                w_sub(w, k, lb[low_id(k, m)], m)

            @pl.when(k >= FB)
            def _():
                w_sub(w, k, h[m, rows_of(k - FB), :], m)

        @pl.when(kind == HSUB)
        def _():
            w_sub(h, k, lb[low_id(k, m)], m)

        @pl.when(kind == VSOLVE)
        def _():
            v_solve(v, 0, k)

        @pl.when(kind == WSOLVE)
        def _():
            w_solve(w, k, w_send.at[k], w_full.at[k])

        @pl.when(kind == HSOLVE)
        def _():
            w_solve(h, k, h_send.at[4, k], h_full.at[k])

        @pl.when(kind == TSUB)
        def _():
            swapped(w, k, w_full.at[k])
            t_sub(0, k, v[k])

    table = plan()
    count = [len(ops) for ops in table]
    flat = [64 * kind + 8 * k + m for ops in table for kind, k, m in ops]
    before = [sum(count[:n]) for n in range(len(count))]

    @pl.when(plain)
    def _():
        @pl.loop(0, max(len(table), 50))
        def _(slot):
            n_c = slot - 2 * c_depth

            @pl.when(c_in & within(n_c, 32))
            def _():
                c_event(n_c)

            n_d = slot - 2 * d_depth

            @pl.when(d_in & within(n_d, 32))
            def _():
                d_event(n_d)

            n_r = slot - 2 * y

            @pl.when(full & within(n_r, 16))
            def _():
                r_event(2 * n_r, 0, lax.rem(c + 2, 8), True, 3)

            n_s = slot - 2 * lax.rem(4 - y, 4)

            @pl.when(full & within(n_s, 16))
            def _():
                r_event(2 * n_s + 1, 1, lax.rem(c + 6, 8), False, 1)

            n_a = lookup(slot - a_depth - y_depth, [STREAM_SLOTS.index(q) if q in STREAM_SLOTS else -1
                                                      for q in range(STREAM_SLOTS[-1] + 1)])

            @pl.when(a_in & (n_a >= 0))
            def _():
                a_event(n_a)

            n_h = slot - b_depth - y_depth

            @pl.when(b_in & within(n_h, 16))
            def _():
                h_event(n_h)

            @pl.when(c == 2)
            def _():
                n_e = slot - 32 - 2 * d_depth

                @pl.when(d_in & within(n_e, 8))
                def _():
                    e_even(n_e)

                n_f = slot - 32 - jnp.where(r == 1, 0, 2 + 2 * c_depth)

                @pl.when((c_in | (r == 1)) & within(n_f, 8))
                def _():
                    e_odd(n_f)

            @pl.when(full)
            def _():
                first = lookup(slot, before, 0)

                @pl.loop(first, first + lookup(slot, count, 0))
                def _(n):
                    code = lookup(n, flat)
                    run_op(lax.div(code, 64), lax.rem(lax.div(code, 8), 8), lax.rem(code, 8))

    @pl.when(plain & (r < 2))
    def _():
        @pl.when(r == 0)
        def _():
            for k in range(FB):
                drain_outs(c_out, lambda d: c_send.at[d, k], 256)

        @pl.when(r == 1)
        def _():
            for k in range(FB):
                drain_outs(d_out, lambda d: d_send.at[d, k], 256)
                h_drain(k)

            @pl.when((y == 1) | (y == 3))
            def _():
                drain(y_send.at[2], 256)

            @pl.when(c == 0)
            def _():
                for other in (1, 2, 3, 6, 7):
                    drain(root_send.at[other], 512)

    @pl.when(r >= 11)
    def _():
        for k in range(FB):
            drain_outs(c_out, lambda d: c_send.at[d, k], 256)
            drain_outs(d_out, lambda d: d_send.at[d, k], 256)
            h_drain(k)

    @pl.when(c == 2)
    def _():
        drain_outs(d_out, lambda d: e_send.at[0, d], 512)
        drain_outs(c_out[:3] + (c_out[3] | (r == 1),), lambda d: e_send.at[1, d], 512)

    @pl.when(full & (c == 2))
    def _():
        target(1).wait()

    @pl.when((r == 1) & (c == 0))
    def _():
        for k in range(FB):
            drain(r_send.at[2, k], 256)

    @pl.when(plain)
    def _():
        @pl.loop(0, FB)
        def _(k):
            last_events(k)

            @pl.when(full)
            def _():
                late_row(FB + k)

                @pl.when(c == 2)
                def _():
                    @pl.loop(FB, FB + k)
                    def _(m):
                        v_sub(v10, FB, FB + k, lb[low_id(FB + k, m)], m)

                    v_solve(v10, FB, FB + k)
                    t_sub(1, FB + k, v10[k])

    def run(copies):
        for cp in copies:
            cp.start()
        for cp in copies:
            cp.wait()

    @pl.when(full)
    def _():
        main = local(t.at[0], out.at[slot_a], osem.at[0])

        @pl.when(c < 2)
        def _():
            run([main] + [local(w.at[4 * c + k], out.at[0, :, pl.ds(k * BLK, BLK)], osem.at[2 + k])
                          for k in range(FB)])

        @pl.when(c == 2)
        def _():
            run([main, local(t.at[1], out.at[1], osem.at[1])])

        @pl.when(c > 2)
        def _():
            run([main])
            pass_out(1).wait()

        drain(s_send, 640)
        for k in range(FB):
            drain(h_send.at[4, k], 128)
        for k in range(NB):
            drain(w_send.at[k], 128)

    @pl.when(r >= 11)
    def _():
        for n in range(2):
            pass_out(n).wait()

    @pl.when(r < 2)
    def _():
        t[0] = jnp.zeros((TILE, TILE), F32)
        blank = [local(t.at[0], out.at[n], osem.at[n]) for n in range(2)]

        @pl.when(c <= r)
        def _():
            run(blank[1:])

        @pl.when(c > r)
        def _():
            run(blank)

    @pl.when((r == 1) & (c == 0))
    def _():
        for k in range(FB):
            for i in range(FB):
                arrived(w.at[k, pl.ds(i * BLK, BLK), :], p_recv.at[4 * k + i])
        run([local(w.at[k], out.at[0, :, pl.ds(k * BLK, BLK)], osem.at[2 + k]) for k in range(FB)])

    @pl.when(plain)
    def _():
        drain_outs(a_out, lambda d: a_send.at[d], 320)
        drain_outs(b_out, lambda d: b_send.at[d], 320)

        @pl.when(x == 3)
        def _():
            drain(y_send.at[3], 320)

        @pl.when((r < 2) & ((y == 1) | (y == 3)))
        def _():
            @pl.when(r == 0)
            def _():
                drain(y_send.at[0], 160)

            @pl.when(r == 1)
            def _():
                drain(y_send.at[1], 160)


def on_device(kernel_tiles, profile):
    tiles = kernel_tiles.reshape(2, TILE, TILE)
    dma = pltpu.SemaphoreType.DMA
    out = pl.pallas_call(
        kernel,
        out_shape=jax.ShapeDtypeStruct((2, TILE, TILE), F32),
        in_specs=[pl.BlockSpec(memory_space=pl.ANY)],
        out_specs=pl.BlockSpec(memory_space=pl.ANY),
        scratch_shapes=[
            pltpu.VMEM((NB, TILE, BLK), F32),
            pltpu.VMEM((NB, BLK, TILE), F32),
            pltpu.VMEM((FB, BLK, TILE), F32),
            pltpu.VMEM((FB, TILE, BLK), F32),
            pltpu.VMEM((2, TILE, TILE), F32),
            pltpu.VMEM((20, BLK, BLK), F32),
            pltpu.VMEM((FB, TILE, BLK), F32),
            pltpu.VMEM((HALF, 2 * HALF), F32),
            pltpu.VMEM((TILE, BLK), BF16),
            pltpu.VMEM((TILE, BLK), BF16),
            pltpu.VMEM((BLK, TILE), BF16),
            pltpu.VMEM((BLK, TILE), BF16),
            dma((12,)), dma((2,)),
            dma((32,)), dma((32,)), dma((16,)), dma((16,)), dma((4,)), dma((8,)), dma((16,)),
            dma((32,)), dma((4,)), dma((20,)), dma((20,)),
            dma((4, 4)), dma((4, 4)), dma((2, 4)), dma((5, 4)), dma((8,)), dma((3, 8)),
            dma((4,)), dma((4,)), dma((4,)), dma, dma((10,)), dma((6,)),
        ],
        compiler_params=pltpu.CompilerParams(
            vmem_limit_bytes=58 * 2**20, collective_id=0, has_side_effects=True
        ),
        name="panel_steps",
    )(tiles)
    return out.reshape(kernel_tiles.shape)


def solution(mesh):
    placed = (P(None, "row", None, "col", None, None), P())
    return jax.shard_map(
        on_device,
        mesh=mesh,
        in_specs=placed,
        out_specs=P(None, "row", None, "col", None, None),
        check_vma=False,
    )
```

```python
import jax
import jax.numpy as jnp
from jax import lax
from jax.experimental import pallas as pl
from jax.experimental.pallas import tpu as pltpu
from jax.sharding import PartitionSpec as P

F32 = jnp.float32
BF16 = jnp.bfloat16
TILE = 1024
HALF = 128
BLK = 256
NB = 8
GROUP = 32


def dot_nt(a, b):
    return lax.dot_general(
        a, b, (((1,), (1,)), ((), ())),
        precision=lax.Precision.HIGHEST, preferred_element_type=F32,
    )


def dot_nn(a, b):
    return lax.dot_general(
        a, b, (((1,), (0,)), ((), ())),
        precision=lax.Precision.HIGHEST, preferred_element_type=F32,
    )


def split3(x):
    high = x.astype(BF16).astype(F32)
    rest = x - high
    mid = rest.astype(BF16).astype(F32)
    return high, mid, rest - mid


def split2(x):
    high = x.astype(BF16)
    return high, (x - high.astype(F32)).astype(BF16)


def dot3(a, b, b_dim):
    dims = (((1,), (b_dim,)), ((), ()))

    def one(p, q):
        return lax.dot_general(p, q, dims, preferred_element_type=F32)

    return one(a[0], b[0]) + one(a[0], b[1]) + one(a[1], b[0])


def leaf(work):
    sub = lax.broadcasted_iota(jnp.int32, (8, 2 * HALF), 0)

    def wide(x):
        return jnp.concatenate([x, x], axis=1)

    for o in range(0, HALF, GROUP):
        end = o + GROUP
        for r in range(o, end, 8):
            rows = [jnp.broadcast_to(work[r + p:r + p + 1, :], (8, 2 * HALF)) for p in range(8)]
            a = [
                [jnp.broadcast_to(rows[p][:, r + q:r + q + 1], (8, HALF)) for q in range(p + 1)]
                for p in range(8)
            ]
            low = [[None] * 8 for _ in range(8)]
            done = []
            scale = []
            for q in range(8):
                s = lax.rsqrt(a[q][q])
                scale.append(s)
                for p in range(q + 1, 8):
                    low[p][q] = a[p][q] * s
                for p in range(q + 1, 8):
                    for t in range(q + 1, p + 1):
                        a[p][t] = a[p][t] - low[p][q] * low[t][q]
                acc = rows[q]
                for t in range(q):
                    acc = acc - wide(low[q][t]) * done[t]
                done.append(acc * wide(s))
            u = done[0]
            for q in range(1, 8):
                u = jnp.where(sub == q, done[q], u)
            work[r:r + 8, :] = u
            for r2 in range(r + 8, end, 8):
                x = work[r2:r2 + 8, :]
                cols = []
                for q in range(8):
                    col = jnp.broadcast_to(x[:, r + q:r + q + 1], (8, HALF))
                    for t in range(q):
                        col = col - cols[t] * low[q][t]
                    cols.append(col * scale[q])
                for q in range(8):
                    x = x - wide(cols[q]) * done[q]
                work[r2:r2 + 8, :] = x
        if end < HALF:
            h, m, l = split3(work[o:end, :])
            left = jnp.concatenate([v[:, :HALF] for v in (h, h, m, h, l, m)], axis=0).astype(BF16)
            right = jnp.concatenate([h, m, h, l, h, m], axis=0).astype(BF16)
            update = lax.dot_general(
                left, right, (((0,), (0,)), ((), ())), preferred_element_type=F32
            )
            work[end:, :] = work[end:, :] - update[end:, :]


def leaf_factor(work, block):
    ri = lax.broadcasted_iota(jnp.int32, (HALF, HALF), 0)
    ci = lax.broadcasted_iota(jnp.int32, (HALF, HALF), 1)
    work[:, :HALF] = block
    work[:, HALF:] = jnp.where(ri == ci, 1.0, 0.0).astype(F32)
    leaf(work)
    upper = jnp.where(ci >= ri, work[:, :HALF], 0.0)
    inverse = jnp.where(ci <= ri, work[:, HALF:], 0.0)
    return upper, inverse


def block_factor(k, s, work, linv, n):
    here = pl.ds(pl.multiple_of(k * BLK, BLK), BLK)
    block = s[k, here, :]
    u1, inv1 = leaf_factor(work, block[:HALF, :HALF])
    l21 = dot_nt(block[HALF:, :HALF], inv1)
    u2, inv2 = leaf_factor(work, block[HALF:, HALF:] - dot_nt(l21, l21))
    inv21 = -dot_nn(inv2, dot_nn(l21, inv1))
    zero = jnp.zeros((HALF, HALF), F32)
    linv[n, :HALF, :HALF] = inv1
    linv[n, :HALF, HALF:] = zero
    linv[n, HALF:, :HALF] = inv21
    linv[n, HALF:, HALF:] = inv2
    s[k, here, :] = jnp.concatenate(
        [jnp.concatenate([u1.T, zero], axis=1), jnp.concatenate([l21, u2.T], axis=1)], axis=0
    )


def rows_of(i):
    return pl.ds(pl.multiple_of(i * BLK, BLK), BLK)


FB = 4
STREAM_SLOTS = (5, 6, 7, 8, 9, 10, 11, 13, 14, 17)
LAST_SLOTS = (21, 22, 23, 24, 25, 26, 27, 29, 30, 32)
PANEL_SLOTS = (0, 1, 2, 3, 4, 12, 15, 16, 18, 19, 20, 21, 22, 23, 24, 25)
EXTRA_SLOT = 32
SLOT_TIME = 1.5
PREP, VSUB, VSOLVE, WSUB, WSOLVE, HSUB, HSOLVE, TSUB, XSUB, XSOLVE, XT = range(11)


def plan():
    stream = [q[4 * k - k * (k - 1) // 2] + 8 for q in (STREAM_SLOTS, LAST_SLOTS) for k in range(FB)]
    ops = []

    def add(kind, k, m, ready, after):
        ops.append(((kind, k, m), ready, after))

    for k in range(FB):
        add(PREP, k, 0, max(PANEL_SLOTS[4 * k + 3] + 8, stream[k]), [])
        add(PREP, k, 3, 0, [(HSOLVE, k, 0)])
        add(PREP, k, 1, 8 * k + 15, [])
        add(PREP, k, 2, 8 * k + 13, [])
        add(PREP, FB + k, 0, 2 * k + 15, [])
        add(PREP, FB + k, 4, stream[FB + k], [])
        add(PREP, FB + k, 5, EXTRA_SLOT + 2 * k + 11, [])
    for k in range(FB):
        for m in range(k):
            add(WSUB, k, m, 0, [(PREP, k, 0), (WSOLVE, m, 0)])
            add(HSUB, k, m, 0, [(PREP, k, 0), (HSOLVE, m, 0)])
            add(VSUB, k, m, 0, [(PREP, k, 0), (PREP, k, 1), (VSOLVE, m, 0)])
        add(WSOLVE, k, 0, 0, [(PREP, k, 0)] + [(WSUB, k, m) for m in range(k)])
        add(HSOLVE, k, 0, 0, [(PREP, k, 0)] + [(HSUB, k, m) for m in range(k)])
        add(VSOLVE, k, 0, 0, [(PREP, k, 0), (PREP, k, 1)] + [(VSUB, k, m) for m in range(k)])
        add(TSUB, k, 0, 0, [(VSOLVE, k, 0), (WSOLVE, k, 0)])
    for k in range(FB, NB):
        for m in range(FB):
            add(WSUB, k, m, 0, [(PREP, k, 0), (WSOLVE, m, 0), (PREP, m, 3)])
            add(VSUB, k, m, 0, [(PREP, k - FB, 2), (VSOLVE, m, 0), (PREP, m, 3)])
        for m in range(FB, k):
            add(WSUB, k, m, 0, [(PREP, k, 0), (PREP, k, 4), (WSOLVE, m, 0)])
            add(VSUB, k, m, 0, [(PREP, k - FB, 2), (PREP, k, 4), (VSOLVE, m, 0)])
            add(XSUB, k, m, 0, [(PREP, k, 4), (PREP, k, 5), (XSOLVE, m, 0)])
        add(WSOLVE, k, 0, 0, [(PREP, k, 4)] + [(WSUB, k, m) for m in range(k)])
        add(VSOLVE, k, 0, 0, [(PREP, k, 4)] + [(VSUB, k, m) for m in range(k)])
        add(XSOLVE, k, 0, 0, [(PREP, k, 4), (PREP, k, 5)] + [(XSUB, k, m) for m in range(FB, k)])
        add(TSUB, k, 0, 0, [(VSOLVE, k, 0), (WSOLVE, k, 0)])
        add(XT, k, 0, 0, [(XSOLVE, k, 0), (TSUB, k, 0)])
    slots, done, slot = [], set(), 0
    while len(done) < len(ops):
        here, used = [], 0.0
        moved = True
        while moved:
            moved = False
            for op, ready, after in ops:
                cost = {PREP: 0.1, TSUB: 1.8, VSUB: 0.6, VSOLVE: 0.6, XSUB: 0, XSOLVE: 0, XT: 0}.get(op[0], 0.35)
                fits = used == 0.0 or used + cost <= SLOT_TIME + 0.5
                if op not in done and ready <= slot and fits and used < SLOT_TIME and all(o in done for o in after):
                    here.append(op)
                    done.add(op)
                    used += cost
                    moved = True
                    break
        slots.append(here)
        slot += 1
    return slots


def lookup(i, values, other=-1):
    bits = max(1, (len(values) - 1).bit_length())
    at = jnp.clip(i, 0, 2 ** bits - 1)
    level = list(values) + [other] * (2 ** bits - len(values))
    for b in range(bits):
        odd = lax.rem(lax.shift_right_logical(at, b), 2) == 1
        level = [p if isinstance(p, int) and isinstance(q, int) and p == q
                 else jnp.where(odd, jnp.int32(q), jnp.int32(p)) for p, q in zip(level[::2], level[1::2])]
    return jnp.where(at == i, level[0], other)


def first_id(k):
    return 4 * k - lax.div(k * (k - 1), jnp.int32(2))


def kernel(tiles, out, w, v, v10, h, t, lb, s, work, ph, pw, vh, vw,
           load, load_t, c_recv, d_recv, e_recv, h_own, h_full, w_full, p_recv, r_own, r_sib, l_own, l_sib,
           c_send, d_send, e_send, h_send, w_send, r_send, a_send, b_send, y_send, s_send, root_send, osem):
    r = lax.axis_index("row")
    c = lax.axis_index("col")
    x = lax.div(r, 4)
    z = lax.rem(r, 4)
    y = lax.div(c, 2)
    core = lax.rem(c, 2)
    sibling = (r, c + 1 - 2 * core)
    dirs = (
        (lax.rem(x + 1, 4) * 4 + z, c),
        (lax.rem(x + 3, 4) * 4 + z, c),
        (x * 4 + lax.rem(z + 1, 4), c),
        (x * 4 + lax.rem(z + 3, 4), c),
    )
    is_f = (r == 0) & (c == 0)
    is_g = (r == 1) & (c == 1)
    plain = jnp.logical_not(is_f | is_g)
    full = (r >= 2) & (r <= 10)
    slot_a = jnp.where(c >= 2, 0, 1)
    never = r < 0

    c_out = (((x <= 1) & (z == 0)), never, ((x == 1) | (x == 2)) & (z <= 1),
             ((x == 0) & ((z == 0) | (z == 3))) | ((x == 1) & (z == 0)))
    c_in = jnp.logical_not((x == 3) | ((x == 0) & (z == 1)) | ((x == 2) & (z == 3)))
    c_depth = jnp.where(x == 0, lax.rem(4 - z, 4), jnp.where(x == 1, 1 + jnp.minimum(z, 4 - z), 2 + z))
    d_out = (((x == 0) & (z >= 1)) | ((x == 1) & ((z == 1) | (z == 2))), never,
             (x == 0) & ((z == 1) | (z == 2)), ((x == 1) | (x == 2)) & (z == 1))
    d_in = jnp.logical_not((x == 3) | ((x == 0) & (z == 0)) | ((x == 2) & (z == 3)))
    d_depth = jnp.where(x == 0, z - 1, jnp.where(x == 1, jnp.where(z == 0, 2, z), jnp.where(z == 1, 2, 3)))

    def stream_tree(z0):
        dz = lax.rem(z + 4 - z0, 4)
        root = (x == 0) & (z == z0)
        turn = jnp.minimum(dz, 4 - dz)
        outs = (root | (x == 2) | (x == 3), (x == 3) & (z >= 2), (x == 3) & (dz <= 1), (x == 3) & (dz == 0))
        outs = (outs[1], outs[0], outs[2], outs[3])
        depth = jnp.where(root, 0, jnp.where(x == 0, 2, 4 - x) + turn)
        return outs, (x >= 1) | (z >= 2) | root, depth

    y_depth = jnp.where(y == 0, 0, jnp.where(y == 2, 2, 1))
    a_out, a_in, a_depth = stream_tree(0)
    h_out, b_in, b_depth = stream_tree(1)
    def remote(src, dst, send, recv, device):
        return pltpu.make_async_remote_copy(
            src_ref=src, dst_ref=dst, send_sem=send, recv_sem=recv,
            device_id=device, device_id_type=pl.DeviceIdType.MESH,
        )

    def arrived(ref, sem):
        pltpu.make_async_copy(ref, ref, sem).wait()

    def drain(sem, rows):
        ref = t.at[0, pl.ds(0, rows)]
        pltpu.make_async_copy(ref, ref, sem).wait()

    def forward(outs, ref, sends, recv):
        for d in range(4):
            @pl.when(outs[d])
            def _():
                remote(ref, ref, sends(d), recv, dirs[d]).start()

    def drain_outs(outs, sends, rows):
        for d in range(4):
            @pl.when(outs[d])
            def _():
                drain(sends(d), rows)

    barrier = pltpu.get_barrier_semaphore()
    for n in range(1, 8):
        pl.semaphore_signal(barrier, inc=1, device_id=(r, lax.rem(c + n, 8)),
                            device_id_type=pl.DeviceIdType.MESH)
    for d in range(4):
        pl.semaphore_signal(barrier, inc=1, device_id=dirs[d], device_id_type=pl.DeviceIdType.MESH)

    @pl.when(is_f | is_g)
    def _():
        pl.semaphore_signal(barrier, inc=1, device_id=(1 - r, 1 - c), device_id_type=pl.DeviceIdType.MESH)

    def block_cols(n):
        return pl.ds(pl.multiple_of(n * BLK, BLK), BLK)

    half_512 = pl.ds(pl.multiple_of(core * 512, 512), 512)
    other_512 = pl.ds(pl.multiple_of(512 - core * 512, 512), 512)

    def local(src, dst, sem):
        return pltpu.make_async_copy(src, dst, sem)

    @pl.when(is_f | is_g)
    def _():
        for k in range(FB):
            local(tiles.at[0, pl.ds(k * BLK, TILE - k * BLK), pl.ds(k * BLK, BLK)],
                  s.at[k, pl.ds(k * BLK, TILE - k * BLK), :], load.at[4 + k]).start()
            if k:
                s[k, pl.ds(0, k * BLK), :] = jnp.zeros((k * BLK, BLK), F32)

    def tile_rows(base):
        return [local(tiles.at[slot_a, pl.ds(k * BLK, BLK), :], v.at[base + k], load.at[k]) for k in range(FB)]

    def extra_rows():
        return [local(tiles.at[1, pl.ds(k * BLK, BLK), :], v10.at[k], load.at[8 + k]) for k in range(FB)]

    def own_cols():
        return [local(tiles.at[0, half_512, pl.ds(k * BLK, BLK)], w.at[4 * core + k, half_512, :], load.at[k])
                for k in range(FB)]

    def target(n):
        return local(tiles.at[slot_a if n == 0 else 1], t.at[n], load_t.at[n])

    def pass_in(n):
        return local(tiles.at[n], t.at[n], load_t.at[n])

    def pass_out(n):
        return local(t.at[n], out.at[n], osem.at[n])

    @pl.when(r == 0)
    def _():
        for cp in tile_rows(0):
            cp.start()

    @pl.when(r == 1)
    def _():
        for cp in tile_rows(4):
            cp.start()

        @pl.when(c == 2)
        def _():
            for cp in extra_rows():
                cp.start()

    @pl.when(full & (y == 0))
    def _():
        for cp in own_cols():
            cp.start()

    def panel_in():
        return [local(tiles.at[0, :, pl.ds(k * BLK, BLK)], h.at[k], osem.at[2 + k]) for k in range(FB)]

    @pl.when((r == 1) & (c == 0))
    def _():
        for cp in panel_in():
            cp.start()

    @pl.when(r >= 11)
    def _():
        pass_in(0).start()
        pass_in(1).start()

    @pl.when(full & (c > 2))
    def _():
        pass_in(1).start()

    @pl.when(plain)
    def _():
        pl.semaphore_wait(barrier, 11)

    @pl.when(is_f | is_g)
    def _():
        pl.semaphore_wait(barrier, 12)

    @pl.when(full & (y == 0))
    def _():
        for k in range(FB):
            remote(tiles.at[0, other_512, pl.ds(k * BLK, BLK)], w.at[4 * core + k, other_512, :],
                   r_send.at[2, 4 * core + k], r_sib.at[k], sibling).start()

    @pl.when((r == 1) & (c == 0))
    def _():
        for k in range(FB):
            remote(tiles.at[0, :, pl.ds(k * BLK, BLK)], w.at[k],
                   r_send.at[2, k], r_sib.at[k], sibling).start()

    @pl.when(r == 0)
    def _():
        for cp in tile_rows(0):
            cp.wait()

    @pl.when(r == 1)
    def _():
        for cp in tile_rows(4):
            cp.wait()

        @pl.when(c == 2)
        def _():
            for cp in extra_rows():
                cp.wait()

    @pl.when(r >= 11)
    def _():
        for n in range(2):
            pass_in(n).wait()
            pass_out(n).start()

    @pl.when(full & (c > 2))
    def _():
        pass_in(1).wait()
        pass_out(1).start()

    @pl.when(full)
    def _():
        target(0).start()

        @pl.when(c == 2)
        def _():
            target(1).start()

    def within(n, count):
        return (n >= 0) & (n < count)

    def c_event(n):
        k = lax.div(n, 8)
        ref = v.at[k, pl.ds(pl.multiple_of(lax.rem(n, 8) * 32, 32), 32), :]

        @pl.when(r != 0)
        def _():
            arrived(ref, c_recv.at[n])

        forward(c_out, ref, lambda d: c_send.at[d, k], c_recv.at[n])

    def d_event(n):
        k = lax.div(n, 8)
        ref = v.at[4 + k, pl.ds(pl.multiple_of(lax.rem(n, 8) * 32, 32), 32), :]

        @pl.when(r != 1)
        def _():
            arrived(ref, d_recv.at[n])

        forward(d_out, ref, lambda d: d_send.at[d, k], d_recv.at[n])

    def e_ref(n):
        return v10.at[lax.div(n, 4), pl.ds(pl.multiple_of(lax.rem(n, 4) * 64, 64), 64), :]

    def e_event(n, outs, way):
        @pl.when(r != 1)
        def _():
            arrived(e_ref(n), e_recv.at[n])

        forward(outs, e_ref(n), lambda d: e_send.at[way, d, lax.div(n, 4)], e_recv.at[n])

    e_out = c_out[:3] + (c_out[3] | (r == 1),)

    def e_drain(k):
        drain_outs(d_out, lambda d: e_send.at[0, d, k], 128)
        drain_outs(e_out, lambda d: e_send.at[1, d, k], 128)

    def r_ref(n):
        rows = pl.ds(pl.multiple_of(core * 512 + lax.rem(n, 4) * 128, 128), 128)
        return w.at[lax.div(n, 4), rows, :]

    def r_event(n, way, target, first, last):
        @pl.when(y == 0)
        def _():
            if first:
                b = lax.div(n, 4)
                m = lax.rem(b, 4)

                @pl.when((lax.rem(n, 4) == 0) & (lax.div(b, 4) == core))
                def _():
                    arrived(w.at[b, half_512, :], load.at[m])

                @pl.when((lax.rem(n, 4) == 0) & (lax.div(b, 4) != core))
                def _():
                    arrived(w.at[b, half_512, :], r_sib.at[m])

        @pl.when(y != 0)
        def _():
            arrived(r_ref(n), r_own.at[n])

        @pl.when(y != last)
        def _():
            remote(r_ref(n), r_ref(n), r_send.at[way, lax.div(n, 4)], r_own.at[n], (r, target)).start()

    def w_ready(b):
        @pl.when(y != 3)
        def _():
            drain(r_send.at[0, b], 64)

        @pl.when(y != 1)
        def _():
            drain(r_send.at[1, b], 64)

        @pl.when((y == 0) & (lax.div(b, 4) == core))
        def _():
            drain(r_send.at[2, b], 128)

    half_128 = pl.ds(pl.multiple_of(core * HALF, HALF), HALF)
    other_128 = pl.ds(pl.multiple_of(HALF - core * HALF, HALF), HALF)

    def l_event(n, outs, sends, root_row):
        ref = lb.at[n, half_128, :]
        arrived(ref, l_own.at[n])

        @pl.when(full)
        def _():
            remote(ref, ref, s_send, l_sib.at[n], sibling).start()

        forward(outs, ref, lambda d: sends.at[d], l_own.at[n])
        odd = lax.rem(n, 2)

        @pl.when((r == root_row) & (((y == 1) & (odd == 0)) | ((y == 3) & (odd == 1))))
        def _():
            remote(ref, ref, y_send.at[root_row], l_own.at[n], (r, 4 + core)).start()

    def l_ready(lo, count):
        @pl.loop(lo, lo + count)
        def _(n):
            arrived(lb.at[n, other_128, :], l_sib.at[n])

    def a_event(n):
        l_event(n, a_out, a_send, 0)

    def b_event(n):
        l_event(n, h_out, b_send, 1)

    def h_rows(n, half):
        return pl.ds(pl.multiple_of(half * 512 + lax.rem(n, 4) * 128, 128), 128)

    def h_send_to(n, other):
        part = h.at[lax.div(n, 4), h_rows(n, other % 2), :]
        remote(part, part, root_send.at[other], h_own.at[n], (1, other)).start()

    def h_event(n):
        k = lax.div(n, 4)
        ref = h.at[k, h_rows(n, core), :]
        origin = (r == 1) & (c == 0)

        @pl.when(origin)
        def _():
            for other in (2, 3, 6, 7):
                h_send_to(n, other)

        @pl.when(jnp.logical_not(origin))
        def _():
            arrived(ref, h_own.at[n])

        forward(h_out, ref, lambda d: h_send.at[d, k], h_own.at[n])
        odd = lax.rem(n, 2)

        @pl.when((r == 1) & (((y == 1) & (odd == 0)) | ((y == 3) & (odd == 1))))
        def _():
            remote(ref, ref, y_send.at[2], h_own.at[n], (r, 4 + core)).start()

    def h_drain(k):
        drain_outs(h_out, lambda d: h_send.at[d, k], 128)

    def swap(buf, k, send, recv):
        ref = buf.at[k, half_512, :]
        remote(ref, ref, send, recv, sibling).start()

    def swapped(buf, k, recv):
        arrived(buf.at[k, other_512, :], recv)

    def chain(base, send):
        @pl.loop(0, FB)
        def _(k):
            lo = base + first_id(k)
            block_factor(k, s, work, lb, lo)
            send(lo)

            @pl.loop(k + 1, FB)
            def _(i):
                p = dot_nt(s[k, rows_of(i), :], lb[lo])
                s[k, rows_of(i), :] = p
                lb[lo + i - k] = p
                send(lo + i - k)

            @pl.loop(k + 1, FB)
            def _(j):
                @pl.loop(j, FB)
                def _(i):
                    s[j, rows_of(i), :] = s[j, rows_of(i), :] - dot_nt(s[k, rows_of(i), :], s[k, rows_of(j), :])

    def half_of(core_no):
        return pl.ds(core_no * HALF, HALF)

    def send_f(n):
        for q, h in enumerate((0, 1)):
            remote(lb.at[n, half_of(h), :], lb.at[n, half_of(h), :], root_send.at[8 + q],
                   (l_own if h == 1 else l_sib).at[n], (1, 1)).start()
        for other in (1, 2, 3, 6, 7):
            ref = lb.at[n, half_of(other % 2), :]
            remote(ref, ref, root_send.at[other], l_own.at[n], (0, other)).start()
        forward(a_out, lb.at[n, half_of(0), :], lambda d: a_send.at[d], l_own.at[n])

    def send_g(n):
        for other in (0, 2, 3, 6, 7):
            ref = lb.at[n, half_of(other % 2), :]
            remote(ref, ref, root_send.at[other], l_own.at[n], (1, other)).start()
        forward(h_out, lb.at[n, half_of(1), :], lambda d: b_send.at[d], l_own.at[n])

    def factor_out():
        return [local(s.at[k], out.at[0, :, pl.ds(k * BLK, BLK)], osem.at[2 + k]) for k in range(FB)]

    @pl.when(is_f)
    def _():
        for k in range(FB):
            arrived(s.at[k, pl.ds(k * BLK, TILE - k * BLK), :], load.at[4 + k])

        @pl.loop(0, 32)
        def _(n):
            c_event(n)

        chain(0, send_f)
        for cp in factor_out():
            cp.start()
        for cp in factor_out():
            cp.wait()
        for k in range(FB):
            drain_outs(c_out, lambda d: c_send.at[d, k], 256)
        drain_outs(a_out, lambda d: a_send.at[d], 320)
        for other in (1, 2, 3, 6, 7, 8, 9):
            drain(root_send.at[other], 320)

    @pl.when(is_g)
    def _():
        @pl.loop(0, 32)
        def _(n):
            d_event(n)

        @pl.loop(0, 16)
        def _(n):
            h_event(n)

        for k in range(FB):
            arrived(s.at[k, pl.ds(k * BLK, TILE - k * BLK), :], load.at[4 + k])
            arrived(w.at[k], r_sib.at[k])

        @pl.loop(0, FB)
        def _(k):
            lo = first_id(k)

            @pl.loop(lo, lo + 4 - k)
            def _(n):
                arrived(lb.at[n, half_of(1), :], l_own.at[n])
                arrived(lb.at[n, half_of(0), :], l_sib.at[n])

            @pl.loop(0, FB)
            def _(i):
                p = dot_nt(w[k, rows_of(i), :], lb[lo])
                w[k, rows_of(i), :] = p
                ref = w.at[k, rows_of(i), :]
                remote(ref, ref, root_send.at[8], p_recv.at[4 * k + i], (1, 0)).start()

            @pl.loop(0, FB)
            def _(j):
                @pl.loop(j, FB)
                def _(i):
                    s[j, rows_of(i), :] = s[j, rows_of(i), :] - dot_nt(w[k, rows_of(i), :], w[k, rows_of(j), :])

            @pl.loop(k + 1, FB)
            def _(j):
                @pl.loop(0, FB)
                def _(i):
                    w[j, rows_of(i), :] = w[j, rows_of(i), :] - dot_nt(w[k, rows_of(i), :], lb[lo + j - k])

        chain(10, send_g)
        for cp in factor_out():
            cp.start()
        for cp in factor_out():
            cp.wait()
        for k in range(FB):
            drain_outs(d_out, lambda d: d_send.at[d, k], 256)
            h_drain(k)
        drain_outs(h_out, lambda d: b_send.at[d], 320)
        for other in (0, 2, 3, 6, 7):
            drain(root_send.at[other], 320)
        drain(root_send.at[8], 1024)

    def low_id(k, m):
        return jnp.where(k < FB, first_id(m), 10 + first_id(m - FB)) + k - m

    def v_sub(buf, at, k, low, m):
        buf[k - at] = buf[k - at] - dot3(split2(low), split2(buf[m - at]), 0)

    def v_solve(buf, at, k):
        buf[k - at] = dot3(split2(lb[low_id(k, k)]), split2(buf[k - at]), 0)

    def w_sub(buf, k, low, m):
        buf[k, half_512, :] = buf[k, half_512, :] - dot3(split2(buf[m, half_512, :]), split2(low), 1)

    def w_solve(buf, k, send, recv):
        buf[k, half_512, :] = dot3(split2(buf[k, half_512, :]), split2(lb[low_id(k, k)]), 1)
        swap(buf, k, send, recv)

    def t_sub(slot, k, right):
        hi, lo = split2(w[k])
        ph[...] = hi
        pw[...] = lo
        hi, lo = split2(right)
        vh[...] = hi
        vw[...] = lo
        for n in range(4):
            cols = pl.ds(n * BLK, BLK)
            t[slot, :, cols] = t[slot, :, cols] - dot3((ph[...], pw[...]), (vh[:, cols], vw[:, cols]), 0)

    def run_op(kind, k, m):
        @pl.when(kind == PREP)
        def _():
            @pl.when(m == 0)
            def _():
                w_ready(k)

                @pl.when(k < FB)
                def _():
                    h_drain(k)

                    @pl.loop(0, k + 1)
                    def _(q):
                        l_ready(low_id(k, q), 1)

            @pl.when(m == 1)
            def _():
                drain_outs(c_out, lambda d: c_send.at[d, k], 256)

                @pl.when(k == 0)
                def _():
                    target(0).wait()

            @pl.when(m == 3)
            def _():
                swapped(h, k, h_full.at[k])

            @pl.when(m == 4)
            def _():
                @pl.loop(FB, k + 1)
                def _(q):
                    l_ready(low_id(k, q), 1)

            @pl.when((m == 5) & (c == 2))
            def _():
                e_drain(k - FB)

                @pl.when(k == FB)
                def _():
                    target(1).wait()

            @pl.when(m == 2)
            def _():
                drain_outs(d_out, lambda d: d_send.at[d, k], 256)

        @pl.when(kind == VSUB)
        def _():
            @pl.when((k < FB) | (m >= FB))
            def _():
                v_sub(v, 0, k, lb[low_id(k, m)], m)

            @pl.when((k >= FB) & (m < FB))
            def _():
                v_sub(v, 0, k, h[m, rows_of(k - FB), :], m)

        @pl.when(kind == WSUB)
        def _():
            @pl.when((k < FB) | (m >= FB))
            def _():
                w_sub(w, k, lb[low_id(k, m)], m)

            @pl.when((k >= FB) & (m < FB))
            def _():
                w_sub(w, k, h[m, rows_of(k - FB), :], m)

        @pl.when(kind == HSUB)
        def _():
            w_sub(h, k, lb[low_id(k, m)], m)

        @pl.when(kind == VSOLVE)
        def _():
            v_solve(v, 0, k)

        @pl.when(kind == WSOLVE)
        def _():
            w_solve(w, k, w_send.at[k], w_full.at[k])

        @pl.when(kind == HSOLVE)
        def _():
            w_solve(h, k, h_send.at[4, k], h_full.at[k])

        @pl.when(kind == TSUB)
        def _():
            swapped(w, k, w_full.at[k])
            t_sub(0, k, v[k])

        @pl.when(c == 2)
        def _():
            @pl.when(kind == XSUB)
            def _():
                v_sub(v10, FB, k, lb[low_id(k, m)], m)

            @pl.when(kind == XSOLVE)
            def _():
                v_solve(v10, FB, k)

            @pl.when(kind == XT)
            def _():
                t_sub(1, k, v10[k - FB])

    table = plan()
    count = [len(ops) for ops in table]
    flat = [64 * kind + 8 * k + m for ops in table for kind, k, m in ops]
    before = [sum(count[:n]) for n in range(len(count))]

    @pl.when((r == 1) & (c == 0))
    def _():
        for k in range(FB):
            arrived(h.at[k], osem.at[2 + k])

        @pl.loop(0, 16)
        def _(n):
            h_send_to(n, 1)

    @pl.when(plain)
    def _():
        @pl.loop(0, max(len(table), EXTRA_SLOT + 18))
        def _(slot):
            n_c = slot - 2 * c_depth

            @pl.when(c_in & within(n_c, 32))
            def _():
                c_event(n_c)

            n_d = slot - 2 * d_depth

            @pl.when(d_in & within(n_d, 32))
            def _():
                d_event(n_d)

            n_r = slot - 2 * y

            @pl.when(full & within(n_r, 16))
            def _():
                r_event(2 * n_r, 0, lax.rem(c + 2, 8), True, 3)

            n_s = slot - 2 * lax.rem(4 - y, 4)

            @pl.when(full & within(n_s, 16))
            def _():
                r_event(2 * n_s + 1, 1, lax.rem(c + 6, 8), False, 1)

            n_a = lookup(slot - a_depth - y_depth, [STREAM_SLOTS.index(q) if q in STREAM_SLOTS else -1
                                                      for q in range(STREAM_SLOTS[-1] + 1)])

            @pl.when(a_in & (n_a >= 0))
            def _():
                a_event(n_a)

            n_h = lookup(slot - b_depth - y_depth, [PANEL_SLOTS.index(q) if q in PANEL_SLOTS else -1
                                                    for q in range(PANEL_SLOTS[-1] + 1)])

            @pl.when(b_in & (n_h >= 0))
            def _():
                h_event(n_h)

            n_b = lookup(slot - b_depth - y_depth, [LAST_SLOTS.index(q) if q in LAST_SLOTS else -1
                                                    for q in range(LAST_SLOTS[-1] + 1)])

            @pl.when(b_in & (n_b >= 0))
            def _():
                b_event(10 + n_b)

            @pl.when(c == 2)
            def _():
                n_e = slot - EXTRA_SLOT - 2 * d_depth

                @pl.when(d_in & within(n_e, 8))
                def _():
                    e_event(2 * n_e, d_out, 0)

                n_f = slot - EXTRA_SLOT - jnp.where(r == 1, 0, 2 + 2 * c_depth)

                @pl.when((c_in | (r == 1)) & within(n_f, 8))
                def _():
                    e_event(2 * n_f + 1, e_out, 1)

            @pl.when(full)
            def _():
                first = lookup(slot, before, 0)

                @pl.loop(first, first + lookup(slot, count, 0))
                def _(n):
                    code = lookup(n, flat)
                    run_op(lax.div(code, 64), lax.rem(lax.div(code, 8), 8), lax.rem(code, 8))

    @pl.when(plain & (r < 2))
    def _():
        @pl.when(r == 0)
        def _():
            for k in range(FB):
                drain_outs(c_out, lambda d: c_send.at[d, k], 256)

        @pl.when(r == 1)
        def _():
            for k in range(FB):
                drain_outs(d_out, lambda d: d_send.at[d, k], 256)
                h_drain(k)

            @pl.when((y == 1) | (y == 3))
            def _():
                drain(y_send.at[2], 256)

            @pl.when(c == 0)
            def _():
                for other in (1, 2, 3, 6, 7):
                    drain(root_send.at[other], 512)

    @pl.when(r >= 11)
    def _():
        for k in range(FB):
            drain_outs(c_out, lambda d: c_send.at[d, k], 256)
            drain_outs(d_out, lambda d: d_send.at[d, k], 256)
            h_drain(k)

    @pl.when((c == 2) & jnp.logical_not(full))
    def _():
        for k in range(FB):
            e_drain(k)

    @pl.when((r == 1) & (c == 0))
    def _():
        for k in range(FB):
            drain(r_send.at[2, k], 256)

    def run(copies):
        for cp in copies:
            cp.start()
        for cp in copies:
            cp.wait()

    @pl.when(full)
    def _():
        main = local(t.at[0], out.at[slot_a], osem.at[0])

        @pl.when(c < 2)
        def _():
            run([main] + [local(w.at[4 * c + k], out.at[0, :, pl.ds(k * BLK, BLK)], osem.at[2 + k])
                          for k in range(FB)])

        @pl.when(c == 2)
        def _():
            run([main, local(t.at[1], out.at[1], osem.at[1])])

        @pl.when(c > 2)
        def _():
            run([main])
            pass_out(1).wait()

        drain(s_send, 640)
        for k in range(FB):
            drain(h_send.at[4, k], 128)
        for k in range(NB):
            drain(w_send.at[k], 128)

    @pl.when(r >= 11)
    def _():
        for n in range(2):
            pass_out(n).wait()

    @pl.when(r < 2)
    def _():
        t[0] = jnp.zeros((TILE, TILE), F32)
        blank = [local(t.at[0], out.at[n], osem.at[n]) for n in range(2)]

        @pl.when(c <= r)
        def _():
            run(blank[1:])

        @pl.when(c > r)
        def _():
            run(blank)

    @pl.when((r == 1) & (c == 0))
    def _():
        for k in range(FB):
            for i in range(FB):
                arrived(w.at[k, pl.ds(i * BLK, BLK), :], p_recv.at[4 * k + i])
        run([local(w.at[k], out.at[0, :, pl.ds(k * BLK, BLK)], osem.at[2 + k]) for k in range(FB)])

    @pl.when(plain)
    def _():
        drain_outs(a_out, lambda d: a_send.at[d], 320)
        drain_outs(h_out, lambda d: b_send.at[d], 320)

        @pl.when((r < 2) & ((y == 1) | (y == 3)))
        def _():
            @pl.when(r == 0)
            def _():
                drain(y_send.at[0], 160)

            @pl.when(r == 1)
            def _():
                drain(y_send.at[1], 160)


def on_device(kernel_tiles, profile):
    tiles = kernel_tiles.reshape(2, TILE, TILE)
    dma = pltpu.SemaphoreType.DMA
    out = pl.pallas_call(
        kernel,
        out_shape=jax.ShapeDtypeStruct((2, TILE, TILE), F32),
        in_specs=[pl.BlockSpec(memory_space=pl.ANY)],
        out_specs=pl.BlockSpec(memory_space=pl.ANY),
        scratch_shapes=[
            pltpu.VMEM((NB, TILE, BLK), F32),
            pltpu.VMEM((NB, BLK, TILE), F32),
            pltpu.VMEM((FB, BLK, TILE), F32),
            pltpu.VMEM((FB, TILE, BLK), F32),
            pltpu.VMEM((2, TILE, TILE), F32),
            pltpu.VMEM((20, BLK, BLK), F32),
            pltpu.VMEM((FB, TILE, BLK), F32),
            pltpu.VMEM((HALF, 2 * HALF), F32),
            pltpu.VMEM((TILE, BLK), BF16),
            pltpu.VMEM((TILE, BLK), BF16),
            pltpu.VMEM((BLK, TILE), BF16),
            pltpu.VMEM((BLK, TILE), BF16),
            dma((12,)), dma((2,)),
            dma((32,)), dma((32,)), dma((16,)), dma((16,)), dma((4,)), dma((8,)), dma((16,)),
            dma((32,)), dma((4,)), dma((20,)), dma((20,)),
            dma((4, 4)), dma((4, 4)), dma((2, 4, 4)), dma((5, 4)), dma((8,)), dma((3, 8)),
            dma((4,)), dma((4,)), dma((3,)), dma, dma((10,)), dma((6,)),
        ],
        compiler_params=pltpu.CompilerParams(
            vmem_limit_bytes=58 * 2**20, collective_id=0, has_side_effects=True
        ),
        name="panel_steps",
    )(tiles)
    return out.reshape(kernel_tiles.shape)


def solution(mesh):
    placed = (P(None, "row", None, "col", None, None), P())
    return jax.shard_map(
        on_device,
        mesh=mesh,
        in_specs=placed,
        out_specs=P(None, "row", None, "col", None, None),
        check_vma=False,
    )
```

```python
import jax
import jax.numpy as jnp
from jax import lax
from jax.experimental import pallas as pl
from jax.experimental.pallas import tpu as pltpu
from jax.sharding import PartitionSpec as P

F32 = jnp.float32
BF16 = jnp.bfloat16
TILE = 1024
HALF = 128
BLK = 256
NB = 8
GROUP = 32


def dot_nt(a, b):
    return lax.dot_general(
        a, b, (((1,), (1,)), ((), ())),
        precision=lax.Precision.HIGHEST, preferred_element_type=F32,
    )


def dot_nn(a, b):
    return lax.dot_general(
        a, b, (((1,), (0,)), ((), ())),
        precision=lax.Precision.HIGHEST, preferred_element_type=F32,
    )


def split3(x):
    high = x.astype(BF16).astype(F32)
    rest = x - high
    mid = rest.astype(BF16).astype(F32)
    return high, mid, rest - mid


def split2(x):
    high = x.astype(BF16)
    return high, (x - high.astype(F32)).astype(BF16)


def dot3(a, b, b_dim):
    dims = (((1,), (b_dim,)), ((), ()))

    def one(p, q):
        return lax.dot_general(p, q, dims, preferred_element_type=F32)

    return one(a[0], b[0]) + one(a[0], b[1]) + one(a[1], b[0])


def leaf(work):
    sub = lax.broadcasted_iota(jnp.int32, (8, 2 * HALF), 0)

    def wide(x):
        return jnp.concatenate([x, x], axis=1)

    for o in range(0, HALF, GROUP):
        end = o + GROUP
        for r in range(o, end, 8):
            rows = [jnp.broadcast_to(work[r + p:r + p + 1, :], (8, 2 * HALF)) for p in range(8)]
            a = [
                [jnp.broadcast_to(rows[p][:, r + q:r + q + 1], (8, HALF)) for q in range(p + 1)]
                for p in range(8)
            ]
            low = [[None] * 8 for _ in range(8)]
            done = []
            scale = []
            for q in range(8):
                s = lax.rsqrt(a[q][q])
                scale.append(s)
                for p in range(q + 1, 8):
                    low[p][q] = a[p][q] * s
                for p in range(q + 1, 8):
                    for t in range(q + 1, p + 1):
                        a[p][t] = a[p][t] - low[p][q] * low[t][q]
                acc = rows[q]
                for t in range(q):
                    acc = acc - wide(low[q][t]) * done[t]
                done.append(acc * wide(s))
            u = done[0]
            for q in range(1, 8):
                u = jnp.where(sub == q, done[q], u)
            work[r:r + 8, :] = u
            for r2 in range(r + 8, end, 8):
                x = work[r2:r2 + 8, :]
                cols = []
                for q in range(8):
                    col = jnp.broadcast_to(x[:, r + q:r + q + 1], (8, HALF))
                    for t in range(q):
                        col = col - cols[t] * low[q][t]
                    cols.append(col * scale[q])
                for q in range(8):
                    x = x - wide(cols[q]) * done[q]
                work[r2:r2 + 8, :] = x
        if end < HALF:
            h, m, l = split3(work[o:end, :])
            left = jnp.concatenate([v[:, :HALF] for v in (h, h, m, h, l, m)], axis=0).astype(BF16)
            right = jnp.concatenate([h, m, h, l, h, m], axis=0).astype(BF16)
            update = lax.dot_general(
                left, right, (((0,), (0,)), ((), ())), preferred_element_type=F32
            )
            work[end:, :] = work[end:, :] - update[end:, :]


def leaf_factor(work, block):
    ri = lax.broadcasted_iota(jnp.int32, (HALF, HALF), 0)
    ci = lax.broadcasted_iota(jnp.int32, (HALF, HALF), 1)
    work[:, :HALF] = block
    work[:, HALF:] = jnp.where(ri == ci, 1.0, 0.0).astype(F32)
    leaf(work)
    upper = jnp.where(ci >= ri, work[:, :HALF], 0.0)
    inverse = jnp.where(ci <= ri, work[:, HALF:], 0.0)
    return upper, inverse


def block_factor(k, s, work, linv, n):
    here = pl.ds(pl.multiple_of(k * BLK, BLK), BLK)
    block = s[k, here, :]
    u1, inv1 = leaf_factor(work, block[:HALF, :HALF])
    l21 = dot_nt(block[HALF:, :HALF], inv1)
    u2, inv2 = leaf_factor(work, block[HALF:, HALF:] - dot_nt(l21, l21))
    inv21 = -dot_nn(inv2, dot_nn(l21, inv1))
    zero = jnp.zeros((HALF, HALF), F32)
    linv[n, :HALF, :HALF] = inv1
    linv[n, :HALF, HALF:] = zero
    linv[n, HALF:, :HALF] = inv21
    linv[n, HALF:, HALF:] = inv2
    s[k, here, :] = jnp.concatenate(
        [jnp.concatenate([u1.T, zero], axis=1), jnp.concatenate([l21, u2.T], axis=1)], axis=0
    )


def rows_of(i):
    return pl.ds(pl.multiple_of(i * BLK, BLK), BLK)


FB = 4
STREAM_SLOTS = (5, 6, 7, 8, 9, 10, 11, 13, 14, 17)
LAST_SLOTS = (21, 22, 23, 24, 25, 26, 27, 29, 30, 32)
PANEL_SLOTS = (0, 1, 2, 3, 4, 12, 15, 16, 18, 19, 20, 21, 22, 23, 24, 25)
EXTRA_SLOT = 32
SLOT_TIME = 1.5
PREP, VSUB, VSOLVE, WSUB, WSOLVE, HSUB, HSOLVE, TSUB, XSUB, XSOLVE, XT = range(11)


def plan():
    stream = [q[4 * k - k * (k - 1) // 2] + 8 for q in (STREAM_SLOTS, LAST_SLOTS) for k in range(FB)]
    ops = []

    def add(kind, k, m, ready, after):
        ops.append(((kind, k, m), ready, after))

    for k in range(FB):
        add(PREP, k, 0, max(2 * k + 9, stream[k]), [])
        add(PREP, k, 6, PANEL_SLOTS[4 * k + 3] + 8, [])
        add(PREP, k, 3, 0, [(HSOLVE, k, 0)])
        add(PREP, k, 1, 8 * k + 15, [])
        add(PREP, k, 2, 8 * k + 13, [])
        add(PREP, FB + k, 0, 2 * k + 15, [])
        add(PREP, FB + k, 4, stream[FB + k], [])
        add(PREP, FB + k, 5, EXTRA_SLOT + 2 * k + 11, [])
    for k in range(FB):
        for m in range(k):
            add(WSUB, k, m, 0, [(PREP, k, 0), (WSOLVE, m, 0)])
            add(HSUB, k, m, 0, [(PREP, k, 0), (PREP, k, 6), (HSOLVE, m, 0)])
            add(VSUB, k, m, 0, [(PREP, k, 0), (PREP, k, 1), (VSOLVE, m, 0)])
        add(WSOLVE, k, 0, 0, [(PREP, k, 0)] + [(WSUB, k, m) for m in range(k)])
        add(HSOLVE, k, 0, 0, [(PREP, k, 0), (PREP, k, 6)] + [(HSUB, k, m) for m in range(k)])
        add(VSOLVE, k, 0, 0, [(PREP, k, 0), (PREP, k, 1)] + [(VSUB, k, m) for m in range(k)])
        add(TSUB, k, 0, 0, [(VSOLVE, k, 0), (WSOLVE, k, 0)])
    for k in range(FB, NB):
        for m in range(FB):
            add(WSUB, k, m, 0, [(PREP, k, 0), (WSOLVE, m, 0), (PREP, m, 3)])
            add(VSUB, k, m, 0, [(PREP, k - FB, 2), (VSOLVE, m, 0), (PREP, m, 3)])
        for m in range(FB, k):
            add(WSUB, k, m, 0, [(PREP, k, 0), (PREP, k, 4), (WSOLVE, m, 0)])
            add(VSUB, k, m, 0, [(PREP, k - FB, 2), (PREP, k, 4), (VSOLVE, m, 0)])
            add(XSUB, k, m, 0, [(PREP, k, 4), (PREP, k, 5), (XSOLVE, m, 0)])
        add(WSOLVE, k, 0, 0, [(PREP, k, 4)] + [(WSUB, k, m) for m in range(k)])
        add(VSOLVE, k, 0, 0, [(PREP, k, 4)] + [(VSUB, k, m) for m in range(k)])
        add(XSOLVE, k, 0, 0, [(PREP, k, 4), (PREP, k, 5)] + [(XSUB, k, m) for m in range(FB, k)]
            + [(XT, m, 0) for m in range(FB, k)])
        add(TSUB, k, 0, 0, [(VSOLVE, k, 0), (WSOLVE, k, 0)])
        add(XT, k, 0, 0, [(XSOLVE, k, 0), (TSUB, k, 0)])
    slots, done, slot = [], set(), 0
    while len(done) < len(ops):
        here, used = [], 0.0
        moved = True
        while moved:
            moved = False
            for op, ready, after in ops:
                cost = {PREP: 0.1, TSUB: 1.8, VSUB: 0.6, VSOLVE: 0.6, XSUB: 0, XSOLVE: 0, XT: 0}.get(op[0], 0.35)
                fits = used == 0.0 or used + cost <= SLOT_TIME + 0.5
                if op not in done and ready <= slot and fits and used < SLOT_TIME and all(o in done for o in after):
                    here.append(op)
                    done.add(op)
                    used += cost
                    moved = True
                    break
        slots.append(here)
        slot += 1
    return slots


def lookup(i, values, other=-1):
    bits = max(1, (len(values) - 1).bit_length())
    at = jnp.clip(i, 0, 2 ** bits - 1)
    level = list(values) + [other] * (2 ** bits - len(values))
    for b in range(bits):
        odd = lax.rem(lax.shift_right_logical(at, b), 2) == 1
        level = [p if isinstance(p, int) and isinstance(q, int) and p == q
                 else jnp.where(odd, jnp.int32(q), jnp.int32(p)) for p, q in zip(level[::2], level[1::2])]
    return jnp.where(at == i, level[0], other)


def first_id(k):
    return 4 * k - lax.div(k * (k - 1), jnp.int32(2))


def kernel(tiles, out, w, v, v10, h, t, lb, s, work, ph, pw, vh, vw, xh, xw,
           load, load_t, c_recv, d_recv, e_recv, h_own, h_full, w_full, p_recv, r_own, r_sib, l_own, l_sib,
           c_send, d_send, e_send, h_send, w_send, r_send, a_send, b_send, y_send, s_send, root_send, osem):
    r = lax.axis_index("row")
    c = lax.axis_index("col")
    x = lax.div(r, 4)
    z = lax.rem(r, 4)
    y = lax.div(c, 2)
    core = lax.rem(c, 2)
    sibling = (r, c + 1 - 2 * core)
    dirs = (
        (lax.rem(x + 1, 4) * 4 + z, c),
        (lax.rem(x + 3, 4) * 4 + z, c),
        (x * 4 + lax.rem(z + 1, 4), c),
        (x * 4 + lax.rem(z + 3, 4), c),
    )
    is_f = (r == 0) & (c == 0)
    is_g = (r == 1) & (c == 1)
    plain = jnp.logical_not(is_f | is_g)
    full = (r >= 2) & (r <= 10)
    slot_a = jnp.where(c >= 2, 0, 1)
    never = r < 0

    c_out = (((x <= 1) & (z == 0)), never, ((x == 1) | (x == 2)) & (z <= 1),
             ((x == 0) & ((z == 0) | (z == 3))) | ((x == 1) & (z == 0)))
    c_in = jnp.logical_not((x == 3) | ((x == 0) & (z == 1)) | ((x == 2) & (z == 3)))
    c_depth = jnp.where(x == 0, lax.rem(4 - z, 4), jnp.where(x == 1, 1 + jnp.minimum(z, 4 - z), 2 + z))
    d_out = (((x == 0) & (z >= 1)) | ((x == 1) & ((z == 1) | (z == 2))), never,
             (x == 0) & ((z == 1) | (z == 2)), ((x == 1) | (x == 2)) & (z == 1))
    d_in = jnp.logical_not((x == 3) | ((x == 0) & (z == 0)) | ((x == 2) & (z == 3)))
    d_depth = jnp.where(x == 0, z - 1, jnp.where(x == 1, jnp.where(z == 0, 2, z), jnp.where(z == 1, 2, 3)))

    def stream_tree(z0):
        dz = lax.rem(z + 4 - z0, 4)
        root = (x == 0) & (z == z0)
        turn = jnp.minimum(dz, 4 - dz)
        outs = (root | (x == 2) | (x == 3), (x == 3) & (z >= 2), (x == 3) & (dz <= 1), (x == 3) & (dz == 0))
        outs = (outs[1], outs[0], outs[2], outs[3])
        depth = jnp.where(root, 0, jnp.where(x == 0, 2, 4 - x) + turn)
        return outs, (x >= 1) | (z >= 2) | root, depth

    y_depth = jnp.where(y == 0, 0, jnp.where(y == 2, 2, 1))
    a_out, a_in, a_depth = stream_tree(0)
    h_out, b_in, b_depth = stream_tree(1)
    def remote(src, dst, send, recv, device):
        return pltpu.make_async_remote_copy(
            src_ref=src, dst_ref=dst, send_sem=send, recv_sem=recv,
            device_id=device, device_id_type=pl.DeviceIdType.MESH,
        )

    def arrived(ref, sem):
        pltpu.make_async_copy(ref, ref, sem).wait()

    def drain(sem, rows):
        ref = t.at[0, pl.ds(0, rows)]
        pltpu.make_async_copy(ref, ref, sem).wait()

    def forward(outs, ref, sends, recv):
        for d in range(4):
            @pl.when(outs[d])
            def _():
                remote(ref, ref, sends(d), recv, dirs[d]).start()

    def drain_outs(outs, sends, rows):
        for d in range(4):
            @pl.when(outs[d])
            def _():
                drain(sends(d), rows)

    barrier = pltpu.get_barrier_semaphore()
    for n in range(1, 8):
        pl.semaphore_signal(barrier, inc=1, device_id=(r, lax.rem(c + n, 8)),
                            device_id_type=pl.DeviceIdType.MESH)
    for d in range(4):
        pl.semaphore_signal(barrier, inc=1, device_id=dirs[d], device_id_type=pl.DeviceIdType.MESH)

    @pl.when(is_f | is_g)
    def _():
        pl.semaphore_signal(barrier, inc=1, device_id=(1 - r, 1 - c), device_id_type=pl.DeviceIdType.MESH)

    def block_cols(n):
        return pl.ds(pl.multiple_of(n * BLK, BLK), BLK)

    half_512 = pl.ds(pl.multiple_of(core * 512, 512), 512)
    other_512 = pl.ds(pl.multiple_of(512 - core * 512, 512), 512)

    def local(src, dst, sem):
        return pltpu.make_async_copy(src, dst, sem)

    @pl.when(is_f | is_g)
    def _():
        for k in range(FB):
            local(tiles.at[0, pl.ds(k * BLK, TILE - k * BLK), pl.ds(k * BLK, BLK)],
                  s.at[k, pl.ds(k * BLK, TILE - k * BLK), :], load.at[4 + k]).start()
            if k:
                s[k, pl.ds(0, k * BLK), :] = jnp.zeros((k * BLK, BLK), F32)

    def tile_rows(base):
        return [local(tiles.at[slot_a, pl.ds(k * BLK, BLK), :], v.at[base + k], load.at[k]) for k in range(FB)]

    def extra_rows():
        return [local(tiles.at[1, pl.ds(k * BLK, BLK), :], v10.at[k], load.at[8 + k]) for k in range(FB)]

    def own_cols():
        return [local(tiles.at[0, half_512, pl.ds(k * BLK, BLK)], w.at[4 * core + k, half_512, :], load.at[k])
                for k in range(FB)]

    def target(n):
        return local(tiles.at[slot_a if n == 0 else 1], t.at[n], load_t.at[n])

    def pass_in(n):
        return local(tiles.at[n], t.at[n], load_t.at[n])

    def pass_out(n):
        return local(t.at[n], out.at[n], osem.at[n])

    @pl.when(r == 0)
    def _():
        for cp in tile_rows(0):
            cp.start()

    @pl.when(r == 1)
    def _():
        for cp in tile_rows(4):
            cp.start()

        @pl.when(c == 2)
        def _():
            for cp in extra_rows():
                cp.start()

    @pl.when(full & (y == 0))
    def _():
        for cp in own_cols():
            cp.start()

    def panel_in():
        return [local(tiles.at[0, :, pl.ds(k * BLK, BLK)], h.at[k], osem.at[2 + k]) for k in range(FB)]

    @pl.when((r == 1) & (c == 0))
    def _():
        for cp in panel_in():
            cp.start()

    @pl.when(r >= 11)
    def _():
        pass_in(0).start()
        pass_in(1).start()

    @pl.when(full & (c > 2))
    def _():
        pass_in(1).start()

    @pl.when(plain)
    def _():
        pl.semaphore_wait(barrier, 11)

    @pl.when(is_f | is_g)
    def _():
        pl.semaphore_wait(barrier, 12)

    @pl.when(full & (y == 0))
    def _():
        for k in range(FB):
            remote(tiles.at[0, other_512, pl.ds(k * BLK, BLK)], w.at[4 * core + k, other_512, :],
                   r_send.at[2, 4 * core + k], r_sib.at[k], sibling).start()

    @pl.when((r == 1) & (c == 0))
    def _():
        for k in range(FB):
            remote(tiles.at[0, :, pl.ds(k * BLK, BLK)], w.at[k],
                   r_send.at[2, k], r_sib.at[k], sibling).start()

    @pl.when((r == 1) & (c == 2))
    def _():
        for cp in extra_rows():
            cp.wait()

    @pl.when(r >= 11)
    def _():
        for n in range(2):
            pass_in(n).wait()
            pass_out(n).start()

    @pl.when(full & (c > 2))
    def _():
        pass_in(1).wait()
        pass_out(1).start()

    @pl.when(full)
    def _():
        target(0).start()

        @pl.when(c == 2)
        def _():
            target(1).start()

    def within(n, count):
        return (n >= 0) & (n < count)

    def c_event(n):
        k = lax.div(n, 8)
        ref = v.at[k, pl.ds(pl.multiple_of(lax.rem(n, 8) * 32, 32), 32), :]

        @pl.when(r != 0)
        def _():
            arrived(ref, c_recv.at[n])

        @pl.when((r == 0) & (lax.rem(n, 8) == 0))
        def _():
            arrived(v.at[k], load.at[k])

        forward(c_out, ref, lambda d: c_send.at[d, k], c_recv.at[n])

    def d_event(n):
        k = lax.div(n, 8)
        ref = v.at[4 + k, pl.ds(pl.multiple_of(lax.rem(n, 8) * 32, 32), 32), :]

        @pl.when(r != 1)
        def _():
            arrived(ref, d_recv.at[n])

        @pl.when((r == 1) & (lax.rem(n, 8) == 0))
        def _():
            arrived(v.at[4 + k], load.at[k])

        forward(d_out, ref, lambda d: d_send.at[d, k], d_recv.at[n])

    def e_ref(n):
        return v10.at[lax.div(n, 4), pl.ds(pl.multiple_of(lax.rem(n, 4) * 64, 64), 64), :]

    def e_event(n, outs, way):
        @pl.when(r != 1)
        def _():
            arrived(e_ref(n), e_recv.at[n])

        forward(outs, e_ref(n), lambda d: e_send.at[way, d, lax.div(n, 4)], e_recv.at[n])

    e_out = c_out[:3] + (c_out[3] | (r == 1),)

    def e_drain(k):
        drain_outs(d_out, lambda d: e_send.at[0, d, k], 128)
        drain_outs(e_out, lambda d: e_send.at[1, d, k], 128)

    def r_ref(n):
        rows = pl.ds(pl.multiple_of(core * 512 + lax.rem(n, 4) * 128, 128), 128)
        return w.at[lax.div(n, 4), rows, :]

    def r_event(n, way, target, first, last):
        @pl.when(y == 0)
        def _():
            if first:
                b = lax.div(n, 4)
                m = lax.rem(b, 4)

                @pl.when((lax.rem(n, 4) == 0) & (lax.div(b, 4) == core))
                def _():
                    arrived(w.at[b, half_512, :], load.at[m])

                @pl.when((lax.rem(n, 4) == 0) & (lax.div(b, 4) != core))
                def _():
                    arrived(w.at[b, half_512, :], r_sib.at[m])

        @pl.when(y != 0)
        def _():
            arrived(r_ref(n), r_own.at[n])

        @pl.when(y != last)
        def _():
            remote(r_ref(n), r_ref(n), r_send.at[way, lax.div(n, 4)], r_own.at[n], (r, target)).start()

    def w_ready(b):
        @pl.when(y != 3)
        def _():
            drain(r_send.at[0, b], 64)

        @pl.when(y != 1)
        def _():
            drain(r_send.at[1, b], 64)

        @pl.when((y == 0) & (lax.div(b, 4) == core))
        def _():
            drain(r_send.at[2, b], 128)

    half_128 = pl.ds(pl.multiple_of(core * HALF, HALF), HALF)
    other_128 = pl.ds(pl.multiple_of(HALF - core * HALF, HALF), HALF)

    def l_event(n, outs, sends, root_row):
        ref = lb.at[n, half_128, :]
        arrived(ref, l_own.at[n])

        @pl.when(full)
        def _():
            remote(ref, ref, s_send, l_sib.at[n], sibling).start()

        forward(outs, ref, lambda d: sends.at[d], l_own.at[n])
        odd = lax.rem(n, 2)

        @pl.when((r == root_row) & (((y == 1) & (odd == 0)) | ((y == 3) & (odd == 1))))
        def _():
            remote(ref, ref, y_send.at[root_row], l_own.at[n], (r, 4 + core)).start()

    def l_ready(lo, count):
        @pl.loop(lo, lo + count)
        def _(n):
            arrived(lb.at[n, other_128, :], l_sib.at[n])

    def a_event(n):
        l_event(n, a_out, a_send, 0)

    def b_event(n):
        l_event(n, h_out, b_send, 1)

    def h_rows(n, half):
        return pl.ds(pl.multiple_of(half * 512 + lax.rem(n, 4) * 128, 128), 128)

    def h_send_to(n, other):
        part = h.at[lax.div(n, 4), h_rows(n, other % 2), :]
        remote(part, part, root_send.at[other], h_own.at[n], (1, other)).start()

    def h_event(n):
        k = lax.div(n, 4)
        ref = h.at[k, h_rows(n, core), :]
        origin = (r == 1) & (c == 0)

        @pl.when(origin)
        def _():
            for other in (2, 3, 6, 7):
                h_send_to(n, other)

        @pl.when(jnp.logical_not(origin))
        def _():
            arrived(ref, h_own.at[n])

        forward(h_out, ref, lambda d: h_send.at[d, k], h_own.at[n])
        odd = lax.rem(n, 2)

        @pl.when((r == 1) & (((y == 1) & (odd == 0)) | ((y == 3) & (odd == 1))))
        def _():
            remote(ref, ref, y_send.at[2], h_own.at[n], (r, 4 + core)).start()

    def h_drain(k):
        drain_outs(h_out, lambda d: h_send.at[d, k], 128)

    def swap(buf, k, send, recv):
        ref = buf.at[k, half_512, :]
        remote(ref, ref, send, recv, sibling).start()

    def swapped(buf, k, recv):
        arrived(buf.at[k, other_512, :], recv)

    def chain(base, send):
        @pl.loop(0, FB)
        def _(k):
            lo = base + first_id(k)
            block_factor(k, s, work, lb, lo)
            send(lo)

            @pl.loop(k + 1, FB)
            def _(i):
                p = dot_nt(s[k, rows_of(i), :], lb[lo])
                s[k, rows_of(i), :] = p
                lb[lo + i - k] = p
                send(lo + i - k)

            @pl.loop(k + 1, FB)
            def _(j):
                @pl.loop(j, FB)
                def _(i):
                    s[j, rows_of(i), :] = s[j, rows_of(i), :] - dot_nt(s[k, rows_of(i), :], s[k, rows_of(j), :])

    def half_of(core_no):
        return pl.ds(core_no * HALF, HALF)

    def send_f(n):
        for q, h in enumerate((0, 1)):
            remote(lb.at[n, half_of(h), :], lb.at[n, half_of(h), :], root_send.at[8 + q],
                   (l_own if h == 1 else l_sib).at[n], (1, 1)).start()
        for other in (1, 2, 3, 6, 7):
            ref = lb.at[n, half_of(other % 2), :]
            remote(ref, ref, root_send.at[other], l_own.at[n], (0, other)).start()
        forward(a_out, lb.at[n, half_of(0), :], lambda d: a_send.at[d], l_own.at[n])

    def send_g(n):
        for other in (0, 2, 3, 6, 7):
            ref = lb.at[n, half_of(other % 2), :]
            remote(ref, ref, root_send.at[other], l_own.at[n], (1, other)).start()
        forward(h_out, lb.at[n, half_of(1), :], lambda d: b_send.at[d], l_own.at[n])

    def factor_out():
        return [local(s.at[k], out.at[0, :, pl.ds(k * BLK, BLK)], osem.at[2 + k]) for k in range(FB)]

    @pl.when(is_f)
    def _():
        for k in range(FB):
            arrived(s.at[k, pl.ds(k * BLK, TILE - k * BLK), :], load.at[4 + k])

        @pl.loop(0, 32)
        def _(n):
            c_event(n)

        chain(0, send_f)
        for cp in factor_out():
            cp.start()
        for cp in factor_out():
            cp.wait()
        for k in range(FB):
            drain_outs(c_out, lambda d: c_send.at[d, k], 256)
        drain_outs(a_out, lambda d: a_send.at[d], 320)
        for other in (1, 2, 3, 6, 7, 8, 9):
            drain(root_send.at[other], 320)

    @pl.when(is_g)
    def _():
        @pl.loop(0, 32)
        def _(n):
            d_event(n)

        @pl.loop(0, 16)
        def _(n):
            h_event(n)

        for k in range(FB):
            arrived(s.at[k, pl.ds(k * BLK, TILE - k * BLK), :], load.at[4 + k])
            arrived(w.at[k], r_sib.at[k])

        @pl.loop(0, FB)
        def _(k):
            lo = first_id(k)

            @pl.loop(lo, lo + 4 - k)
            def _(n):
                arrived(lb.at[n, half_of(1), :], l_own.at[n])
                arrived(lb.at[n, half_of(0), :], l_sib.at[n])

            @pl.loop(0, FB)
            def _(i):
                p = dot_nt(w[k, rows_of(i), :], lb[lo])
                w[k, rows_of(i), :] = p
                ref = w.at[k, rows_of(i), :]
                remote(ref, ref, root_send.at[8], p_recv.at[4 * k + i], (1, 0)).start()

            @pl.loop(0, FB)
            def _(j):
                @pl.loop(j, FB)
                def _(i):
                    s[j, rows_of(i), :] = s[j, rows_of(i), :] - dot_nt(w[k, rows_of(i), :], w[k, rows_of(j), :])

            @pl.loop(k + 1, FB)
            def _(j):
                @pl.loop(0, FB)
                def _(i):
                    w[j, rows_of(i), :] = w[j, rows_of(i), :] - dot_nt(w[k, rows_of(i), :], lb[lo + j - k])

        chain(10, send_g)
        for cp in factor_out():
            cp.start()
        for cp in factor_out():
            cp.wait()
        for k in range(FB):
            drain_outs(d_out, lambda d: d_send.at[d, k], 256)
            h_drain(k)
        drain_outs(h_out, lambda d: b_send.at[d], 320)
        for other in (0, 2, 3, 6, 7):
            drain(root_send.at[other], 320)
        drain(root_send.at[8], 1024)

    def low_id(k, m):
        return jnp.where(k < FB, first_id(m), 10 + first_id(m - FB)) + k - m

    def v_sub(k, low, m):
        v[k] = v[k] - dot3(split2(low), (vh[m], vw[m]), 0)

    def v_solve(k):
        solved = dot3(split2(lb[low_id(k, k)]), split2(v[k]), 0)
        hi, lo = split2(solved)
        vh[k] = hi
        vw[k] = lo

    def x_sub(k, m):
        v10[k - FB] = v10[k - FB] - dot3(split2(lb[low_id(k, m)]), split2(v10[m - FB]), 0)

    def x_solve(k):
        v10[k - FB] = dot3(split2(lb[low_id(k, k)]), split2(v10[k - FB]), 0)
        hi, lo = split2(v10[k - FB])
        xh[...] = hi
        xw[...] = lo

    def w_sub(buf, k, low, m):
        buf[k, half_512, :] = buf[k, half_512, :] - dot3(split2(buf[m, half_512, :]), split2(low), 1)

    def w_solve(buf, k, send, recv):
        buf[k, half_512, :] = dot3(split2(buf[k, half_512, :]), split2(lb[low_id(k, k)]), 1)
        swap(buf, k, send, recv)

    def t_sub(slot, k, right):
        hi, lo = split2(w[k])
        ph[...] = hi
        pw[...] = lo
        for n in range(4):
            cols = pl.ds(n * BLK, BLK)
            t[slot, :, cols] = t[slot, :, cols] - dot3(
                (ph[...], pw[...]), (right[0][:, cols], right[1][:, cols]), 0
            )

    def run_op(kind, k, m):
        @pl.when(kind == PREP)
        def _():
            @pl.when(m == 0)
            def _():
                w_ready(k)

                @pl.when(k < FB)
                def _():
                    @pl.loop(0, k + 1)
                    def _(q):
                        l_ready(low_id(k, q), 1)

            @pl.when(m == 1)
            def _():
                drain_outs(c_out, lambda d: c_send.at[d, k], 256)

                @pl.when(k == 0)
                def _():
                    target(0).wait()

            @pl.when(m == 3)
            def _():
                swapped(h, k, h_full.at[k])

            @pl.when(m == 6)
            def _():
                h_drain(k)

            @pl.when(m == 4)
            def _():
                @pl.loop(FB, k + 1)
                def _(q):
                    l_ready(low_id(k, q), 1)

            @pl.when((m == 5) & (c == 2))
            def _():
                e_drain(k - FB)

                @pl.when(k == FB)
                def _():
                    target(1).wait()

            @pl.when(m == 2)
            def _():
                drain_outs(d_out, lambda d: d_send.at[d, k], 256)

        @pl.when(kind == VSUB)
        def _():
            @pl.when((k < FB) | (m >= FB))
            def _():
                v_sub(k, lb[low_id(k, m)], m)

            @pl.when((k >= FB) & (m < FB))
            def _():
                v_sub(k, h[m, rows_of(k - FB), :], m)

        @pl.when(kind == WSUB)
        def _():
            @pl.when((k < FB) | (m >= FB))
            def _():
                w_sub(w, k, lb[low_id(k, m)], m)

            @pl.when((k >= FB) & (m < FB))
            def _():
                w_sub(w, k, h[m, rows_of(k - FB), :], m)

        @pl.when(kind == HSUB)
        def _():
            w_sub(h, k, lb[low_id(k, m)], m)

        @pl.when(kind == VSOLVE)
        def _():
            v_solve(k)

        @pl.when(kind == WSOLVE)
        def _():
            w_solve(w, k, w_send.at[k], w_full.at[k])

        @pl.when(kind == HSOLVE)
        def _():
            w_solve(h, k, h_send.at[4, k], h_full.at[k])

        @pl.when(kind == TSUB)
        def _():
            swapped(w, k, w_full.at[k])
            t_sub(0, k, (vh.at[k], vw.at[k]))

        @pl.when(c == 2)
        def _():
            @pl.when(kind == XSUB)
            def _():
                x_sub(k, m)

            @pl.when(kind == XSOLVE)
            def _():
                x_solve(k)

            @pl.when(kind == XT)
            def _():
                t_sub(1, k, (xh, xw))

    table = plan()
    count = [len(ops) for ops in table]
    flat = [64 * kind + 8 * k + m for ops in table for kind, k, m in ops]
    before = [sum(count[:n]) for n in range(len(count))]

    @pl.when((r == 1) & (c == 0))
    def _():
        for k in range(FB):
            arrived(h.at[k], osem.at[2 + k])

        @pl.loop(0, 16)
        def _(n):
            h_send_to(n, 1)

    @pl.when(plain)
    def _():
        @pl.loop(0, max(len(table), EXTRA_SLOT + 18))
        def _(slot):
            n_c = slot - 2 * c_depth

            @pl.when(c_in & within(n_c, 32))
            def _():
                c_event(n_c)

            n_d = slot - 2 * d_depth

            @pl.when(d_in & within(n_d, 32))
            def _():
                d_event(n_d)

            n_r = slot - 2 * y

            @pl.when(full & within(n_r, 16))
            def _():
                r_event(2 * n_r, 0, lax.rem(c + 2, 8), True, 3)

            n_s = slot - 2 * lax.rem(4 - y, 4)

            @pl.when(full & within(n_s, 16))
            def _():
                r_event(2 * n_s + 1, 1, lax.rem(c + 6, 8), False, 1)

            n_a = lookup(slot - a_depth - y_depth, [STREAM_SLOTS.index(q) if q in STREAM_SLOTS else -1
                                                      for q in range(STREAM_SLOTS[-1] + 1)])

            @pl.when(a_in & (n_a >= 0))
            def _():
                a_event(n_a)

            n_h = lookup(slot - b_depth - y_depth, [PANEL_SLOTS.index(q) if q in PANEL_SLOTS else -1
                                                    for q in range(PANEL_SLOTS[-1] + 1)])

            @pl.when(b_in & (n_h >= 0))
            def _():
                h_event(n_h)

            n_b = lookup(slot - b_depth - y_depth, [LAST_SLOTS.index(q) if q in LAST_SLOTS else -1
                                                    for q in range(LAST_SLOTS[-1] + 1)])

            @pl.when(b_in & (n_b >= 0))
            def _():
                b_event(10 + n_b)

            @pl.when(c == 2)
            def _():
                n_e = slot - EXTRA_SLOT - 2 * d_depth

                @pl.when(d_in & within(n_e, 8))
                def _():
                    e_event(2 * n_e, d_out, 0)

                n_f = slot - EXTRA_SLOT - jnp.where(r == 1, 0, 2 + 2 * c_depth)

                @pl.when((c_in | (r == 1)) & within(n_f, 8))
                def _():
                    e_event(2 * n_f + 1, e_out, 1)

            @pl.when(full)
            def _():
                first = lookup(slot, before, 0)

                @pl.loop(first, first + lookup(slot, count, 0))
                def _(n):
                    code = lookup(n, flat)
                    run_op(lax.div(code, 64), lax.rem(lax.div(code, 8), 8), lax.rem(code, 8))

    @pl.when(plain & (r < 2))
    def _():
        @pl.when(r == 0)
        def _():
            for k in range(FB):
                drain_outs(c_out, lambda d: c_send.at[d, k], 256)

        @pl.when(r == 1)
        def _():
            for k in range(FB):
                drain_outs(d_out, lambda d: d_send.at[d, k], 256)
                h_drain(k)

            @pl.when((y == 1) | (y == 3))
            def _():
                drain(y_send.at[2], 256)

            @pl.when(c == 0)
            def _():
                for other in (1, 2, 3, 6, 7):
                    drain(root_send.at[other], 512)

    @pl.when(r >= 11)
    def _():
        for k in range(FB):
            drain_outs(c_out, lambda d: c_send.at[d, k], 256)
            drain_outs(d_out, lambda d: d_send.at[d, k], 256)
            h_drain(k)

    @pl.when((c == 2) & jnp.logical_not(full))
    def _():
        for k in range(FB):
            e_drain(k)

    @pl.when((r == 1) & (c == 0))
    def _():
        for k in range(FB):
            drain(r_send.at[2, k], 256)

    def run(copies):
        for cp in copies:
            cp.start()
        for cp in copies:
            cp.wait()

    @pl.when(full)
    def _():
        main = local(t.at[0], out.at[slot_a], osem.at[0])

        @pl.when(c < 2)
        def _():
            run([main] + [local(w.at[4 * c + k], out.at[0, :, pl.ds(k * BLK, BLK)], osem.at[2 + k])
                          for k in range(FB)])

        @pl.when(c == 2)
        def _():
            run([main, local(t.at[1], out.at[1], osem.at[1])])

        @pl.when(c > 2)
        def _():
            run([main])
            pass_out(1).wait()

        drain(s_send, 640)
        for k in range(FB):
            drain(h_send.at[4, k], 128)
        for k in range(NB):
            drain(w_send.at[k], 128)

    @pl.when(r >= 11)
    def _():
        for n in range(2):
            pass_out(n).wait()

    @pl.when(r < 2)
    def _():
        t[0] = jnp.zeros((TILE, TILE), F32)
        blank = [local(t.at[0], out.at[n], osem.at[n]) for n in range(2)]

        @pl.when(c <= r)
        def _():
            run(blank[1:])

        @pl.when(c > r)
        def _():
            run(blank)

    @pl.when((r == 1) & (c == 0))
    def _():
        for k in range(FB):
            for i in range(FB):
                arrived(w.at[k, pl.ds(i * BLK, BLK), :], p_recv.at[4 * k + i])
        run([local(w.at[k], out.at[0, :, pl.ds(k * BLK, BLK)], osem.at[2 + k]) for k in range(FB)])

    @pl.when(plain)
    def _():
        drain_outs(a_out, lambda d: a_send.at[d], 320)
        drain_outs(h_out, lambda d: b_send.at[d], 320)

        @pl.when((r < 2) & ((y == 1) | (y == 3)))
        def _():
            @pl.when(r == 0)
            def _():
                drain(y_send.at[0], 160)

            @pl.when(r == 1)
            def _():
                drain(y_send.at[1], 160)


def hand_on(src, out, buf, load, store):
    def parts(n):
        return n // 4, pl.ds(n % 4 * BLK, BLK)

    loads = [pltpu.make_async_copy(src.at[parts(n)], buf.at[parts(n)], load.at[n]) for n in range(8)]
    stores = [pltpu.make_async_copy(buf.at[parts(n)], out.at[parts(n)], store.at[n]) for n in range(8)]
    for cp in loads:
        cp.start()
    for n in range(8):
        loads[n].wait()
        stores[n].start()
    for cp in stores:
        cp.wait()


def on_device(kernel_tiles, profile):
    tiles = kernel_tiles.reshape(2, TILE, TILE)
    dma = pltpu.SemaphoreType.DMA
    out = pl.pallas_call(
        kernel,
        out_shape=jax.ShapeDtypeStruct((2, TILE, TILE), F32),
        in_specs=[pl.BlockSpec(memory_space=pl.ANY)],
        out_specs=pl.BlockSpec(memory_space=pl.ANY),
        scratch_shapes=[
            pltpu.VMEM((NB, TILE, BLK), F32),
            pltpu.VMEM((NB, BLK, TILE), F32),
            pltpu.VMEM((FB, BLK, TILE), F32),
            pltpu.VMEM((FB, TILE, BLK), F32),
            pltpu.VMEM((2, TILE, TILE), F32),
            pltpu.VMEM((20, BLK, BLK), F32),
            pltpu.VMEM((FB, TILE, BLK), F32),
            pltpu.VMEM((HALF, 2 * HALF), F32),
            pltpu.VMEM((TILE, BLK), BF16),
            pltpu.VMEM((TILE, BLK), BF16),
            pltpu.VMEM((NB, BLK, TILE), BF16),
            pltpu.VMEM((NB, BLK, TILE), BF16),
            pltpu.VMEM((BLK, TILE), BF16),
            pltpu.VMEM((BLK, TILE), BF16),
            dma((12,)), dma((2,)),
            dma((32,)), dma((32,)), dma((16,)), dma((16,)), dma((4,)), dma((8,)), dma((16,)),
            dma((32,)), dma((4,)), dma((20,)), dma((20,)),
            dma((4, 4)), dma((4, 4)), dma((2, 4, 4)), dma((5, 4)), dma((8,)), dma((3, 8)),
            dma((4,)), dma((4,)), dma((3,)), dma, dma((10,)), dma((6,)),
        ],
        compiler_params=pltpu.CompilerParams(
            vmem_limit_bytes=58 * 2**20, collective_id=0, has_side_effects=True
        ),
        name="panel_steps",
    )(tiles)
    out = pl.pallas_call(
        hand_on,
        out_shape=jax.ShapeDtypeStruct((2, TILE, TILE), F32),
        in_specs=[pl.BlockSpec(memory_space=pl.ANY)],
        out_specs=pl.BlockSpec(memory_space=pl.ANY),
        scratch_shapes=[pltpu.VMEM((2, TILE, TILE), F32), dma((8,)), dma((8,))],
        compiler_params=pltpu.CompilerParams(vmem_limit_bytes=56 * 2**20),
        name="hand_on",
    )(out)
    return out.reshape(kernel_tiles.shape)


def solution(mesh):
    placed = (P(None, "row", None, "col", None, None), P())
    return jax.shard_map(
        on_device,
        mesh=mesh,
        in_specs=placed,
        out_specs=P(None, "row", None, "col", None, None),
        check_vma=False,
    )
```

```python
import jax
import jax.numpy as jnp
from jax import lax
from jax.experimental import pallas as pl
from jax.experimental.pallas import tpu as pltpu
from jax.sharding import PartitionSpec as P

F32 = jnp.float32
BF16 = jnp.bfloat16
TILE = 1024
HALF = 128
BLK = 256
NB = 8
GROUP = 32


def dot_nt(a, b):
    return lax.dot_general(
        a, b, (((1,), (1,)), ((), ())),
        precision=lax.Precision.HIGHEST, preferred_element_type=F32,
    )


def dot_nn(a, b):
    return lax.dot_general(
        a, b, (((1,), (0,)), ((), ())),
        precision=lax.Precision.HIGHEST, preferred_element_type=F32,
    )


def split3(x):
    high = x.astype(BF16).astype(F32)
    rest = x - high
    mid = rest.astype(BF16).astype(F32)
    return high, mid, rest - mid


def split2(x):
    high = x.astype(BF16)
    return high, (x - high.astype(F32)).astype(BF16)


def dot3(a, b, b_dim):
    dims = (((1,), (b_dim,)), ((), ()))

    def one(p, q):
        return lax.dot_general(p, q, dims, preferred_element_type=F32)

    return one(a[0], b[0]) + one(a[0], b[1]) + one(a[1], b[0])


def leaf(work):
    sub = lax.broadcasted_iota(jnp.int32, (8, 2 * HALF), 0)

    def wide(x):
        return jnp.concatenate([x, x], axis=1)

    for o in range(0, HALF, GROUP):
        end = o + GROUP
        for r in range(o, end, 8):
            rows = [jnp.broadcast_to(work[r + p:r + p + 1, :], (8, 2 * HALF)) for p in range(8)]
            a = [
                [jnp.broadcast_to(rows[p][:, r + q:r + q + 1], (8, HALF)) for q in range(p + 1)]
                for p in range(8)
            ]
            low = [[None] * 8 for _ in range(8)]
            done = []
            scale = []
            for q in range(8):
                s = lax.rsqrt(a[q][q])
                scale.append(s)
                for p in range(q + 1, 8):
                    low[p][q] = a[p][q] * s
                for p in range(q + 1, 8):
                    for t in range(q + 1, p + 1):
                        a[p][t] = a[p][t] - low[p][q] * low[t][q]
                acc = rows[q]
                for t in range(q):
                    acc = acc - wide(low[q][t]) * done[t]
                done.append(acc * wide(s))
            u = done[0]
            for q in range(1, 8):
                u = jnp.where(sub == q, done[q], u)
            work[r:r + 8, :] = u
            for r2 in range(r + 8, end, 8):
                x = work[r2:r2 + 8, :]
                cols = []
                for q in range(8):
                    col = jnp.broadcast_to(x[:, r + q:r + q + 1], (8, HALF))
                    for t in range(q):
                        col = col - cols[t] * low[q][t]
                    cols.append(col * scale[q])
                for q in range(8):
                    x = x - wide(cols[q]) * done[q]
                work[r2:r2 + 8, :] = x
        if end < HALF:
            h, m, l = split3(work[o:end, :])
            left = jnp.concatenate([v[:, :HALF] for v in (h, h, m, h, l, m)], axis=0).astype(BF16)
            right = jnp.concatenate([h, m, h, l, h, m], axis=0).astype(BF16)
            update = lax.dot_general(
                left, right, (((0,), (0,)), ((), ())), preferred_element_type=F32
            )
            work[end:, :] = work[end:, :] - update[end:, :]


def leaf_factor(work, block):
    ri = lax.broadcasted_iota(jnp.int32, (HALF, HALF), 0)
    ci = lax.broadcasted_iota(jnp.int32, (HALF, HALF), 1)
    work[:, :HALF] = block
    work[:, HALF:] = jnp.where(ri == ci, 1.0, 0.0).astype(F32)
    leaf(work)
    upper = jnp.where(ci >= ri, work[:, :HALF], 0.0)
    inverse = jnp.where(ci <= ri, work[:, HALF:], 0.0)
    return upper, inverse


def block_factor(k, s, work, linv, n):
    here = pl.ds(pl.multiple_of(k * BLK, BLK), BLK)
    block = s[k, here, :]
    u1, inv1 = leaf_factor(work, block[:HALF, :HALF])
    l21 = dot_nt(block[HALF:, :HALF], inv1)
    u2, inv2 = leaf_factor(work, block[HALF:, HALF:] - dot_nt(l21, l21))
    inv21 = -dot_nn(inv2, dot_nn(l21, inv1))
    zero = jnp.zeros((HALF, HALF), F32)
    linv[n, :HALF, :HALF] = inv1
    linv[n, :HALF, HALF:] = zero
    linv[n, HALF:, :HALF] = inv21
    linv[n, HALF:, HALF:] = inv2
    s[k, here, :] = jnp.concatenate(
        [jnp.concatenate([u1.T, zero], axis=1), jnp.concatenate([l21, u2.T], axis=1)], axis=0
    )


def rows_of(i):
    return pl.ds(pl.multiple_of(i * BLK, BLK), BLK)


FB = 4
STREAM_SLOTS = (5, 6, 7, 8, 9, 10, 11, 13, 14, 17)
LAST_SLOTS = (21, 22, 23, 24, 25, 26, 27, 29, 30, 32)
PANEL_SLOTS = (0, 1, 2, 3, 4, 12, 15, 16, 18, 19, 20, 21, 22, 23, 24, 25)
EXTRA_SLOT = 26
SLOT_TIME = 1.5
PREP, VSUB, VSOLVE, WSUB, WSOLVE, HSUB, HSOLVE, TSUB, XSUB, XSOLVE, XT = range(11)


def plan():
    stream = [q[4 * k - k * (k - 1) // 2] + 8 for q in (STREAM_SLOTS, LAST_SLOTS) for k in range(FB)]
    ops = []

    def add(kind, k, m, ready, after):
        ops.append(((kind, k, m), ready, after))

    for k in range(FB):
        add(PREP, k, 0, max(2 * k + 9, stream[k]), [])
        add(PREP, k, 6, PANEL_SLOTS[4 * k + 3] + 8, [])
        add(PREP, k, 3, 0, [(HSOLVE, k, 0)])
        add(PREP, k, 1, 8 * k + 15, [])
        add(PREP, k, 2, 8 * k + 13, [])
        add(PREP, FB + k, 0, 2 * k + 15, [])
        add(PREP, FB + k, 4, stream[FB + k], [])
        add(PREP, FB + k, 5, EXTRA_SLOT + 2 * k + 11, [])
    for k in range(FB):
        for m in range(k):
            add(WSUB, k, m, 0, [(PREP, k, 0), (WSOLVE, m, 0)])
            add(HSUB, k, m, 0, [(PREP, k, 0), (PREP, k, 6), (HSOLVE, m, 0)])
            add(VSUB, k, m, 0, [(PREP, k, 0), (PREP, k, 1), (VSOLVE, m, 0)])
        add(WSOLVE, k, 0, 0, [(PREP, k, 0)] + [(WSUB, k, m) for m in range(k)])
        add(HSOLVE, k, 0, 0, [(PREP, k, 0), (PREP, k, 6)] + [(HSUB, k, m) for m in range(k)])
        add(VSOLVE, k, 0, 0, [(PREP, k, 0), (PREP, k, 1)] + [(VSUB, k, m) for m in range(k)])
        add(TSUB, k, 0, 0, [(VSOLVE, k, 0), (WSOLVE, k, 0)])
    for k in range(FB, NB):
        for m in range(FB):
            add(WSUB, k, m, 0, [(PREP, k, 0), (WSOLVE, m, 0), (PREP, m, 3)])
            add(VSUB, k, m, 0, [(PREP, k - FB, 2), (VSOLVE, m, 0), (PREP, m, 3)])
        for m in range(FB, k):
            add(WSUB, k, m, 0, [(PREP, k, 0), (PREP, k, 4), (WSOLVE, m, 0)])
            add(VSUB, k, m, 0, [(PREP, k - FB, 2), (PREP, k, 4), (VSOLVE, m, 0)])
            add(XSUB, k, m, 0, [(PREP, k, 4), (PREP, k, 5), (XSOLVE, m, 0)])
        add(WSOLVE, k, 0, 0, [(PREP, k, 4)] + [(WSUB, k, m) for m in range(k)])
        add(VSOLVE, k, 0, 0, [(PREP, k, 4)] + [(VSUB, k, m) for m in range(k)])
        add(XSOLVE, k, 0, 0, [(PREP, k, 4), (PREP, k, 5)] + [(XSUB, k, m) for m in range(FB, k)]
            + [(XT, m, 0) for m in range(FB, k)])
        add(TSUB, k, 0, 0, [(VSOLVE, k, 0), (WSOLVE, k, 0)])
        add(XT, k, 0, 0, [(XSOLVE, k, 0), (TSUB, k, 0)])
    slots, done, slot = [], set(), 0
    while len(done) < len(ops):
        here, used = [], 0.0
        moved = True
        while moved:
            moved = False
            for op, ready, after in ops:
                cost = {PREP: 0.1, TSUB: 1.8, VSUB: 0.6, VSOLVE: 0.6, XSUB: 0, XSOLVE: 0, XT: 0}.get(op[0], 0.35)
                fits = used == 0.0 or used + cost <= SLOT_TIME + 0.5
                if op not in done and ready <= slot and fits and used < SLOT_TIME and all(o in done for o in after):
                    here.append(op)
                    done.add(op)
                    used += cost
                    moved = True
                    break
        slots.append(here)
        slot += 1
    return slots


def lookup(i, values, other=-1):
    bits = max(1, (len(values) - 1).bit_length())
    at = jnp.clip(i, 0, 2 ** bits - 1)
    level = list(values) + [other] * (2 ** bits - len(values))
    for b in range(bits):
        odd = lax.rem(lax.shift_right_logical(at, b), 2) == 1
        level = [p if isinstance(p, int) and isinstance(q, int) and p == q
                 else jnp.where(odd, jnp.int32(q), jnp.int32(p)) for p, q in zip(level[::2], level[1::2])]
    return jnp.where(at == i, level[0], other)


def first_id(k):
    return 4 * k - lax.div(k * (k - 1), jnp.int32(2))


def kernel(tiles, out, w, v, v10, h, t, lb, s, work, ph, pw, vh, vw, xh, xw,
           load, load_t, c_recv, d_recv, e_recv, h_own, h_full, w_full, p_recv, r_own, r_sib, l_own, l_sib,
           c_send, d_send, e_send, h_send, w_send, r_send, a_send, b_send, y_send, s_send, root_send, osem):
    r = lax.axis_index("row")
    c = lax.axis_index("col")
    x = lax.div(r, 4)
    z = lax.rem(r, 4)
    y = lax.div(c, 2)
    core = lax.rem(c, 2)
    sibling = (r, c + 1 - 2 * core)
    dirs = (
        (lax.rem(x + 1, 4) * 4 + z, c),
        (lax.rem(x + 3, 4) * 4 + z, c),
        (x * 4 + lax.rem(z + 1, 4), c),
        (x * 4 + lax.rem(z + 3, 4), c),
    )
    is_f = (r == 0) & (c == 0)
    is_g = (r == 1) & (c == 1)
    plain = jnp.logical_not(is_f | is_g)
    full = (r >= 2) & (r <= 10)
    slot_a = jnp.where(c >= 2, 0, 1)
    never = r < 0

    c_out = (((x <= 1) & (z == 0)), never, ((x == 1) | (x == 2)) & (z <= 1),
             ((x == 0) & ((z == 0) | (z == 3))) | ((x == 1) & (z == 0)))
    c_in = jnp.logical_not((x == 3) | ((x == 0) & (z == 1)) | ((x == 2) & (z == 3)))
    c_depth = jnp.where(x == 0, lax.rem(4 - z, 4), jnp.where(x == 1, 1 + jnp.minimum(z, 4 - z), 2 + z))
    d_out = (((x == 0) & (z >= 1)) | ((x == 1) & ((z == 1) | (z == 2))), never,
             (x == 0) & ((z == 1) | (z == 2)), ((x == 1) | (x == 2)) & (z == 1))
    d_in = jnp.logical_not((x == 3) | ((x == 0) & (z == 0)) | ((x == 2) & (z == 3)))
    d_depth = jnp.where(x == 0, z - 1, jnp.where(x == 1, jnp.where(z == 0, 2, z), jnp.where(z == 1, 2, 3)))

    def stream_tree(z0):
        dz = lax.rem(z + 4 - z0, 4)
        root = (x == 0) & (z == z0)
        turn = jnp.minimum(dz, 4 - dz)
        outs = (root | (x == 2) | (x == 3), (x == 3) & (z >= 2), (x == 3) & (dz <= 1), (x == 3) & (dz == 0))
        outs = (outs[1], outs[0], outs[2], outs[3])
        depth = jnp.where(root, 0, jnp.where(x == 0, 2, 4 - x) + turn)
        return outs, (x >= 1) | (z >= 2) | root, depth

    y_depth = jnp.where(y == 0, 0, jnp.where(y == 2, 2, 1))
    a_out, a_in, a_depth = stream_tree(0)
    h_out, b_in, b_depth = stream_tree(1)
    def remote(src, dst, send, recv, device):
        return pltpu.make_async_remote_copy(
            src_ref=src, dst_ref=dst, send_sem=send, recv_sem=recv,
            device_id=device, device_id_type=pl.DeviceIdType.MESH,
        )

    def arrived(ref, sem):
        pltpu.make_async_copy(ref, ref, sem).wait()

    def drain(sem, rows):
        ref = t.at[0, pl.ds(0, rows)]
        pltpu.make_async_copy(ref, ref, sem).wait()

    def forward(outs, ref, sends, recv):
        for d in range(4):
            @pl.when(outs[d])
            def _():
                remote(ref, ref, sends(d), recv, dirs[d]).start()

    def drain_outs(outs, sends, rows):
        for d in range(4):
            @pl.when(outs[d])
            def _():
                drain(sends(d), rows)

    barrier = pltpu.get_barrier_semaphore()
    for n in range(1, 8):
        pl.semaphore_signal(barrier, inc=1, device_id=(r, lax.rem(c + n, 8)),
                            device_id_type=pl.DeviceIdType.MESH)
    for d in range(4):
        pl.semaphore_signal(barrier, inc=1, device_id=dirs[d], device_id_type=pl.DeviceIdType.MESH)

    @pl.when(is_f | is_g)
    def _():
        pl.semaphore_signal(barrier, inc=1, device_id=(1 - r, 1 - c), device_id_type=pl.DeviceIdType.MESH)

    def block_cols(n):
        return pl.ds(pl.multiple_of(n * BLK, BLK), BLK)

    half_512 = pl.ds(pl.multiple_of(core * 512, 512), 512)
    other_512 = pl.ds(pl.multiple_of(512 - core * 512, 512), 512)

    def local(src, dst, sem):
        return pltpu.make_async_copy(src, dst, sem)

    @pl.when(is_f | is_g)
    def _():
        for k in range(FB):
            local(tiles.at[0, pl.ds(k * BLK, TILE - k * BLK), pl.ds(k * BLK, BLK)],
                  s.at[k, pl.ds(k * BLK, TILE - k * BLK), :], load.at[4 + k]).start()
            if k:
                s[k, pl.ds(0, k * BLK), :] = jnp.zeros((k * BLK, BLK), F32)

    def tile_rows(base):
        return [local(tiles.at[slot_a, pl.ds(k * BLK, BLK), :], v.at[base + k], load.at[k]) for k in range(FB)]

    def extra_rows():
        return [local(tiles.at[1, pl.ds(k * BLK, BLK), :], v10.at[k], load.at[8 + k]) for k in range(FB)]

    def own_cols():
        return [local(tiles.at[0, half_512, pl.ds(k * BLK, BLK)], w.at[4 * core + k, half_512, :], load.at[k])
                for k in range(FB)]

    def target(n):
        return local(tiles.at[slot_a if n == 0 else 1], t.at[n], load_t.at[n])

    def pass_in(n):
        return local(tiles.at[n], t.at[n], load_t.at[n])

    def pass_out(n):
        return local(t.at[n], out.at[n], osem.at[n])

    @pl.when(r == 0)
    def _():
        for cp in tile_rows(0):
            cp.start()

    @pl.when(r == 1)
    def _():
        for cp in tile_rows(4):
            cp.start()

        @pl.when(c == 2)
        def _():
            for cp in extra_rows():
                cp.start()

    @pl.when(full & (y == 0))
    def _():
        for cp in own_cols():
            cp.start()

    def panel_in():
        return [local(tiles.at[0, :, pl.ds(k * BLK, BLK)], h.at[k], osem.at[2 + k]) for k in range(FB)]

    @pl.when((r == 1) & (c == 0))
    def _():
        for cp in panel_in():
            cp.start()

    @pl.when(r >= 11)
    def _():
        pass_in(0).start()
        pass_in(1).start()

    @pl.when(full & (c > 2))
    def _():
        pass_in(1).start()

    @pl.when(plain)
    def _():
        pl.semaphore_wait(barrier, 11)

    @pl.when(is_f | is_g)
    def _():
        pl.semaphore_wait(barrier, 12)

    @pl.when(full & (y == 0))
    def _():
        for k in range(FB):
            remote(tiles.at[0, other_512, pl.ds(k * BLK, BLK)], w.at[4 * core + k, other_512, :],
                   r_send.at[2, 4 * core + k], r_sib.at[k], sibling).start()

    @pl.when((r == 1) & (c == 0))
    def _():
        for k in range(FB):
            remote(tiles.at[0, :, pl.ds(k * BLK, BLK)], w.at[k],
                   r_send.at[2, k], r_sib.at[k], sibling).start()

    @pl.when((r == 1) & (c == 2))
    def _():
        for cp in extra_rows():
            cp.wait()

    @pl.when(r >= 11)
    def _():
        for n in range(2):
            pass_in(n).wait()
            pass_out(n).start()

    @pl.when(full & (c > 2))
    def _():
        pass_in(1).wait()
        pass_out(1).start()

    @pl.when(full)
    def _():
        target(0).start()

        @pl.when(c == 2)
        def _():
            target(1).start()

    def within(n, count):
        return (n >= 0) & (n < count)

    def c_event(n):
        k = lax.div(n, 8)
        ref = v.at[k, pl.ds(pl.multiple_of(lax.rem(n, 8) * 32, 32), 32), :]

        @pl.when(r != 0)
        def _():
            arrived(ref, c_recv.at[n])

        @pl.when((r == 0) & (lax.rem(n, 8) == 0))
        def _():
            arrived(v.at[k], load.at[k])

        forward(c_out, ref, lambda d: c_send.at[d, k], c_recv.at[n])

    def d_event(n):
        k = lax.div(n, 8)
        ref = v.at[4 + k, pl.ds(pl.multiple_of(lax.rem(n, 8) * 32, 32), 32), :]

        @pl.when(r != 1)
        def _():
            arrived(ref, d_recv.at[n])

        @pl.when((r == 1) & (lax.rem(n, 8) == 0))
        def _():
            arrived(v.at[4 + k], load.at[k])

        forward(d_out, ref, lambda d: d_send.at[d, k], d_recv.at[n])

    def e_ref(n):
        return v10.at[lax.div(n, 4), pl.ds(pl.multiple_of(lax.rem(n, 4) * 64, 64), 64), :]

    def e_event(n, outs, way):
        @pl.when(r != 1)
        def _():
            arrived(e_ref(n), e_recv.at[n])

        forward(outs, e_ref(n), lambda d: e_send.at[way, d, lax.div(n, 4)], e_recv.at[n])

    e_out = c_out[:3] + (c_out[3] | (r == 1),)

    def e_drain(k):
        drain_outs(d_out, lambda d: e_send.at[0, d, k], 128)
        drain_outs(e_out, lambda d: e_send.at[1, d, k], 128)

    def r_ref(n):
        rows = pl.ds(pl.multiple_of(core * 512 + lax.rem(n, 4) * 128, 128), 128)
        return w.at[lax.div(n, 4), rows, :]

    def r_event(n, way, target, first, last):
        @pl.when(y == 0)
        def _():
            if first:
                b = lax.div(n, 4)
                m = lax.rem(b, 4)

                @pl.when((lax.rem(n, 4) == 0) & (lax.div(b, 4) == core))
                def _():
                    arrived(w.at[b, half_512, :], load.at[m])

                @pl.when((lax.rem(n, 4) == 0) & (lax.div(b, 4) != core))
                def _():
                    arrived(w.at[b, half_512, :], r_sib.at[m])

        @pl.when(y != 0)
        def _():
            arrived(r_ref(n), r_own.at[n])

        @pl.when(y != last)
        def _():
            remote(r_ref(n), r_ref(n), r_send.at[way, lax.div(n, 4)], r_own.at[n], (r, target)).start()

    def w_ready(b):
        @pl.when(y != 3)
        def _():
            drain(r_send.at[0, b], 64)

        @pl.when(y != 1)
        def _():
            drain(r_send.at[1, b], 64)

        @pl.when((y == 0) & (lax.div(b, 4) == core))
        def _():
            drain(r_send.at[2, b], 128)

    half_128 = pl.ds(pl.multiple_of(core * HALF, HALF), HALF)
    other_128 = pl.ds(pl.multiple_of(HALF - core * HALF, HALF), HALF)

    def l_event(n, outs, sends, root_row):
        ref = lb.at[n, half_128, :]
        arrived(ref, l_own.at[n])

        @pl.when(full)
        def _():
            remote(ref, ref, s_send, l_sib.at[n], sibling).start()

        forward(outs, ref, lambda d: sends.at[d], l_own.at[n])
        odd = lax.rem(n, 2)

        @pl.when((r == root_row) & (((y == 1) & (odd == 0)) | ((y == 3) & (odd == 1))))
        def _():
            remote(ref, ref, y_send.at[root_row], l_own.at[n], (r, 4 + core)).start()

    def l_ready(lo, count):
        @pl.loop(lo, lo + count)
        def _(n):
            arrived(lb.at[n, other_128, :], l_sib.at[n])

    def a_event(n):
        l_event(n, a_out, a_send, 0)

    def b_event(n):
        l_event(n, h_out, b_send, 1)

    def h_rows(n, half):
        return pl.ds(pl.multiple_of(half * 512 + lax.rem(n, 4) * 128, 128), 128)

    def h_send_to(n, other):
        part = h.at[lax.div(n, 4), h_rows(n, other % 2), :]
        remote(part, part, root_send.at[other], h_own.at[n], (1, other)).start()

    def h_event(n):
        k = lax.div(n, 4)
        ref = h.at[k, h_rows(n, core), :]
        origin = (r == 1) & (c == 0)

        @pl.when(origin)
        def _():
            for other in (2, 3, 6, 7):
                h_send_to(n, other)

        @pl.when(jnp.logical_not(origin))
        def _():
            arrived(ref, h_own.at[n])

        forward(h_out, ref, lambda d: h_send.at[d, k], h_own.at[n])
        odd = lax.rem(n, 2)

        @pl.when((r == 1) & (((y == 1) & (odd == 0)) | ((y == 3) & (odd == 1))))
        def _():
            remote(ref, ref, y_send.at[2], h_own.at[n], (r, 4 + core)).start()

    def h_drain(k):
        drain_outs(h_out, lambda d: h_send.at[d, k], 128)

    def swap(buf, k, send, recv):
        ref = buf.at[k, half_512, :]
        remote(ref, ref, send, recv, sibling).start()

    def swapped(buf, k, recv):
        arrived(buf.at[k, other_512, :], recv)

    def chain(base, send):
        @pl.loop(0, FB)
        def _(k):
            lo = base + first_id(k)
            block_factor(k, s, work, lb, lo)
            send(lo)

            @pl.loop(k + 1, FB)
            def _(i):
                p = dot_nt(s[k, rows_of(i), :], lb[lo])
                s[k, rows_of(i), :] = p
                lb[lo + i - k] = p
                send(lo + i - k)

            @pl.loop(k + 1, FB)
            def _(j):
                @pl.loop(j, FB)
                def _(i):
                    s[j, rows_of(i), :] = s[j, rows_of(i), :] - dot_nt(s[k, rows_of(i), :], s[k, rows_of(j), :])

    def half_of(core_no):
        return pl.ds(core_no * HALF, HALF)

    def send_f(n):
        for q, h in enumerate((0, 1)):
            remote(lb.at[n, half_of(h), :], lb.at[n, half_of(h), :], root_send.at[8 + q],
                   (l_own if h == 1 else l_sib).at[n], (1, 1)).start()
        for other in (1, 2, 3, 6, 7):
            ref = lb.at[n, half_of(other % 2), :]
            remote(ref, ref, root_send.at[other], l_own.at[n], (0, other)).start()
        forward(a_out, lb.at[n, half_of(0), :], lambda d: a_send.at[d], l_own.at[n])

    def send_g(n):
        for other in (0, 2, 3, 6, 7):
            ref = lb.at[n, half_of(other % 2), :]
            remote(ref, ref, root_send.at[other], l_own.at[n], (1, other)).start()
        forward(h_out, lb.at[n, half_of(1), :], lambda d: b_send.at[d], l_own.at[n])

    def factor_out():
        return [local(s.at[k], out.at[0, :, pl.ds(k * BLK, BLK)], osem.at[2 + k]) for k in range(FB)]

    @pl.when(is_f)
    def _():
        for k in range(FB):
            arrived(s.at[k, pl.ds(k * BLK, TILE - k * BLK), :], load.at[4 + k])

        @pl.loop(0, 32)
        def _(n):
            c_event(n)

        chain(0, send_f)
        for cp in factor_out():
            cp.start()
        for cp in factor_out():
            cp.wait()
        for k in range(FB):
            drain_outs(c_out, lambda d: c_send.at[d, k], 256)
        drain_outs(a_out, lambda d: a_send.at[d], 320)
        for other in (1, 2, 3, 6, 7, 8, 9):
            drain(root_send.at[other], 320)

    @pl.when(is_g)
    def _():
        @pl.loop(0, 32)
        def _(n):
            d_event(n)

        @pl.loop(0, 16)
        def _(n):
            h_event(n)

        for k in range(FB):
            arrived(s.at[k, pl.ds(k * BLK, TILE - k * BLK), :], load.at[4 + k])
            arrived(w.at[k], r_sib.at[k])

        @pl.loop(0, FB)
        def _(k):
            lo = first_id(k)

            @pl.loop(lo, lo + 4 - k)
            def _(n):
                arrived(lb.at[n, half_of(1), :], l_own.at[n])
                arrived(lb.at[n, half_of(0), :], l_sib.at[n])

            @pl.loop(0, FB)
            def _(i):
                p = dot_nt(w[k, rows_of(i), :], lb[lo])
                w[k, rows_of(i), :] = p
                ref = w.at[k, rows_of(i), :]
                remote(ref, ref, root_send.at[8], p_recv.at[4 * k + i], (1, 0)).start()

            @pl.loop(0, FB)
            def _(j):
                @pl.loop(j, FB)
                def _(i):
                    s[j, rows_of(i), :] = s[j, rows_of(i), :] - dot_nt(w[k, rows_of(i), :], w[k, rows_of(j), :])

            @pl.loop(k + 1, FB)
            def _(j):
                @pl.loop(0, FB)
                def _(i):
                    w[j, rows_of(i), :] = w[j, rows_of(i), :] - dot_nt(w[k, rows_of(i), :], lb[lo + j - k])

        chain(10, send_g)
        for cp in factor_out():
            cp.start()
        for cp in factor_out():
            cp.wait()
        for k in range(FB):
            drain_outs(d_out, lambda d: d_send.at[d, k], 256)
            h_drain(k)
        drain_outs(h_out, lambda d: b_send.at[d], 320)
        for other in (0, 2, 3, 6, 7):
            drain(root_send.at[other], 320)
        drain(root_send.at[8], 1024)

    def low_id(k, m):
        return jnp.where(k < FB, first_id(m), 10 + first_id(m - FB)) + k - m

    def v_sub(k, low, m):
        v[k] = v[k] - dot3(split2(low), (vh[m], vw[m]), 0)

    def v_solve(k):
        solved = dot3(split2(lb[low_id(k, k)]), split2(v[k]), 0)
        hi, lo = split2(solved)
        vh[k] = hi
        vw[k] = lo

    def x_sub(k, m):
        v10[k - FB] = v10[k - FB] - dot3(split2(lb[low_id(k, m)]), split2(v10[m - FB]), 0)

    def x_solve(k):
        v10[k - FB] = dot3(split2(lb[low_id(k, k)]), split2(v10[k - FB]), 0)
        hi, lo = split2(v10[k - FB])
        xh[...] = hi
        xw[...] = lo

    def w_sub(buf, k, low, m):
        buf[k, half_512, :] = buf[k, half_512, :] - dot3(split2(buf[m, half_512, :]), split2(low), 1)

    def w_solve(buf, k, send, recv):
        buf[k, half_512, :] = dot3(split2(buf[k, half_512, :]), split2(lb[low_id(k, k)]), 1)
        swap(buf, k, send, recv)

    def t_sub(slot, k, right):
        hi, lo = split2(w[k])
        ph[...] = hi
        pw[...] = lo
        for n in range(4):
            cols = pl.ds(n * BLK, BLK)
            t[slot, :, cols] = t[slot, :, cols] - dot3(
                (ph[...], pw[...]), (right[0][:, cols], right[1][:, cols]), 0
            )

    def run_op(kind, k, m):
        @pl.when(kind == PREP)
        def _():
            @pl.when(m == 0)
            def _():
                w_ready(k)

                @pl.when(k < FB)
                def _():
                    @pl.loop(0, k + 1)
                    def _(q):
                        l_ready(low_id(k, q), 1)

            @pl.when(m == 1)
            def _():
                drain_outs(c_out, lambda d: c_send.at[d, k], 256)

                @pl.when(k == 0)
                def _():
                    target(0).wait()

            @pl.when(m == 3)
            def _():
                swapped(h, k, h_full.at[k])

            @pl.when(m == 6)
            def _():
                h_drain(k)

            @pl.when(m == 4)
            def _():
                @pl.loop(FB, k + 1)
                def _(q):
                    l_ready(low_id(k, q), 1)

            @pl.when((m == 5) & (c == 2))
            def _():
                e_drain(k - FB)

                @pl.when(k == FB)
                def _():
                    target(1).wait()

            @pl.when(m == 2)
            def _():
                drain_outs(d_out, lambda d: d_send.at[d, k], 256)

        @pl.when(kind == VSUB)
        def _():
            @pl.when((k < FB) | (m >= FB))
            def _():
                v_sub(k, lb[low_id(k, m)], m)

            @pl.when((k >= FB) & (m < FB))
            def _():
                v_sub(k, h[m, rows_of(k - FB), :], m)

        @pl.when(kind == WSUB)
        def _():
            @pl.when((k < FB) | (m >= FB))
            def _():
                w_sub(w, k, lb[low_id(k, m)], m)

            @pl.when((k >= FB) & (m < FB))
            def _():
                w_sub(w, k, h[m, rows_of(k - FB), :], m)

        @pl.when(kind == HSUB)
        def _():
            w_sub(h, k, lb[low_id(k, m)], m)

        @pl.when(kind == VSOLVE)
        def _():
            v_solve(k)

        @pl.when(kind == WSOLVE)
        def _():
            w_solve(w, k, w_send.at[k], w_full.at[k])

        @pl.when(kind == HSOLVE)
        def _():
            w_solve(h, k, h_send.at[4, k], h_full.at[k])

        @pl.when(kind == TSUB)
        def _():
            swapped(w, k, w_full.at[k])
            t_sub(0, k, (vh.at[k], vw.at[k]))

        @pl.when(c == 2)
        def _():
            @pl.when(kind == XSUB)
            def _():
                x_sub(k, m)

            @pl.when(kind == XSOLVE)
            def _():
                x_solve(k)

            @pl.when(kind == XT)
            def _():
                t_sub(1, k, (xh, xw))

    table = plan()
    count = [len(ops) for ops in table]
    flat = [64 * kind + 8 * k + m for ops in table for kind, k, m in ops]
    before = [sum(count[:n]) for n in range(len(count))]

    @pl.when((r == 1) & (c == 0))
    def _():
        for k in range(FB):
            arrived(h.at[k], osem.at[2 + k])

        @pl.loop(0, 16)
        def _(n):
            h_send_to(n, 1)

    @pl.when(plain)
    def _():
        @pl.loop(0, max(len(table), EXTRA_SLOT + 18))
        def _(slot):
            n_c = slot - 2 * c_depth

            @pl.when(c_in & within(n_c, 32))
            def _():
                c_event(n_c)

            n_d = slot - 2 * d_depth

            @pl.when(d_in & within(n_d, 32))
            def _():
                d_event(n_d)

            n_r = slot - 2 * y

            @pl.when(full & within(n_r, 16))
            def _():
                r_event(2 * n_r, 0, lax.rem(c + 2, 8), True, 3)

            n_s = slot - 2 * lax.rem(4 - y, 4)

            @pl.when(full & within(n_s, 16))
            def _():
                r_event(2 * n_s + 1, 1, lax.rem(c + 6, 8), False, 1)

            n_a = lookup(slot - a_depth - y_depth, [STREAM_SLOTS.index(q) if q in STREAM_SLOTS else -1
                                                      for q in range(STREAM_SLOTS[-1] + 1)])

            @pl.when(a_in & (n_a >= 0))
            def _():
                a_event(n_a)

            n_h = lookup(slot - b_depth - y_depth, [PANEL_SLOTS.index(q) if q in PANEL_SLOTS else -1
                                                    for q in range(PANEL_SLOTS[-1] + 1)])

            @pl.when(b_in & (n_h >= 0))
            def _():
                h_event(n_h)

            n_b = lookup(slot - b_depth - y_depth, [LAST_SLOTS.index(q) if q in LAST_SLOTS else -1
                                                    for q in range(LAST_SLOTS[-1] + 1)])

            @pl.when(b_in & (n_b >= 0))
            def _():
                b_event(10 + n_b)

            @pl.when(c == 2)
            def _():
                n_e = slot - EXTRA_SLOT - 2 * d_depth

                @pl.when(d_in & within(n_e, 8))
                def _():
                    e_event(2 * n_e, d_out, 0)

                n_f = slot - EXTRA_SLOT - jnp.where(r == 1, 0, 2 + 2 * c_depth)

                @pl.when((c_in | (r == 1)) & within(n_f, 8))
                def _():
                    e_event(2 * n_f + 1, e_out, 1)

            @pl.when(full)
            def _():
                first = lookup(slot, before, 0)

                @pl.loop(first, first + lookup(slot, count, 0))
                def _(n):
                    code = lookup(n, flat)
                    run_op(lax.div(code, 64), lax.rem(lax.div(code, 8), 8), lax.rem(code, 8))

    @pl.when(plain & (r < 2))
    def _():
        @pl.when(r == 0)
        def _():
            for k in range(FB):
                drain_outs(c_out, lambda d: c_send.at[d, k], 256)

        @pl.when(r == 1)
        def _():
            for k in range(FB):
                drain_outs(d_out, lambda d: d_send.at[d, k], 256)
                h_drain(k)

            @pl.when((y == 1) | (y == 3))
            def _():
                drain(y_send.at[2], 256)

            @pl.when(c == 0)
            def _():
                for other in (1, 2, 3, 6, 7):
                    drain(root_send.at[other], 512)

    @pl.when(r >= 11)
    def _():
        for k in range(FB):
            drain_outs(c_out, lambda d: c_send.at[d, k], 256)
            drain_outs(d_out, lambda d: d_send.at[d, k], 256)
            h_drain(k)

    @pl.when((c == 2) & jnp.logical_not(full))
    def _():
        for k in range(FB):
            e_drain(k)

    @pl.when((r == 1) & (c == 0))
    def _():
        for k in range(FB):
            drain(r_send.at[2, k], 256)

    def run(copies):
        for cp in copies:
            cp.start()
        for cp in copies:
            cp.wait()

    @pl.when(full)
    def _():
        main = local(t.at[0], out.at[slot_a], osem.at[0])

        @pl.when(c < 2)
        def _():
            run([main] + [local(w.at[4 * c + k], out.at[0, :, pl.ds(k * BLK, BLK)], osem.at[2 + k])
                          for k in range(FB)])

        @pl.when(c == 2)
        def _():
            run([main, local(t.at[1], out.at[1], osem.at[1])])

        @pl.when(c > 2)
        def _():
            run([main])
            pass_out(1).wait()

        drain(s_send, 640)
        for k in range(FB):
            drain(h_send.at[4, k], 128)
        for k in range(NB):
            drain(w_send.at[k], 128)

    @pl.when(r >= 11)
    def _():
        for n in range(2):
            pass_out(n).wait()

    @pl.when(r < 2)
    def _():
        t[0] = jnp.zeros((TILE, TILE), F32)
        blank = [local(t.at[0], out.at[n], osem.at[n]) for n in range(2)]

        @pl.when(c <= r)
        def _():
            run(blank[1:])

        @pl.when(c > r)
        def _():
            run(blank)

    @pl.when((r == 1) & (c == 0))
    def _():
        for k in range(FB):
            for i in range(FB):
                arrived(w.at[k, pl.ds(i * BLK, BLK), :], p_recv.at[4 * k + i])
        run([local(w.at[k], out.at[0, :, pl.ds(k * BLK, BLK)], osem.at[2 + k]) for k in range(FB)])

    @pl.when(plain)
    def _():
        drain_outs(a_out, lambda d: a_send.at[d], 320)
        drain_outs(h_out, lambda d: b_send.at[d], 320)

        @pl.when((r < 2) & ((y == 1) | (y == 3)))
        def _():
            @pl.when(r == 0)
            def _():
                drain(y_send.at[0], 160)

            @pl.when(r == 1)
            def _():
                drain(y_send.at[1], 160)


def hand_on(src, out, buf, load, store):
    def parts(n):
        return n // 4, pl.ds(n % 4 * BLK, BLK)

    loads = [pltpu.make_async_copy(src.at[parts(n)], buf.at[parts(n)], load.at[n]) for n in range(8)]
    stores = [pltpu.make_async_copy(buf.at[parts(n)], out.at[parts(n)], store.at[n]) for n in range(8)]
    for cp in loads:
        cp.start()
    for n in range(8):
        loads[n].wait()
        stores[n].start()
    for cp in stores:
        cp.wait()


def on_device(kernel_tiles, profile):
    tiles = kernel_tiles.reshape(2, TILE, TILE)
    dma = pltpu.SemaphoreType.DMA
    out = pl.pallas_call(
        kernel,
        out_shape=jax.ShapeDtypeStruct((2, TILE, TILE), F32),
        in_specs=[pl.BlockSpec(memory_space=pl.ANY)],
        out_specs=pl.BlockSpec(memory_space=pl.ANY),
        scratch_shapes=[
            pltpu.VMEM((NB, TILE, BLK), F32),
            pltpu.VMEM((NB, BLK, TILE), F32),
            pltpu.VMEM((FB, BLK, TILE), F32),
            pltpu.VMEM((FB, TILE, BLK), F32),
            pltpu.VMEM((2, TILE, TILE), F32),
            pltpu.VMEM((20, BLK, BLK), F32),
            pltpu.VMEM((FB, TILE, BLK), F32),
            pltpu.VMEM((HALF, 2 * HALF), F32),
            pltpu.VMEM((TILE, BLK), BF16),
            pltpu.VMEM((TILE, BLK), BF16),
            pltpu.VMEM((NB, BLK, TILE), BF16),
            pltpu.VMEM((NB, BLK, TILE), BF16),
            pltpu.VMEM((BLK, TILE), BF16),
            pltpu.VMEM((BLK, TILE), BF16),
            dma((12,)), dma((2,)),
            dma((32,)), dma((32,)), dma((16,)), dma((16,)), dma((4,)), dma((8,)), dma((16,)),
            dma((32,)), dma((4,)), dma((20,)), dma((20,)),
            dma((4, 4)), dma((4, 4)), dma((2, 4, 4)), dma((5, 4)), dma((8,)), dma((3, 8)),
            dma((4,)), dma((4,)), dma((3,)), dma, dma((10,)), dma((6,)),
        ],
        compiler_params=pltpu.CompilerParams(
            vmem_limit_bytes=58 * 2**20, collective_id=0, has_side_effects=True
        ),
        name="panel_steps",
    )(tiles)
    out = pl.pallas_call(
        hand_on,
        out_shape=jax.ShapeDtypeStruct((2, TILE, TILE), F32),
        in_specs=[pl.BlockSpec(memory_space=pl.ANY)],
        out_specs=pl.BlockSpec(memory_space=pl.ANY),
        scratch_shapes=[pltpu.VMEM((2, TILE, TILE), F32), dma((8,)), dma((8,))],
        compiler_params=pltpu.CompilerParams(vmem_limit_bytes=56 * 2**20),
        name="hand_on",
    )(out)
    return out.reshape(kernel_tiles.shape)


def solution(mesh):
    placed = (P(None, "row", None, "col", None, None), P())
    return jax.shard_map(
        on_device,
        mesh=mesh,
        in_specs=placed,
        out_specs=P(None, "row", None, "col", None, None),
        check_vma=False,
    )
```
